32 devices in a mesh: dp: 8 (over z, core), expert: 4 (over y, x).
Axes of the slice: x: 2, y: 2, z: 4, core: 2. Of those that a mesh axis runs over, the one named last changes fastest.
Arguments:
- teacher_in: bfloat16 [1024, 2048], P('dp'), may hold values from -6 to 6
- student_in: bfloat16 [1024, 2048], P('dp'), may hold values from -6 to 6
- teacher_route: int32 [1024, 1], P('dp'), may hold values from 0 to 3, as said below
- student_route: int32 [1024, 1], P('dp'), may hold values from 0 to 3, as said below
- teacher_w1: bfloat16 [8, 2048, 2048], P('dp', None, 'expert'), may hold values from -0.125 to 0.125
- teacher_w2: bfloat16 [8, 2048, 2048], P('dp', 'expert'), may hold values from -0.09375 to 0.09375
- student_w1: bfloat16 [8, 2048, 2048], P('dp', None, 'expert'), may hold values from -0.125 to 0.125
- student_w2: bfloat16 [8, 2048, 2048], P('dp', 'expert'), may hold values from -0.09375 to 0.09375
Outputs:
- grad_w1: bfloat16 [8, 2048, 2048], P('dp', None, 'expert')
- grad_w2: bfloat16 [8, 2048, 2048], P('dp', 'expert')
The draws below stay inside these ranges and needn't reach their ends.
Inputs may be any that keep to these rules, and one draw needn't show every extreme that they name: `teacher_route`: in each aligned block of 128 rows (the rows of one index of dp) no expert is named by more than 48 rows, and some expert exactly 48 times; every expert is named exactly 48 times in some block. `student_route`: in each aligned block of 128 rows (the rows of one index of dp) no expert is named by more than 48 rows, and some expert exactly 48 times; every expert is named exactly 48 times in some block.
All inputs are finite; a program needn't handle non-finite values.
Results may differ from the reference program's by a relative error of at most 0.015.
Values may be sent and summed in bfloat16 or wider, within the bound.
No kernel may reach another device: no remote copies, remote signals or barrier semaphores. Data moves between devices by JAX's collectives and lax.ppermute only.
A program may use at most 64 MiB of HBM per device.

```python
import math
import jax
import jax.numpy as jnp
from jax import lax

D = 2048
FF = 4096
TOK_DEV = 128
EXPERTS = 4
CAP = 48
HID = 512
TOKENS = 1024
N_DP = 8


def route_table(key):
    key_offset, key_slots, key_rows = jax.random.split(key, 3)
    slot_total = EXPERTS * CAP
    offset = jax.random.randint(key_offset, (), 0, EXPERTS, dtype=jnp.int32)
    full_expert = (jnp.arange(N_DP, dtype=jnp.int32) + offset) % EXPERTS
    slot_iota = jnp.arange(slot_total, dtype=jnp.int32)
    slot_expert = slot_iota // CAP
    forced = slot_expert[None, :] == full_expert[:, None]
    raw_scores = jax.random.randint(key_slots, (N_DP, slot_total), 0, 2 ** 19, dtype=jnp.int32)
    scores = jnp.where(forced, -1 - slot_iota[None, :], raw_scores * slot_total + slot_iota[None, :])
    order = jnp.argsort(scores, axis=1, stable=True)[:, :TOK_DEV].astype(jnp.int32)
    chosen = order // CAP
    row_iota = jnp.arange(TOK_DEV, dtype=jnp.int32)
    row_scores = jax.random.randint(key_rows, (N_DP, TOK_DEV), 0, 2 ** 19, dtype=jnp.int32) * TOK_DEV + row_iota[None, :]
    shuffle = jnp.argsort(row_scores, axis=1, stable=True).astype(jnp.int32)
    mixed = jnp.take_along_axis(chosen, shuffle, axis=1)
    return mixed.reshape(TOKENS, 1).astype(jnp.int32)


def draw_teacher_route(key, part):
    key = jax.random.fold_in(key, 11)
    return route_table(key)


def draw_student_route(key, part):
    key = jax.random.fold_in(key, 23)
    return route_table(key)


def block_levels(stream_key, shape, shards, least, high):
    factor_of = 1.0
    for dim, shards_of in shards:
        heights = jax.random.uniform(jax.random.fold_in(jax.random.fold_in(stream_key, 6), dim), (shards_of,), jnp.float32, least / len(shards), high / len(shards))
        factor_of = factor_of * jnp.repeat(jnp.exp(heights), shape[dim] // shards_of).reshape((-1,) + (1,) * (len(shape) - 1 - dim))
    return factor_of


def gaussian(rng, shape, spread, limit, shards=(), held_as=jnp.bfloat16):
    loudness = block_levels(rng, shape, shards, -0.22, 0.18) if shards else 1.0
    array = jax.random.normal(rng, shape, jnp.float32) * spread * loudness
    return jnp.minimum(jnp.maximum(array, -limit), limit).astype(held_as)


def setup_inputs(seed: int = 0) -> dict:
    key_of = jax.random.split(jax.random.key(seed), 9)
    return {
        "teacher_in": gaussian(key_of[0], (TOKENS, D), 1.0, 6.0, ((0, 8),)),
        "student_in": gaussian(key_of[1], (TOKENS, D), 1.0, 6.0, ((0, 8),)),
        "teacher_route": draw_teacher_route(jax.random.fold_in(key_of[8], 71), 0),
        "student_route": draw_student_route(jax.random.fold_in(key_of[8], 71), 0),
        "teacher_w1": gaussian(key_of[4], (2 * EXPERTS, D, FF // 2), D ** -0.5, 0.125, ((0, 8), (2, 4))),
        "teacher_w2": gaussian(key_of[5], (2 * EXPERTS, FF // 2, D), FF ** -0.5, 0.09375, ((0, 8), (1, 4))),
        "student_w1": gaussian(key_of[6], (2 * EXPERTS, D, FF // 2), D ** -0.5, 0.125, ((0, 8), (2, 4))),
        "student_w2": gaussian(key_of[7], (2 * EXPERTS, FF // 2, D), FF ** -0.5, 0.09375, ((0, 8), (1, 4))),
    }


root_coef = math.sqrt(2.0 / math.pi)
cubic_coef = 0.044715

def gelu_tanh(pre_act):
    inner_arg = root_coef * (pre_act + cubic_coef * pre_act * pre_act * pre_act)
    return 0.5 * pre_act * (1.0 + jnp.tanh(inner_arg))

def gelu_slope(pre_act):
    tangent = jnp.tanh(root_coef * (pre_act + cubic_coef * pre_act * pre_act * pre_act))
    return 0.5 * (1.0 + tangent) + 0.5 * pre_act * (1.0 - tangent * tangent) * root_coef * (1.0 + 3.0 * cubic_coef * pre_act * pre_act)

def slot_positions(routes):
    choose = routes[:, 0].astype(jnp.int32)
    onehot = (choose[:, None] == jnp.arange(EXPERTS, dtype=jnp.int32)[None, :]).astype(jnp.int32)
    blocked = onehot.reshape(N_DP, TOK_DEV, EXPERTS)
    rank_table = jnp.cumsum(blocked, axis=1) - 1
    position = lax.optimization_barrier(jnp.sum(blocked * rank_table, axis=2)).reshape(TOKENS).astype(jnp.int32)
    block_id = (jnp.arange(TOKENS, dtype=jnp.int32) // TOK_DEV).astype(jnp.int32)
    return (choose, block_id, position)

def to_slots(values, route_info):
    choose, block_id, position = route_info
    empty = jnp.zeros((EXPERTS, N_DP, CAP, D), values.dtype)
    return empty.at[choose, block_id, position].set(values)

def from_slots(slots, route_info):
    choose, block_id, position = route_info
    return slots[choose, block_id, position]

def join_first(w1_pair):
    return jnp.concatenate([w1_pair[0], w1_pair[1]], axis=1)

def expert_output(x_rows, w1_pair, w2_full):
    pre_act = jnp.dot(x_rows, join_first(w1_pair), preferred_element_type=jnp.float32)
    hidden = gelu_tanh(pre_act).astype(jnp.bfloat16)
    group_count = FF // HID
    parts = jnp.einsum('sgi,gid->sgd', hidden.reshape(-1, group_count, HID).astype(jnp.float32), w2_full.reshape(group_count, HID, D).astype(jnp.float32))
    rounded = lax.optimization_barrier(parts.astype(jnp.bfloat16))
    return lax.optimization_barrier(jnp.sum(rounded.astype(jnp.float32), axis=1))

def forward_expert(inputs):
    teacher_slots, student_slots, w1_teacher, w2_teacher, w1_student, w2_student = inputs
    teacher_out = expert_output(teacher_slots.reshape(-1, D), w1_teacher, w2_teacher)
    student_out = expert_output(student_slots.reshape(-1, D), w1_student, w2_student)
    return (teacher_out, student_out)

def backward_expert(inputs):
    student_slots, grad_slots, w1_student, w2_student = inputs
    x_rows = student_slots.reshape(-1, D)
    up_rows = grad_slots.reshape(-1, D)
    pre_act = jnp.dot(x_rows, join_first(w1_student), preferred_element_type=jnp.float32)
    hidden = gelu_tanh(pre_act).astype(jnp.bfloat16)
    hidden_grad = jnp.dot(up_rows, w2_student.T, preferred_element_type=jnp.float32)
    pre_grad = (hidden_grad * gelu_slope(pre_act)).astype(jnp.bfloat16)
    grad_second = jnp.dot(hidden.T, up_rows, preferred_element_type=jnp.float32).astype(jnp.bfloat16)
    grad_first = jnp.dot(x_rows.T, pre_grad, preferred_element_type=jnp.float32).astype(jnp.bfloat16)
    grad_first = grad_first.reshape(D, 2, FF // 2).transpose(1, 0, 2)
    return (grad_first, grad_second)

def reference(teacher_in, student_in, teacher_route, student_route, teacher_w1, teacher_w2, student_w1, student_w2):
    teacher_info = slot_positions(teacher_route)
    student_info = slot_positions(student_route)
    w1_teacher = teacher_w1.reshape(EXPERTS, 2, D, FF // 2)
    w2_teacher = teacher_w2.reshape(EXPERTS, FF, D)
    w1_student = student_w1.reshape(EXPERTS, 2, D, FF // 2)
    w2_student = student_w2.reshape(EXPERTS, FF, D)
    teacher_slots = to_slots(teacher_in, teacher_info)
    student_slots = to_slots(student_in, student_info)
    teacher_sums, student_sums = lax.map(forward_expert, (teacher_slots, student_slots, w1_teacher, w2_teacher, w1_student, w2_student))
    teacher_out = from_slots(teacher_sums.reshape(EXPERTS, N_DP, CAP, D), teacher_info)
    student_out = from_slots(student_sums.reshape(EXPERTS, N_DP, CAP, D), student_info)
    upstream = ((student_out - teacher_out) * (1.0 / math.sqrt(TOK_DEV))).astype(jnp.bfloat16)
    grad_slots = to_slots(upstream, student_info)
    grad_first, grad_second = lax.map(backward_expert, (student_slots, grad_slots, w1_student, w2_student))
    grad_w1 = grad_first.reshape(2 * EXPERTS, D, FF // 2)
    grad_w2 = grad_second.reshape(2 * EXPERTS, FF // 2, D)
    return (grad_w1, grad_w2)
```

```python
import math

import jax
import jax.numpy as jnp
from jax import lax
from jax.experimental import pallas as pl
from jax.experimental.pallas import tpu as pltpu
from jax.sharding import PartitionSpec as P

root_coef = math.sqrt(2.0 / math.pi)
cubic_coef = 0.044715


def partner(value, axis, mask):
    return lax.ppermute(value, axis, [(i, i ^ mask) for i in range(lax.axis_size(axis))])


def gelu_tanh(pre_act):
    inner_arg = root_coef * (pre_act + cubic_coef * pre_act * pre_act * pre_act)
    return 0.5 * pre_act * (1.0 + jnp.tanh(inner_arg))


def gelu_slope(pre_act):
    tangent = jnp.tanh(root_coef * (pre_act + cubic_coef * pre_act * pre_act * pre_act))
    return 0.5 * (1.0 + tangent) + 0.5 * pre_act * (1.0 - tangent * tangent) * root_coef * (
        1.0 + 3.0 * cubic_coef * pre_act * pre_act
    )


def dot(left, right):
    return jnp.dot(left, right, preferred_element_type=jnp.float32)


def ranks(routes, experts):
    onehot = (routes[..., None] == jnp.arange(experts, dtype=jnp.int32)).astype(jnp.int32)
    rank_table = jnp.cumsum(onehot, axis=1) - 1
    return jnp.sum(onehot * rank_table, axis=2)


def sizes(rows):
    groups = lax.axis_size("dp")
    experts = groups // 2
    row_count, width = rows.shape
    capacity = 2 * max(1, 3 * row_count // (4 * experts))
    return groups, lax.axis_size("expert"), experts, row_count, width, capacity


def by_ops(
    teacher_in,
    student_in,
    teacher_route,
    student_route,
    teacher_w1,
    teacher_w2,
    student_w1,
    student_w2,
):
    groups, columns, experts, row_count, width, capacity = sizes(teacher_in)
    plane_rows = groups * capacity
    dp = lax.axis_index("dp")
    column = lax.axis_index("expert")
    plane, core = dp // 2, dp % 2
    loss_scale = 1.0 / math.sqrt(row_count)
    feat = width // columns
    piece = feat // 2

    def dispatch(values, routes):
        position = ranks(routes[:, 0][None], experts)[0]
        slot = (routes[:, 0] ^ plane) * capacity + position
        placing = (
            jnp.arange(experts * capacity, dtype=jnp.int32)[:, None] == slot[None, :]
        ).astype(jnp.bfloat16)
        own_slice = lax.dynamic_slice(values, (0, column * feat), (row_count, feat))
        slots = dot(placing[capacity:], own_slice).astype(jnp.bfloat16)
        stay = dot(placing[:capacity], values).astype(jnp.bfloat16)
        moved = [
            partner(slots[(s - 1) * capacity : s * capacity], "dp", s << 1)
            for s in range(1, experts)
        ]
        mine = jnp.concatenate(moved, axis=0)
        buffer = jnp.concatenate([stay, jnp.zeros((mine.shape[0], width), jnp.bfloat16)], axis=0)
        for m in range(columns):
            got = partner(mine, "expert", m) if m else mine
            buffer = lax.dynamic_update_slice(buffer, got, (capacity, (column ^ m) * feat))
        other = partner(buffer, "dp", 1)
        first = jnp.where(core == 0, buffer, other)
        second = jnp.where(core == 0, other, buffer)
        return jnp.concatenate([first, second], axis=0)

    def forward(flat, w1, w2):
        pre = dot(flat, w1)
        hidden = gelu_tanh(pre).astype(jnp.bfloat16)
        part = dot(hidden, w2).astype(jnp.bfloat16).reshape(plane_rows, 2, columns, piece)
        part = part.transpose(1, 2, 0, 3)
        return pre, hidden, part

    def plane_sum(part):
        keep = lax.dynamic_index_in_dim(part, core, 0, keepdims=False)
        send = lax.dynamic_index_in_dim(part, 1 - core, 0, keepdims=False)
        pair = (
            keep.astype(jnp.float32) + partner(send, "dp", 1).astype(jnp.float32)
        ).astype(jnp.bfloat16)
        total = lax.dynamic_index_in_dim(pair, column, 0, keepdims=False).astype(jnp.float32)
        for m in range(1, columns):
            out = lax.dynamic_index_in_dim(pair, column ^ m, 0, keepdims=False)
            total = total + partner(out, "expert", m).astype(jnp.float32)
        return total

    routes = jnp.concatenate([teacher_route, student_route], axis=1)
    table = lax.all_gather(routes, "dp", axis=0, tiled=True).reshape(groups, row_count, 2)
    teacher_all, student_all = table[:, :, 0], table[:, :, 1]
    block = jnp.arange(groups, dtype=jnp.int32)[:, None]
    block_plane, block_core = block // 2, block % 2
    teacher_row = (
        (teacher_all ^ plane) * plane_rows
        + (block_core * experts + (block_plane ^ teacher_all)) * capacity
        + ranks(teacher_all, experts)
    )
    student_row = jnp.where(student_all == plane, ranks(student_all, experts), -1)
    hits = jnp.arange(capacity, dtype=jnp.int32)[None, :, None] == student_row[:, None, :]
    source = jnp.sum(jnp.where(hits, teacher_row[:, None, :] + 1, 0), axis=2) - 1
    source = source.reshape(experts, 2, capacity)
    source = source[jnp.arange(experts, dtype=jnp.int32) ^ plane].transpose(1, 0, 2)
    source = source.reshape(plane_rows)

    teacher_flat = dispatch(teacher_in, teacher_route)
    student_flat = dispatch(student_in, student_route)
    _, _, teacher_part = forward(teacher_flat, teacher_w1[0], teacher_w2[0])
    teacher_sum = plane_sum(teacher_part).astype(jnp.bfloat16)
    teacher_sums = jnp.concatenate(
        [teacher_sum] + [partner(teacher_sum, "dp", s << 1) for s in range(1, experts)], axis=0
    )
    student_pre, student_hidden, student_part = forward(
        student_flat, student_w1[0], student_w2[0]
    )
    pick = (
        source[:, None] == jnp.arange(experts * plane_rows, dtype=jnp.int32)[None, :]
    ).astype(jnp.bfloat16)
    teacher_rows = dot(pick, teacher_sums)
    student_sum = plane_sum(student_part)
    upstream = ((student_sum - teacher_rows) * loss_scale).astype(jnp.bfloat16)

    half = jnp.zeros((plane_rows, width // 2), jnp.bfloat16)
    for m in range(columns):
        got = partner(upstream, "expert", m) if m else upstream
        half = lax.dynamic_update_slice(half, got, (0, (column ^ m) * piece))
    other_half = partner(half, "dp", 1)
    grad_flat = jnp.concatenate(
        [jnp.where(core == 0, half, other_half), jnp.where(core == 0, other_half, half)], axis=1
    )
    hidden_grad = dot(grad_flat, student_w2[0].T)
    pre_grad = (hidden_grad * gelu_slope(student_pre)).astype(jnp.bfloat16)
    grad_second = dot(student_hidden.T, grad_flat).astype(jnp.bfloat16)
    grad_first = dot(student_flat.T, pre_grad).astype(jnp.bfloat16)
    return (grad_first[None], grad_second[None])


def place():
    dp = lax.axis_index("dp")
    return dp // 2, dp % 2, lax.axis_index("expert")


VMEM = pl.BlockSpec(memory_space=pltpu.VMEM)
ANY = pl.BlockSpec(memory_space=pl.ANY)


def call(kernel, outs, operands, out_specs=None, in_specs=None, scratch=(), aliases=None, grant=20 << 20, flops=0, name=None):
    return pl.pallas_call(
        kernel,
        name=name,
        out_shape=outs,
        in_specs=in_specs or [VMEM] * len(operands),
        out_specs=out_specs or [VMEM] * len(outs),
        scratch_shapes=list(scratch),
        input_output_aliases=aliases or {},
        compiler_params=pltpu.CompilerParams(vmem_limit_bytes=grant),
        cost_estimate=pl.CostEstimate(flops=flops, bytes_accessed=0, transcendentals=0),
    )(*operands)


def shape(*dims, dtype=jnp.bfloat16):
    return jax.ShapeDtypeStruct(dims, dtype)


def dot_tn(left, right):
    return lax.dot_general(
        left, right, (((0,), (0,)), ((), ())), preferred_element_type=jnp.float32
    )


def dot_nt(left, right):
    return lax.dot_general(
        left, right, (((1,), (1,)), ((), ())), preferred_element_type=jnp.float32
    )


def placing(route, experts, capacity, plane):
    rows = route.shape[1]
    known = lax.broadcasted_iota(jnp.int32, (16 * (-(-experts // 16)), rows), 0)
    onehot = jnp.where(known == route, 1.0, 0.0)
    upto = lax.broadcasted_iota(jnp.int32, (rows, rows), 0) <= lax.broadcasted_iota(
        jnp.int32, (rows, rows), 1
    )
    counts = dot(onehot.astype(jnp.bfloat16), jnp.where(upto, 1.0, 0.0).astype(jnp.bfloat16))
    position = jnp.sum(onehot * counts, axis=0, keepdims=True).astype(jnp.int32) - 1
    slot = (route ^ plane) * capacity + position
    slots = lax.broadcasted_iota(jnp.int32, (experts * capacity, rows), 0)
    return jnp.where(slots == slot, 1.0, 0.0).astype(jnp.bfloat16)


def pack_kernel(experts, capacity, feat, *refs):
    plane, _, column = place()
    values, routes, refs = refs[:2], refs[2:4], refs[4:]
    moved, refs = refs[: experts - 1], refs[experts - 1 :]
    slices, blocks, sems = refs[:2], refs[2:4], refs[4]
    cols = pl.ds(pl.multiple_of(column * feat, feat), feat)
    copies = [
        pltpu.make_async_copy(routes[0], blocks[0], sems.at[0]),
        pltpu.make_async_copy(routes[1], blocks[1], sems.at[1]),
        pltpu.make_async_copy(values[0].at[:, cols], slices[0], sems.at[2]),
        pltpu.make_async_copy(values[1].at[:, cols], slices[1], sems.at[3]),
    ]
    for copy in copies:
        copy.start()
    for i in range(2):
        copies[i].wait()
        place_rows = placing(blocks[i][...], experts, capacity, plane)
        copies[2 + i].wait()
        sent = dot(place_rows[capacity:], slices[i][...]).astype(jnp.bfloat16)
        for s in range(experts - 1):
            moved[-1 - s][:, i * feat : (i + 1) * feat] = sent[s * capacity : (s + 1) * capacity]


def stay_kernel(experts, capacity, values, route, stay):
    plane, _, _ = place()
    place_rows = placing(route[...], experts, capacity, plane)
    stay[...] = dot(place_rows[:capacity], values[...]).astype(jnp.bfloat16)


def map_kernel(experts, capacity, routes, other_routes, out):
    plane, core, _ = place()
    for c in range(2):
        block = jnp.where(core == c, routes[...], other_routes[...])
        source = placing(block[0:1], experts, capacity, plane)
        target = placing(block[1:2], experts, capacity, plane)
        out[c] = dot_nt(target, source).astype(jnp.bfloat16)


def load_kernel(*refs):
    count = len(refs) // 2
    copies = [
        pltpu.make_async_copy(refs[i], refs[count + i], refs[-1].at[i]) for i in range(count)
    ]
    for copy in copies:
        copy.start()
    for copy in copies:
        copy.wait()


def stack_kernel(*refs):
    out = refs[-1]
    capacity = refs[0].shape[0]
    for s, ref in enumerate(refs[-2::-1]):
        out[s * capacity : (s + 1) * capacity, :] = ref[...]


def join_kernel(columns, stay_t, stay_s, *refs):
    _, _, column = place()
    parts, flats = refs[:-2], refs[-2:]
    capacity = stay_t.shape[0]
    feat = parts[0].shape[1] // 2
    for i, stay in enumerate((stay_t, stay_s)):
        flats[i][:capacity, :] = stay[...]
        for m in range(columns):
            cols = pl.ds(pl.multiple_of((column ^ m) * feat, feat), feat)
            flats[i][capacity:, cols] = parts[m][:, i * feat : (i + 1) * feat]


def part_pieces(hidden, w2, which, columns, out):
    half = w2.shape[1] // 2
    piece = half // columns
    for j in range(columns):
        cols = pl.ds(pl.multiple_of(which * half + j * piece, piece), piece)
        out[j] = dot(hidden, w2[:, cols]).astype(jnp.bfloat16)


def forward_kernel(columns, count, *refs):
    _, core, _ = place()
    flats, refs = refs[:count], refs[count:]
    w1, w2, send, refs = refs[0], refs[1], refs[2], refs[3:]
    for i in range(count):
        pre = dot(flats[i][...], w1[...])
        if len(refs) > count:
            refs[count + i][...] = pre
        hidden = gelu_tanh(pre).astype(jnp.bfloat16)
        refs[i][...] = hidden
        part_pieces(hidden, w2, 1 - core, columns, send.at[i])


def keep_kernel(columns, hidden_own, hidden_other, w2, *refs):
    _, core, _ = place()
    if len(refs) > 2:
        pre_own, pre_other, flat_own, flat_other, keep_own, keep_other = refs[:6]
        flat_t, hidden_t, slope = refs[6:]
    else:
        keep_own, keep_other = refs
    part_pieces(hidden_own[...], w2, core, columns, keep_own)
    part_pieces(hidden_other[...], w2, core, columns, keep_other)
    if len(refs) > 2:
        half = flat_own.shape[0]
        slope[:half, :] = gelu_slope(pre_own[...])
        slope[half:, :] = gelu_slope(pre_other[...])
        hidden_t[...] = jnp.concatenate([hidden_own[...], hidden_other[...]], axis=0).T
        step = 512
        for j in range(0, flat_own.shape[1], step):
            here = slice(j, j + step)
            both = jnp.concatenate([flat_own[:, here], flat_other[:, here]], axis=0)
            flat_t[here, :] = both.T


def pair_kernel(columns, keep_own, keep_other, *refs):
    _, core, column = place()
    half = keep_own.shape[1]
    got, (mine, *out) = refs[:-columns], refs[-columns:]
    got_own, got_other = got[0].at[0], got[-1].at[len(got) % 2]
    for m in range(columns):
        for which, keep, got in ((core, keep_own, got_other), (1 - core, keep_other, got_own)):
            rows = pl.ds(pl.multiple_of(which * half, 16), half)
            both = keep[column ^ m].astype(jnp.float32) + got[column ^ m].astype(jnp.float32)
            if m:
                out[m - 1][rows, :] = both.astype(jnp.bfloat16)
            else:
                mine[rows, :] = both


def total_kernel(columns, experts, *refs):
    sums, out = refs[:columns], refs[columns:]
    total = sums[0][...]
    for ref in sums[1:]:
        total = total + ref[...].astype(jnp.float32)
    total = total.astype(jnp.bfloat16)
    capacity = out[0].shape[0] // 2
    for s in range(experts):
        for c in range(2):
            start = (c * experts + s) * capacity
            out[-1 - s][c * capacity : (c + 1) * capacity, :] = total[start : start + capacity]


def home_kernel(experts, capacity, maps, *refs):
    got, out = refs[:experts], refs[experts:]
    for c in range(2):
        here = slice(c * capacity, (c + 1) * capacity)
        rows = jnp.concatenate([ref[here, :] for ref in got[::-1]], axis=0)
        by_slot = dot(maps[c], rows).astype(jnp.bfloat16)
        for s in range(experts):
            out[-1 - s][here, :] = by_slot[s * capacity : (s + 1) * capacity]


def upstream_kernel(columns, experts, loss_scale, *refs):
    sums, teacher, out = refs[:columns], refs[columns:-1], refs[-1]
    total = sums[0][...]
    for ref in sums[1:]:
        total = total + ref[...].astype(jnp.float32)
    capacity = teacher[0].shape[0] // 2
    rows = jnp.concatenate(
        [
            teacher[-1 - s][c * capacity : (c + 1) * capacity, :]
            for c in range(2)
            for s in range(experts)
        ],
        axis=0,
    ).astype(jnp.float32)
    out[...] = ((total - rows) * loss_scale).astype(jnp.bfloat16)


def backward_kernel(columns, places, first, last, *refs):
    _, core, column = place()
    pieces, refs = refs[: len(places)], refs[len(places) :]
    hidden_t, w2, refs = refs[0], refs[1], refs[2:]
    if not first:
        sum_in, refs = refs[0], refs[2:]
    if last:
        flat_t, slope, grad_second, grad_first, held_first, held_second, sems = refs
    else:
        grad_second, sum_out, held_second, sems = refs
    piece = pieces[0].shape[1]
    width = w2.shape[1]
    hidden_grad = None if first else sum_in[...]
    copies = []

    def leave(source, target):
        copies.append(pltpu.make_async_copy(source, target, sems.at[len(copies)]))
        copies[-1].start()

    used = []
    for ref, (other, m) in zip(pieces, places):
        which = 1 - core if other else core
        start = which * (width // 2) + (column ^ m) * piece
        cols = pl.ds(pl.multiple_of(start, piece), piece)
        half = ref.shape[0] // 2
        rows = jnp.concatenate(
            [ref[pl.ds(pl.multiple_of(block * half, 16), half), :] for block in (core, 1 - core)],
            axis=0,
        )
        used.append((rows, cols))
        term = dot_nt(rows, w2[:, cols])
        hidden_grad = term if hidden_grad is None else hidden_grad + term
    if last:
        pre_grad = (hidden_grad * slope[...]).astype(jnp.bfloat16)
        step = 256
        for j in range(width // step):
            here = slice(j * step, (j + 1) * step)
            held_first[here, :] = dot(flat_t[here, :], pre_grad).astype(jnp.bfloat16)
            leave(held_first.at[here, :], grad_first.at[here, :])
    else:
        sum_out[...] = hidden_grad
    for i, (rows, cols) in enumerate(used):
        held_second[i] = dot(hidden_t[...], rows).astype(jnp.bfloat16)
        leave(held_second.at[i], grad_second.at[:, cols])
    for copy in copies:
        copy.wait()


def by_kernels(
    teacher_in,
    student_in,
    teacher_route,
    student_route,
    teacher_w1,
    teacher_w2,
    student_w1,
    student_w2,
):
    groups, columns, experts, row_count, width, capacity = sizes(teacher_in)
    plane_rows = groups * capacity
    loss_scale = 1.0 / math.sqrt(row_count)
    feat = width // columns
    piece = feat // 2
    hid = teacher_w1.shape[2]
    f32 = jnp.float32

    def after(value, *others):
        return lax.optimization_barrier((value, others))[0]

    def over_planes(sent):
        return [partner(value, "dp", (experts - 1 - i) << 1) for i, value in enumerate(sent)]

    def spread(mine):
        return [mine] + [partner(mine, "expert", m) for m in range(1, columns)]

    def across(value):
        return partner(value, "dp", 1)

    def load(*weights):
        return call(
            load_kernel,
            [shape(*w.shape) for w in weights],
            weights,
            in_specs=[ANY] * len(weights),
            name="load",
            scratch=[pltpu.SemaphoreType.DMA((len(weights),))],
        )

    def forward(flats, w1, w2, keep_pre, name):
        half, count = plane_rows // 2, len(flats)
        pre = [shape(half, hid, dtype=f32)] * count if keep_pre else []
        return call(
            lambda *refs: forward_kernel(columns, count, *refs),
            [shape(count, columns, half, piece)] + [shape(half, hid)] * count + pre,
            [*flats, w1, w2],
            name=name,
        )

    def keep(own, other, w2, state, outs):
        return call(
            lambda *refs: keep_kernel(columns, *refs),
            [shape(columns, plane_rows // 2, piece)] * 2 + outs,
            [own, other, w2, *state],
            flops=(16 if state else 1) * plane_rows * width * hid,
            name="keep_s" if state else "keep_t",
        )

    def pair(kept, got):
        return call(
            lambda *refs: pair_kernel(columns, *refs),
            [shape(plane_rows, piece, dtype=f32)] + [shape(plane_rows, piece)] * (columns - 1),
            [*kept, *got],
            name="pair",
        )

    def collect(mine, *out):
        return [mine] + [partner(value, "expert", m + 1) for m, value in enumerate(out)]

    route_t = teacher_route.reshape(1, row_count)
    route_s = student_route.reshape(1, row_count)
    def stay(values, route):
        return call(
            lambda *refs: stay_kernel(experts, capacity, *refs),
            [shape(capacity, width)],
            [values, route],
            name="stay",
        )[0]

    sent = call(
        lambda *refs: pack_kernel(experts, capacity, feat, *refs),
        [shape(capacity, 2 * feat)] * (experts - 1),
        [teacher_in, student_in, route_t, route_s],
        in_specs=[ANY] * 4,
        grant=(253 << 20) // 4,
        name="pack",
        scratch=[pltpu.VMEM((row_count, feat), jnp.bfloat16)] * 2
        + [pltpu.VMEM((1, row_count), jnp.int32)] * 2
        + [pltpu.SemaphoreType.DMA((4,))],
    )
    stay_t, stay_s = stay(teacher_in, route_t), stay(student_in, route_s)
    routes = jnp.concatenate([route_t, route_s], axis=0)
    other_routes = across(routes)
    moved = after(over_planes(sent), stay_t, stay_s, other_routes)
    got = spread(
        call(stack_kernel, [shape((experts - 1) * capacity, 2 * feat)], moved, name="stack")[0]
    )
    w1_t, w2_t = load(teacher_w1[0], teacher_w2[0])
    w1_s, w2_s = load(student_w1[0], student_w2[0])
    (maps,) = call(
        lambda *refs: map_kernel(experts, capacity, *refs),
        [shape(2, experts * capacity, experts * capacity)],
        [routes, other_routes],
        name="maps",
    )
    flat_t_own, flat_own = call(
        lambda *refs: join_kernel(columns, *refs),
        [shape(plane_rows // 2, width)] * 2,
        [stay_t, stay_s, *after(got, w1_t, w1_s, maps)],
        name="join",
    )
    flat_t_other = across(flat_t_own)
    flat_other = across(flat_own)

    send, hidden_own = forward([flat_t_own], w1_t, w2_t, False, "forward_t")
    got_own = across(send)
    send, hidden_other = forward([flat_t_other], w1_t, w2_t, False, "forward_t")
    got_other = across(send)
    kept = keep(hidden_own, hidden_other, w2_t, [], [])
    pieces_t = pair(kept, [got_own, got_other])
    sums_t = collect(*pieces_t)

    flat_own, flat_other = after((flat_own, flat_other), pieces_t[0])
    send, hidden_own, hidden_other, pre_own, pre_other = forward(
        [flat_own, flat_other], w1_s, w2_s, True, "forward_s"
    )
    got = [across(send)]
    *kept, flat_t, hidden_t, slope = keep(
        hidden_own,
        hidden_other,
        w2_s,
        [pre_own, pre_other, flat_own, flat_other],
        [shape(width, plane_rows), shape(hid, plane_rows), shape(plane_rows, hid, dtype=f32)],
    )

    pieces_s = pair(kept, got)
    sums_s = collect(*pieces_s)

    home = call(
        lambda *refs: total_kernel(columns, experts, *refs),
        [shape(2 * capacity, piece)] * experts,
        after(sums_t, hidden_own),
    )
    home = [*over_planes(home[:-1]), home[-1]]
    slots = call(
        lambda *refs: home_kernel(experts, capacity, *refs),
        [shape(2 * capacity, piece)] * experts,
        [maps, *home],
        flops=2 * plane_rows * width * hid,
        name="home",
    )
    teachers = [*over_planes(slots[:-1]), slots[-1]]
    (upstream,) = call(
        lambda *refs: upstream_kernel(columns, experts, loss_scale, *refs),
        [shape(plane_rows, piece)],
        [*sums_s, *teachers],
    )
    def backward(pieces, state, last):
        first = state is None
        places = tuple(pieces)
        operands = [pieces[key] for key in places] + [hidden_t, w2_s]
        in_specs = [VMEM] * len(operands)
        aliases = {}
        if not first:
            operands += [state[1], state[0]]
            in_specs += [VMEM, ANY]
            aliases = {len(operands) - 1: 0}
        outs = [shape(hid, width)]
        scratch = [pltpu.VMEM((len(places), hid, piece), jnp.bfloat16)]
        copies = len(places)
        if last:
            operands += [flat_t, slope]
            in_specs += [VMEM, VMEM]
            outs += [shape(width, hid)]
            out_specs = [ANY, ANY]
            scratch = [pltpu.VMEM((width, hid), jnp.bfloat16)] + scratch
            copies += width // 256
        else:
            outs += [shape(plane_rows, hid, dtype=f32)]
            out_specs = [ANY, VMEM]
        return call(
            lambda *refs: backward_kernel(columns, places, first, last, *refs),
            outs,
            operands,
            out_specs=out_specs,
            in_specs=in_specs,
            scratch=scratch + [pltpu.SemaphoreType.DMA((copies,))],
            aliases=aliases,
        )

    grads = spread(upstream)
    state = backward({(0, 0): upstream, (1, 0): across(upstream)}, None, False)
    grads = after(grads, state[1])
    masks = range(1, columns)
    others = [across(grads[m]) for m in masks]
    state = backward({(0, m): grads[m] for m in masks}, state, False)
    grad_second, grad_first = backward(
        {(1, m): value for m, value in zip(masks, others)}, state, True
    )
    return (grad_first[None], grad_second[None])

def on_device(*arrays):
    _, columns, _, row_count, width, capacity = sizes(arrays[0])
    aligned = columns == 4 and capacity % 16 == 0 and row_count % 128 == 0 and width % (256 * columns) == 0
    return by_kernels(*arrays) if aligned else by_ops(*arrays)


def solution(mesh):
    return jax.shard_map(
        on_device,
        mesh=mesh,
        in_specs=(
            P("dp", None),
            P("dp", None),
            P("dp", None),
            P("dp", None),
            P("dp", None, "expert"),
            P("dp", "expert", None),
            P("dp", None, "expert"),
            P("dp", "expert", None),
        ),
        out_specs=(P("dp", None, "expert"), P("dp", "expert", None)),
        check_vma=False,
    )
```

```python
import math

import jax
import jax.numpy as jnp
from jax import lax
from jax.experimental import pallas as pl
from jax.experimental.pallas import tpu as pltpu
from jax.sharding import PartitionSpec as P

root_coef = math.sqrt(2.0 / math.pi)
cubic_coef = 0.044715


def partner(value, axis, mask):
    return lax.ppermute(value, axis, [(i, i ^ mask) for i in range(lax.axis_size(axis))])


def gelu_tanh(pre_act):
    inner_arg = root_coef * (pre_act + cubic_coef * pre_act * pre_act * pre_act)
    return 0.5 * pre_act * (1.0 + jnp.tanh(inner_arg))


def gelu_slope(pre_act):
    tangent = jnp.tanh(root_coef * (pre_act + cubic_coef * pre_act * pre_act * pre_act))
    return 0.5 * (1.0 + tangent) + 0.5 * pre_act * (1.0 - tangent * tangent) * root_coef * (
        1.0 + 3.0 * cubic_coef * pre_act * pre_act
    )


def dot(left, right):
    return jnp.dot(left, right, preferred_element_type=jnp.float32)


def ranks(routes, experts):
    onehot = (routes[..., None] == jnp.arange(experts, dtype=jnp.int32)).astype(jnp.int32)
    rank_table = jnp.cumsum(onehot, axis=1) - 1
    return jnp.sum(onehot * rank_table, axis=2)


def sizes(rows):
    groups = lax.axis_size("dp")
    experts = groups // 2
    row_count, width = rows.shape
    capacity = 2 * max(1, 3 * row_count // (4 * experts))
    return groups, lax.axis_size("expert"), experts, row_count, width, capacity


def by_ops(
    teacher_in,
    student_in,
    teacher_route,
    student_route,
    teacher_w1,
    teacher_w2,
    student_w1,
    student_w2,
):
    groups, columns, experts, row_count, width, capacity = sizes(teacher_in)
    plane_rows = groups * capacity
    dp = lax.axis_index("dp")
    column = lax.axis_index("expert")
    plane, core = dp // 2, dp % 2
    loss_scale = 1.0 / math.sqrt(row_count)
    feat = width // columns
    piece = feat // 2

    def dispatch(values, routes):
        position = ranks(routes[:, 0][None], experts)[0]
        slot = (routes[:, 0] ^ plane) * capacity + position
        placing = (
            jnp.arange(experts * capacity, dtype=jnp.int32)[:, None] == slot[None, :]
        ).astype(jnp.bfloat16)
        own_slice = lax.dynamic_slice(values, (0, column * feat), (row_count, feat))
        slots = dot(placing[capacity:], own_slice).astype(jnp.bfloat16)
        stay = dot(placing[:capacity], values).astype(jnp.bfloat16)
        moved = [
            partner(slots[(s - 1) * capacity : s * capacity], "dp", s << 1)
            for s in range(1, experts)
        ]
        mine = jnp.concatenate(moved, axis=0)
        buffer = jnp.concatenate([stay, jnp.zeros((mine.shape[0], width), jnp.bfloat16)], axis=0)
        for m in range(columns):
            got = partner(mine, "expert", m) if m else mine
            buffer = lax.dynamic_update_slice(buffer, got, (capacity, (column ^ m) * feat))
        other = partner(buffer, "dp", 1)
        first = jnp.where(core == 0, buffer, other)
        second = jnp.where(core == 0, other, buffer)
        return jnp.concatenate([first, second], axis=0)

    def forward(flat, w1, w2):
        pre = dot(flat, w1)
        hidden = gelu_tanh(pre).astype(jnp.bfloat16)
        part = dot(hidden, w2).astype(jnp.bfloat16).reshape(plane_rows, 2, columns, piece)
        part = part.transpose(1, 2, 0, 3)
        return pre, hidden, part

    def plane_sum(part):
        keep = lax.dynamic_index_in_dim(part, core, 0, keepdims=False)
        send = lax.dynamic_index_in_dim(part, 1 - core, 0, keepdims=False)
        pair = (
            keep.astype(jnp.float32) + partner(send, "dp", 1).astype(jnp.float32)
        ).astype(jnp.bfloat16)
        total = lax.dynamic_index_in_dim(pair, column, 0, keepdims=False).astype(jnp.float32)
        for m in range(1, columns):
            out = lax.dynamic_index_in_dim(pair, column ^ m, 0, keepdims=False)
            total = total + partner(out, "expert", m).astype(jnp.float32)
        return total

    routes = jnp.concatenate([teacher_route, student_route], axis=1)
    table = lax.all_gather(routes, "dp", axis=0, tiled=True).reshape(groups, row_count, 2)
    teacher_all, student_all = table[:, :, 0], table[:, :, 1]
    block = jnp.arange(groups, dtype=jnp.int32)[:, None]
    block_plane, block_core = block // 2, block % 2
    teacher_row = (
        (teacher_all ^ plane) * plane_rows
        + (block_core * experts + (block_plane ^ teacher_all)) * capacity
        + ranks(teacher_all, experts)
    )
    student_row = jnp.where(student_all == plane, ranks(student_all, experts), -1)
    hits = jnp.arange(capacity, dtype=jnp.int32)[None, :, None] == student_row[:, None, :]
    source = jnp.sum(jnp.where(hits, teacher_row[:, None, :] + 1, 0), axis=2) - 1
    source = source.reshape(experts, 2, capacity)
    source = source[jnp.arange(experts, dtype=jnp.int32) ^ plane].transpose(1, 0, 2)
    source = source.reshape(plane_rows)

    teacher_flat = dispatch(teacher_in, teacher_route)
    student_flat = dispatch(student_in, student_route)
    _, _, teacher_part = forward(teacher_flat, teacher_w1[0], teacher_w2[0])
    teacher_sum = plane_sum(teacher_part).astype(jnp.bfloat16)
    teacher_sums = jnp.concatenate(
        [teacher_sum] + [partner(teacher_sum, "dp", s << 1) for s in range(1, experts)], axis=0
    )
    student_pre, student_hidden, student_part = forward(
        student_flat, student_w1[0], student_w2[0]
    )
    pick = (
        source[:, None] == jnp.arange(experts * plane_rows, dtype=jnp.int32)[None, :]
    ).astype(jnp.bfloat16)
    teacher_rows = dot(pick, teacher_sums)
    student_sum = plane_sum(student_part)
    upstream = ((student_sum - teacher_rows) * loss_scale).astype(jnp.bfloat16)

    half = jnp.zeros((plane_rows, width // 2), jnp.bfloat16)
    for m in range(columns):
        got = partner(upstream, "expert", m) if m else upstream
        half = lax.dynamic_update_slice(half, got, (0, (column ^ m) * piece))
    other_half = partner(half, "dp", 1)
    grad_flat = jnp.concatenate(
        [jnp.where(core == 0, half, other_half), jnp.where(core == 0, other_half, half)], axis=1
    )
    hidden_grad = dot(grad_flat, student_w2[0].T)
    pre_grad = (hidden_grad * gelu_slope(student_pre)).astype(jnp.bfloat16)
    grad_second = dot(student_hidden.T, grad_flat).astype(jnp.bfloat16)
    grad_first = dot(student_flat.T, pre_grad).astype(jnp.bfloat16)
    return (grad_first[None], grad_second[None])


def place():
    dp = lax.axis_index("dp")
    return dp // 2, dp % 2, lax.axis_index("expert")


VMEM = pl.BlockSpec(memory_space=pltpu.VMEM)
ANY = pl.BlockSpec(memory_space=pl.ANY)


def call(kernel, outs, operands, out_specs=None, in_specs=None, scratch=(), aliases=None, grant=20 << 20, flops=0, name=None):
    return pl.pallas_call(
        kernel,
        name=name,
        out_shape=outs,
        in_specs=in_specs or [VMEM] * len(operands),
        out_specs=out_specs or [VMEM] * len(outs),
        scratch_shapes=list(scratch),
        input_output_aliases=aliases or {},
        compiler_params=pltpu.CompilerParams(vmem_limit_bytes=grant),
        cost_estimate=pl.CostEstimate(flops=flops, bytes_accessed=0, transcendentals=0),
    )(*operands)


def shape(*dims, dtype=jnp.bfloat16):
    return jax.ShapeDtypeStruct(dims, dtype)


def dot_tn(left, right):
    return lax.dot_general(
        left, right, (((0,), (0,)), ((), ())), preferred_element_type=jnp.float32
    )


def dot_nt(left, right):
    return lax.dot_general(
        left, right, (((1,), (1,)), ((), ())), preferred_element_type=jnp.float32
    )


def placing(route, experts, capacity, plane):
    rows = route.shape[1]
    known = lax.broadcasted_iota(jnp.int32, (16 * (-(-experts // 16)), rows), 0)
    onehot = jnp.where(known == route, 1.0, 0.0)
    upto = lax.broadcasted_iota(jnp.int32, (rows, rows), 0) <= lax.broadcasted_iota(
        jnp.int32, (rows, rows), 1
    )
    counts = dot(onehot.astype(jnp.bfloat16), jnp.where(upto, 1.0, 0.0).astype(jnp.bfloat16))
    position = jnp.sum(onehot * counts, axis=0, keepdims=True).astype(jnp.int32) - 1
    slot = (route ^ plane) * capacity + position
    slots = lax.broadcasted_iota(jnp.int32, (experts * capacity, rows), 0)
    return jnp.where(slots == slot, 1.0, 0.0).astype(jnp.bfloat16)


def pack_kernel(experts, capacity, feat, *refs):
    plane, _, column = place()
    values, routes, refs = refs[:2], refs[2:4], refs[4:]
    moved, refs = refs[: experts - 1], refs[experts - 1 :]
    slices, blocks, sems = refs[:2], refs[2:4], refs[4]
    cols = pl.ds(pl.multiple_of(column * feat, feat), feat)
    copies = [
        pltpu.make_async_copy(routes[0], blocks[0], sems.at[0]),
        pltpu.make_async_copy(routes[1], blocks[1], sems.at[1]),
        pltpu.make_async_copy(values[0].at[:, cols], slices[0], sems.at[2]),
        pltpu.make_async_copy(values[1].at[:, cols], slices[1], sems.at[3]),
    ]
    for copy in copies:
        copy.start()
    for i in range(2):
        copies[i].wait()
        place_rows = placing(blocks[i][...], experts, capacity, plane)
        copies[2 + i].wait()
        sent = dot(place_rows[capacity:], slices[i][...]).astype(jnp.bfloat16)
        for s in range(experts - 1):
            moved[-1 - s][:, i * feat : (i + 1) * feat] = sent[s * capacity : (s + 1) * capacity]


def stay_kernel(experts, capacity, values, route, stay):
    plane, _, _ = place()
    place_rows = placing(route[...], experts, capacity, plane)
    stay[...] = dot(place_rows[:capacity], values[...]).astype(jnp.bfloat16)


def map_kernel(experts, capacity, routes, other_routes, out):
    plane, core, _ = place()
    for c in range(2):
        block = jnp.where(core == c, routes[...], other_routes[...])
        source = placing(block[0:1], experts, capacity, plane)
        target = placing(block[1:2], experts, capacity, plane)
        out[c] = dot_nt(target, source).astype(jnp.bfloat16)


def load_kernel(*refs):
    count = len(refs) // 2
    copies = [
        pltpu.make_async_copy(refs[i], refs[count + i], refs[-1].at[i]) for i in range(count)
    ]
    for copy in copies:
        copy.start()
    for copy in copies:
        copy.wait()


def stack_kernel(*refs):
    out = refs[-1]
    capacity = refs[0].shape[0]
    for s, ref in enumerate(refs[-2::-1]):
        out[s * capacity : (s + 1) * capacity, :] = ref[...]


def join_kernel(columns, stay_t, stay_s, *refs):
    _, _, column = place()
    parts, flats = refs[:-2], refs[-2:]
    capacity = stay_t.shape[0]
    feat = parts[0].shape[1] // 2
    for i, stay in enumerate((stay_t, stay_s)):
        flats[i][:capacity, :] = stay[...]
        for m in range(columns):
            cols = pl.ds(pl.multiple_of((column ^ m) * feat, feat), feat)
            flats[i][capacity:, cols] = parts[m][:, i * feat : (i + 1) * feat]


def part_pieces(hidden, w2, which, columns, out):
    half = w2.shape[1] // 2
    piece = half // columns
    for j in range(columns):
        cols = pl.ds(pl.multiple_of(which * half + j * piece, piece), piece)
        out[j] = dot(hidden, w2[:, cols]).astype(jnp.bfloat16)


def forward_kernel(columns, count, *refs):
    _, core, _ = place()
    flats, refs = refs[:count], refs[count:]
    w1, w2, send, refs = refs[0], refs[1], refs[2], refs[3:]
    for i in range(count):
        pre = dot(flats[i][...], w1[...])
        if len(refs) > count:
            refs[count + i][...] = pre
        hidden = gelu_tanh(pre).astype(jnp.bfloat16)
        refs[i][...] = hidden
        part_pieces(hidden, w2, 1 - core, columns, send.at[i])


def keep_kernel(columns, hidden_own, hidden_other, w2, *refs):
    _, core, _ = place()
    if len(refs) > 2:
        pre_own, pre_other, flat_own, flat_other, keep_own, keep_other = refs[:6]
        flat_t, hidden_t, slope = refs[6:]
    else:
        keep_own, keep_other = refs
    part_pieces(hidden_own[...], w2, core, columns, keep_own)
    part_pieces(hidden_other[...], w2, core, columns, keep_other)
    if len(refs) > 2:
        half = flat_own.shape[0]
        slope[:half, :] = gelu_slope(pre_own[...])
        slope[half:, :] = gelu_slope(pre_other[...])
        hidden_t[...] = jnp.concatenate([hidden_own[...], hidden_other[...]], axis=0).T
        step = 512
        for j in range(0, flat_own.shape[1], step):
            here = slice(j, j + step)
            both = jnp.concatenate([flat_own[:, here], flat_other[:, here]], axis=0)
            flat_t[here, :] = both.T


def pair_kernel(columns, keep_own, keep_other, *refs):
    _, core, column = place()
    half = keep_own.shape[1]
    got, (mine, *out) = refs[:-columns], refs[-columns:]
    got_own, got_other = got[0].at[0], got[-1].at[len(got) % 2]
    for m in range(columns):
        for which, keep, got in ((core, keep_own, got_other), (1 - core, keep_other, got_own)):
            rows = pl.ds(pl.multiple_of(which * half, 16), half)
            both = keep[column ^ m].astype(jnp.float32) + got[column ^ m].astype(jnp.float32)
            if m:
                out[m - 1][rows, :] = both.astype(jnp.bfloat16)
            else:
                mine[rows, :] = both


def total_kernel(columns, experts, *refs):
    sums, out = refs[:columns], refs[columns:]
    total = sums[0][...]
    for ref in sums[1:]:
        total = total + ref[...].astype(jnp.float32)
    total = total.astype(jnp.bfloat16)
    capacity = out[0].shape[0] // 2
    for s in range(experts):
        for c in range(2):
            start = (c * experts + s) * capacity
            out[-1 - s][c * capacity : (c + 1) * capacity, :] = total[start : start + capacity]


def home_kernel(experts, capacity, maps, *refs):
    got, out = refs[:experts], refs[experts:]
    for c in range(2):
        here = slice(c * capacity, (c + 1) * capacity)
        rows = jnp.concatenate([ref[here, :] for ref in got[::-1]], axis=0)
        by_slot = dot(maps[c], rows).astype(jnp.bfloat16)
        for s in range(experts):
            out[-1 - s][here, :] = by_slot[s * capacity : (s + 1) * capacity]


def upstream_kernel(columns, experts, loss_scale, *refs):
    sums, teacher, out = refs[:columns], refs[columns:-1], refs[-1]
    total = sums[0][...]
    for ref in sums[1:]:
        total = total + ref[...].astype(jnp.float32)
    capacity = teacher[0].shape[0] // 2
    rows = jnp.concatenate(
        [
            teacher[-1 - s][c * capacity : (c + 1) * capacity, :]
            for c in range(2)
            for s in range(experts)
        ],
        axis=0,
    ).astype(jnp.float32)
    out[...] = ((total - rows) * loss_scale).astype(jnp.bfloat16)


def backward_kernel(columns, places, first, last, *refs):
    _, core, column = place()
    pieces, refs = refs[: len(places)], refs[len(places) :]
    hidden_t, w2, refs = refs[0], refs[1], refs[2:]
    if not first:
        sum_in, refs = refs[0], refs[2:]
    if last:
        flat_t, slope, grad_second, grad_first, held_first, held_second, sems = refs
    else:
        grad_second, sum_out, held_second, sems = refs
    piece = pieces[0].shape[1]
    width = w2.shape[1]
    hidden_grad = None if first else sum_in[...]
    copies = []

    def leave(source, target):
        copies.append(pltpu.make_async_copy(source, target, sems.at[len(copies)]))
        copies[-1].start()

    used = []
    for ref, (other, m) in zip(pieces, places):
        which = 1 - core if other else core
        start = which * (width // 2) + (column ^ m) * piece
        cols = pl.ds(pl.multiple_of(start, piece), piece)
        half = ref.shape[0] // 2
        rows = jnp.concatenate(
            [ref[pl.ds(pl.multiple_of(block * half, 16), half), :] for block in (core, 1 - core)],
            axis=0,
        )
        used.append((rows, cols))
        term = dot_nt(rows, w2[:, cols])
        hidden_grad = term if hidden_grad is None else hidden_grad + term
    if last:
        pre_grad = (hidden_grad * slope[...]).astype(jnp.bfloat16)
        step = 512
        for j in range(width // step):
            here = slice(j * step, (j + 1) * step)
            held_first[here, :] = dot(flat_t[here, :], pre_grad).astype(jnp.bfloat16)
            leave(held_first.at[here, :], grad_first.at[here, :])
    else:
        sum_out[...] = hidden_grad
    for i, (rows, cols) in enumerate(used):
        held_second[i] = dot(hidden_t[...], rows).astype(jnp.bfloat16)
        leave(held_second.at[i], grad_second.at[:, cols])
    for copy in copies:
        copy.wait()


def by_kernels(
    teacher_in,
    student_in,
    teacher_route,
    student_route,
    teacher_w1,
    teacher_w2,
    student_w1,
    student_w2,
):
    groups, columns, experts, row_count, width, capacity = sizes(teacher_in)
    plane_rows = groups * capacity
    loss_scale = 1.0 / math.sqrt(row_count)
    feat = width // columns
    piece = feat // 2
    hid = teacher_w1.shape[2]
    f32 = jnp.float32

    def after(value, *others):
        return lax.optimization_barrier((value, others))[0]

    def over_planes(sent):
        return [partner(value, "dp", (experts - 1 - i) << 1) for i, value in enumerate(sent)]

    def spread(mine):
        return [mine] + [partner(mine, "expert", m) for m in range(1, columns)]

    def across(value):
        return partner(value, "dp", 1)

    def load(*weights):
        return call(
            load_kernel,
            [shape(*w.shape) for w in weights],
            weights,
            in_specs=[ANY] * len(weights),
            name="load",
            scratch=[pltpu.SemaphoreType.DMA((len(weights),))],
        )

    def forward(flats, w1, w2, keep_pre, name):
        half, count = plane_rows // 2, len(flats)
        pre = [shape(half, hid, dtype=f32)] * count if keep_pre else []
        return call(
            lambda *refs: forward_kernel(columns, count, *refs),
            [shape(count, columns, half, piece)] + [shape(half, hid)] * count + pre,
            [*flats, w1, w2],
            name=name,
        )

    def keep(own, other, w2, state, outs):
        return call(
            lambda *refs: keep_kernel(columns, *refs),
            [shape(columns, plane_rows // 2, piece)] * 2 + outs,
            [own, other, w2, *state],
            flops=(64 if state else 1) * plane_rows * width * hid,
            name="keep_s" if state else "keep_t",
        )

    def pair(kept, got):
        return call(
            lambda *refs: pair_kernel(columns, *refs),
            [shape(plane_rows, piece, dtype=f32)] + [shape(plane_rows, piece)] * (columns - 1),
            [*kept, *got],
            name="pair",
        )

    def collect(mine, *out):
        return [mine] + [partner(value, "expert", m + 1) for m, value in enumerate(out)]

    route_t = teacher_route.reshape(1, row_count)
    route_s = student_route.reshape(1, row_count)
    def stay(values, route):
        return call(
            lambda *refs: stay_kernel(experts, capacity, *refs),
            [shape(capacity, width)],
            [values, route],
            name="stay",
        )[0]

    sent = call(
        lambda *refs: pack_kernel(experts, capacity, feat, *refs),
        [shape(capacity, 2 * feat)] * (experts - 1),
        [teacher_in, student_in, route_t, route_s],
        in_specs=[ANY] * 4,
        grant=(253 << 20) // 4,
        name="pack",
        scratch=[pltpu.VMEM((row_count, feat), jnp.bfloat16)] * 2
        + [pltpu.VMEM((1, row_count), jnp.int32)] * 2
        + [pltpu.SemaphoreType.DMA((4,))],
    )
    stay_t, stay_s = stay(teacher_in, route_t), stay(student_in, route_s)
    routes = jnp.concatenate([route_t, route_s], axis=0)
    other_routes = across(routes)
    moved = after(over_planes(sent), stay_t, stay_s, other_routes)
    got = spread(
        call(stack_kernel, [shape((experts - 1) * capacity, 2 * feat)], moved, name="stack")[0]
    )
    w1_t, w2_t = load(teacher_w1[0], teacher_w2[0])
    w1_s, w2_s = load(student_w1[0], student_w2[0])
    (maps,) = call(
        lambda *refs: map_kernel(experts, capacity, *refs),
        [shape(2, experts * capacity, experts * capacity)],
        [routes, other_routes],
        name="maps",
    )
    flat_t_own, flat_own = call(
        lambda *refs: join_kernel(columns, *refs),
        [shape(plane_rows // 2, width)] * 2,
        [stay_t, stay_s, *after(got, w1_t, w1_s, maps)],
        name="join",
    )
    flat_t_other = across(flat_t_own)
    flat_other = across(flat_own)

    send, hidden_own = forward([flat_t_own], w1_t, w2_t, False, "forward_t")
    got_own = across(send)
    send, hidden_other = forward([flat_t_other], w1_t, w2_t, False, "forward_t")
    got_other = across(send)
    kept = keep(hidden_own, hidden_other, w2_t, [], [])
    pieces_t = pair(kept, [got_own, got_other])
    sums_t = collect(*pieces_t)

    flat_own, flat_other = after((flat_own, flat_other), pieces_t[0])
    send, hidden_own, hidden_other, pre_own, pre_other = forward(
        [flat_own, flat_other], w1_s, w2_s, True, "forward_s"
    )
    got = [across(send)]
    *kept, flat_t, hidden_t, slope = keep(
        hidden_own,
        hidden_other,
        w2_s,
        [pre_own, pre_other, flat_own, flat_other],
        [shape(width, plane_rows), shape(hid, plane_rows), shape(plane_rows, hid, dtype=f32)],
    )

    pieces_s = pair(kept, got)
    sums_s = collect(*pieces_s)

    home = call(
        lambda *refs: total_kernel(columns, experts, *refs),
        [shape(2 * capacity, piece)] * experts,
        after(sums_t, pieces_s[0]),
    )
    home = [*over_planes(home[:-1]), home[-1]]
    slots = call(
        lambda *refs: home_kernel(experts, capacity, *refs),
        [shape(2 * capacity, piece)] * experts,
        [maps, *home],
        flops=4 * plane_rows * width * hid,
        name="home",
    )
    *sent, near, own = slots
    teachers = [*over_planes([*sent, after(near, sums_s[1])]), own]
    (upstream,) = call(
        lambda *refs: upstream_kernel(columns, experts, loss_scale, *refs),
        [shape(plane_rows, piece)],
        [*sums_s, *teachers],
    )
    def backward(pieces, state, last):
        first = state is None
        places = tuple(pieces)
        operands = [pieces[key] for key in places] + [hidden_t, w2_s]
        in_specs = [VMEM] * len(operands)
        aliases = {}
        if not first:
            operands += [state[1], state[0]]
            in_specs += [VMEM, ANY]
            aliases = {len(operands) - 1: 0}
        outs = [shape(hid, width)]
        scratch = [pltpu.VMEM((len(places), hid, piece), jnp.bfloat16)]
        copies = len(places)
        if last:
            operands += [flat_t, slope]
            in_specs += [VMEM, VMEM]
            outs += [shape(width, hid)]
            out_specs = [ANY, ANY]
            scratch = [pltpu.VMEM((width, hid), jnp.bfloat16)] + scratch
            copies += width // 512
        else:
            outs += [shape(plane_rows, hid, dtype=f32)]
            out_specs = [ANY, VMEM]
        return call(
            lambda *refs: backward_kernel(columns, places, first, last, *refs),
            outs,
            operands,
            out_specs=out_specs,
            in_specs=in_specs,
            scratch=scratch + [pltpu.SemaphoreType.DMA((copies,))],
            aliases=aliases,
        )

    grads = spread(upstream)
    state = backward({(0, 0): upstream, (1, 0): across(upstream)}, None, False)
    *near, far = after(grads[1:], state[1])
    state = backward({(0, 3): far}, state, False)
    near = after(near, state[1])
    others = [across(value) for value in (*near, far)]
    state = backward({(0, m + 1): near[m] for m in range(2)}, state, False)
    grad_second, grad_first = backward(
        {(1, m + 1): value for m, value in enumerate(others)}, state, True
    )
    return (grad_first[None], grad_second[None])

def on_device(*arrays):
    _, columns, _, row_count, width, capacity = sizes(arrays[0])
    aligned = columns == 4 and capacity % 16 == 0 and row_count % 128 == 0 and width % (256 * columns) == 0
    return by_kernels(*arrays) if aligned else by_ops(*arrays)


def solution(mesh):
    return jax.shard_map(
        on_device,
        mesh=mesh,
        in_specs=(
            P("dp", None),
            P("dp", None),
            P("dp", None),
            P("dp", None),
            P("dp", None, "expert"),
            P("dp", "expert", None),
            P("dp", None, "expert"),
            P("dp", "expert", None),
        ),
        out_specs=(P("dp", None, "expert"), P("dp", "expert", None)),
        check_vma=False,
    )
```

```python
import math

import jax
import jax.numpy as jnp
from jax import lax
from jax.experimental import pallas as pl
from jax.experimental.pallas import tpu as pltpu
from jax.sharding import PartitionSpec as P

root_coef = math.sqrt(2.0 / math.pi)
cubic_coef = 0.044715


def partner(value, axis, mask):
    return lax.ppermute(value, axis, [(i, i ^ mask) for i in range(lax.axis_size(axis))])


def gelu_tanh(pre_act):
    inner_arg = root_coef * (pre_act + cubic_coef * pre_act * pre_act * pre_act)
    return 0.5 * pre_act * (1.0 + jnp.tanh(inner_arg))


def gelu_slope(pre_act):
    tangent = jnp.tanh(root_coef * (pre_act + cubic_coef * pre_act * pre_act * pre_act))
    return 0.5 * (1.0 + tangent) + 0.5 * pre_act * (1.0 - tangent * tangent) * root_coef * (
        1.0 + 3.0 * cubic_coef * pre_act * pre_act
    )


def dot(left, right):
    return jnp.dot(left, right, preferred_element_type=jnp.float32)


def ranks(routes, experts):
    onehot = (routes[..., None] == jnp.arange(experts, dtype=jnp.int32)).astype(jnp.int32)
    rank_table = jnp.cumsum(onehot, axis=1) - 1
    return jnp.sum(onehot * rank_table, axis=2)


def sizes(rows):
    groups = lax.axis_size("dp")
    experts = groups // 2
    row_count, width = rows.shape
    capacity = 2 * max(1, 3 * row_count // (4 * experts))
    return groups, lax.axis_size("expert"), experts, row_count, width, capacity


def by_ops(
    teacher_in,
    student_in,
    teacher_route,
    student_route,
    teacher_w1,
    teacher_w2,
    student_w1,
    student_w2,
):
    groups, columns, experts, row_count, width, capacity = sizes(teacher_in)
    plane_rows = groups * capacity
    dp = lax.axis_index("dp")
    column = lax.axis_index("expert")
    plane, core = dp // 2, dp % 2
    loss_scale = 1.0 / math.sqrt(row_count)
    feat = width // columns
    piece = feat // 2

    def dispatch(values, routes):
        position = ranks(routes[:, 0][None], experts)[0]
        slot = (routes[:, 0] ^ plane) * capacity + position
        placing = (
            jnp.arange(experts * capacity, dtype=jnp.int32)[:, None] == slot[None, :]
        ).astype(jnp.bfloat16)
        own_slice = lax.dynamic_slice(values, (0, column * feat), (row_count, feat))
        slots = dot(placing[capacity:], own_slice).astype(jnp.bfloat16)
        stay = dot(placing[:capacity], values).astype(jnp.bfloat16)
        moved = [
            partner(slots[(s - 1) * capacity : s * capacity], "dp", s << 1)
            for s in range(1, experts)
        ]
        mine = jnp.concatenate(moved, axis=0)
        buffer = jnp.concatenate([stay, jnp.zeros((mine.shape[0], width), jnp.bfloat16)], axis=0)
        for m in range(columns):
            got = partner(mine, "expert", m) if m else mine
            buffer = lax.dynamic_update_slice(buffer, got, (capacity, (column ^ m) * feat))
        other = partner(buffer, "dp", 1)
        first = jnp.where(core == 0, buffer, other)
        second = jnp.where(core == 0, other, buffer)
        return jnp.concatenate([first, second], axis=0)

    def forward(flat, w1, w2):
        pre = dot(flat, w1)
        hidden = gelu_tanh(pre).astype(jnp.bfloat16)
        part = dot(hidden, w2).astype(jnp.bfloat16).reshape(plane_rows, 2, columns, piece)
        part = part.transpose(1, 2, 0, 3)
        return pre, hidden, part

    def plane_sum(part):
        keep = lax.dynamic_index_in_dim(part, core, 0, keepdims=False)
        send = lax.dynamic_index_in_dim(part, 1 - core, 0, keepdims=False)
        pair = (
            keep.astype(jnp.float32) + partner(send, "dp", 1).astype(jnp.float32)
        ).astype(jnp.bfloat16)
        total = lax.dynamic_index_in_dim(pair, column, 0, keepdims=False).astype(jnp.float32)
        for m in range(1, columns):
            out = lax.dynamic_index_in_dim(pair, column ^ m, 0, keepdims=False)
            total = total + partner(out, "expert", m).astype(jnp.float32)
        return total

    routes = jnp.concatenate([teacher_route, student_route], axis=1)
    table = lax.all_gather(routes, "dp", axis=0, tiled=True).reshape(groups, row_count, 2)
    teacher_all, student_all = table[:, :, 0], table[:, :, 1]
    block = jnp.arange(groups, dtype=jnp.int32)[:, None]
    block_plane, block_core = block // 2, block % 2
    teacher_row = (
        (teacher_all ^ plane) * plane_rows
        + (block_core * experts + (block_plane ^ teacher_all)) * capacity
        + ranks(teacher_all, experts)
    )
    student_row = jnp.where(student_all == plane, ranks(student_all, experts), -1)
    hits = jnp.arange(capacity, dtype=jnp.int32)[None, :, None] == student_row[:, None, :]
    source = jnp.sum(jnp.where(hits, teacher_row[:, None, :] + 1, 0), axis=2) - 1
    source = source.reshape(experts, 2, capacity)
    source = source[jnp.arange(experts, dtype=jnp.int32) ^ plane].transpose(1, 0, 2)
    source = source.reshape(plane_rows)

    teacher_flat = dispatch(teacher_in, teacher_route)
    student_flat = dispatch(student_in, student_route)
    _, _, teacher_part = forward(teacher_flat, teacher_w1[0], teacher_w2[0])
    teacher_sum = plane_sum(teacher_part).astype(jnp.bfloat16)
    teacher_sums = jnp.concatenate(
        [teacher_sum] + [partner(teacher_sum, "dp", s << 1) for s in range(1, experts)], axis=0
    )
    student_pre, student_hidden, student_part = forward(
        student_flat, student_w1[0], student_w2[0]
    )
    pick = (
        source[:, None] == jnp.arange(experts * plane_rows, dtype=jnp.int32)[None, :]
    ).astype(jnp.bfloat16)
    teacher_rows = dot(pick, teacher_sums)
    student_sum = plane_sum(student_part)
    upstream = ((student_sum - teacher_rows) * loss_scale).astype(jnp.bfloat16)

    half = jnp.zeros((plane_rows, width // 2), jnp.bfloat16)
    for m in range(columns):
        got = partner(upstream, "expert", m) if m else upstream
        half = lax.dynamic_update_slice(half, got, (0, (column ^ m) * piece))
    other_half = partner(half, "dp", 1)
    grad_flat = jnp.concatenate(
        [jnp.where(core == 0, half, other_half), jnp.where(core == 0, other_half, half)], axis=1
    )
    hidden_grad = dot(grad_flat, student_w2[0].T)
    pre_grad = (hidden_grad * gelu_slope(student_pre)).astype(jnp.bfloat16)
    grad_second = dot(student_hidden.T, grad_flat).astype(jnp.bfloat16)
    grad_first = dot(student_flat.T, pre_grad).astype(jnp.bfloat16)
    return (grad_first[None], grad_second[None])


def place():
    dp = lax.axis_index("dp")
    return dp // 2, dp % 2, lax.axis_index("expert")


VMEM = pl.BlockSpec(memory_space=pltpu.VMEM)
ANY = pl.BlockSpec(memory_space=pl.ANY)


def call(kernel, outs, operands, out_specs=None, in_specs=None, scratch=(), aliases=None, grant=20 << 20, flops=0, name=None):
    return pl.pallas_call(
        kernel,
        name=name,
        out_shape=outs,
        in_specs=in_specs or [VMEM] * len(operands),
        out_specs=out_specs or [VMEM] * len(outs),
        scratch_shapes=list(scratch),
        input_output_aliases=aliases or {},
        compiler_params=pltpu.CompilerParams(vmem_limit_bytes=grant),
        cost_estimate=pl.CostEstimate(flops=flops, bytes_accessed=0, transcendentals=0),
    )(*operands)


def shape(*dims, dtype=jnp.bfloat16):
    return jax.ShapeDtypeStruct(dims, dtype)


def dot_tn(left, right):
    return lax.dot_general(
        left, right, (((0,), (0,)), ((), ())), preferred_element_type=jnp.float32
    )


def dot_nt(left, right):
    return lax.dot_general(
        left, right, (((1,), (1,)), ((), ())), preferred_element_type=jnp.float32
    )


def placing(route, experts, capacity, plane):
    rows = route.shape[1]
    known = lax.broadcasted_iota(jnp.int32, (16 * (-(-experts // 16)), rows), 0)
    onehot = jnp.where(known == route, 1.0, 0.0)
    upto = lax.broadcasted_iota(jnp.int32, (rows, rows), 0) <= lax.broadcasted_iota(
        jnp.int32, (rows, rows), 1
    )
    counts = dot(onehot.astype(jnp.bfloat16), jnp.where(upto, 1.0, 0.0).astype(jnp.bfloat16))
    position = jnp.sum(onehot * counts, axis=0, keepdims=True).astype(jnp.int32) - 1
    slot = (route ^ plane) * capacity + position
    slots = lax.broadcasted_iota(jnp.int32, (experts * capacity, rows), 0)
    return jnp.where(slots == slot, 1.0, 0.0).astype(jnp.bfloat16)


def pack_kernel(experts, capacity, feat, *refs):
    plane, _, column = place()
    values, routes, refs = refs[:2], refs[2:4], refs[4:]
    moved, refs = refs[: experts - 1], refs[experts - 1 :]
    slices, blocks, sems = refs[:2], refs[2:4], refs[4]
    cols = pl.ds(pl.multiple_of(column * feat, feat), feat)
    copies = [
        pltpu.make_async_copy(routes[0], blocks[0], sems.at[0]),
        pltpu.make_async_copy(routes[1], blocks[1], sems.at[1]),
        pltpu.make_async_copy(values[0].at[:, cols], slices[0], sems.at[2]),
        pltpu.make_async_copy(values[1].at[:, cols], slices[1], sems.at[3]),
    ]
    for copy in copies:
        copy.start()
    for i in range(2):
        copies[i].wait()
        place_rows = placing(blocks[i][...], experts, capacity, plane)
        copies[2 + i].wait()
        sent = dot(place_rows[capacity:], slices[i][...]).astype(jnp.bfloat16)
        for s in range(experts - 1):
            moved[-1 - s][:, i * feat : (i + 1) * feat] = sent[s * capacity : (s + 1) * capacity]


def stay_kernel(experts, capacity, values, route, stay):
    plane, _, _ = place()
    place_rows = placing(route[...], experts, capacity, plane)
    stay[...] = dot(place_rows[:capacity], values[...]).astype(jnp.bfloat16)


def map_kernel(experts, capacity, routes, other_routes, out):
    plane, core, _ = place()
    for c in range(2):
        block = jnp.where(core == c, routes[...], other_routes[...])
        source = placing(block[0:1], experts, capacity, plane)
        target = placing(block[1:2], experts, capacity, plane)
        out[c] = dot_nt(target, source).astype(jnp.bfloat16)


def load_kernel(*refs):
    count = len(refs) // 2
    copies = [
        pltpu.make_async_copy(refs[i], refs[count + i], refs[-1].at[i]) for i in range(count)
    ]
    for copy in copies:
        copy.start()
    for copy in copies:
        copy.wait()


def stack_kernel(*refs):
    moved, out = refs[:-2], refs[-2:]
    capacity, both = moved[0].shape
    for s, ref in enumerate(moved[::-1]):
        for i in range(2):
            out[i][s * capacity : (s + 1) * capacity, :] = ref[
                :, i * (both // 2) : (i + 1) * (both // 2)
            ]


def join_kernel(columns, stay, *refs):
    _, _, column = place()
    parts, flat = refs[:-1], refs[-1]
    capacity = stay.shape[0]
    feat = parts[0].shape[1]
    flat[:capacity, :] = stay[...]
    for m in range(columns):
        cols = pl.ds(pl.multiple_of((column ^ m) * feat, feat), feat)
        flat[capacity:, cols] = parts[m][...]


def part_pieces(hidden, w2, which, columns, out):
    half = w2.shape[1] // 2
    piece = half // columns
    for j in range(columns):
        cols = pl.ds(pl.multiple_of(which * half + j * piece, piece), piece)
        out[j] = dot(hidden, w2[:, cols]).astype(jnp.bfloat16)


def forward_kernel(columns, count, *refs):
    _, core, _ = place()
    flats, refs = refs[:count], refs[count:]
    w1, w2, send, refs = refs[0], refs[1], refs[2], refs[3:]
    for i in range(count):
        pre = dot(flats[i][...], w1[...])
        if len(refs) > count:
            refs[count + i][...] = pre
        hidden = gelu_tanh(pre).astype(jnp.bfloat16)
        refs[i][...] = hidden
        part_pieces(hidden, w2, 1 - core, columns, send.at[i])


def keep_kernel(columns, hidden_own, hidden_other, w2, *refs):
    _, core, _ = place()
    if len(refs) > 2:
        pre_own, pre_other, flat_own, flat_other, keep_own, keep_other = refs[:6]
        flat_t, hidden_t, slope = refs[6:]
    else:
        keep_own, keep_other = refs
    part_pieces(hidden_own[...], w2, core, columns, keep_own)
    part_pieces(hidden_other[...], w2, core, columns, keep_other)
    if len(refs) > 2:
        half = flat_own.shape[0]
        slope[:half, :] = gelu_slope(pre_own[...])
        slope[half:, :] = gelu_slope(pre_other[...])
        hidden_t[...] = jnp.concatenate([hidden_own[...], hidden_other[...]], axis=0).T
        step = 512
        for j in range(0, flat_own.shape[1], step):
            here = slice(j, j + step)
            both = jnp.concatenate([flat_own[:, here], flat_other[:, here]], axis=0)
            flat_t[here, :] = both.T


def pair_kernel(columns, keep_own, keep_other, *refs):
    _, core, column = place()
    half = keep_own.shape[1]
    got, (mine, *out) = refs[:-columns], refs[-columns:]
    got_own, got_other = got[0].at[0], got[-1].at[len(got) % 2]
    for m in range(columns):
        for which, keep, got in ((core, keep_own, got_other), (1 - core, keep_other, got_own)):
            rows = pl.ds(pl.multiple_of(which * half, 16), half)
            both = keep[column ^ m].astype(jnp.float32) + got[column ^ m].astype(jnp.float32)
            if m:
                out[m - 1][rows, :] = both.astype(jnp.bfloat16)
            else:
                mine[rows, :] = both


def total_kernel(columns, experts, *refs):
    sums, out = refs[:columns], refs[columns:]
    total = sums[0][...]
    for ref in sums[1:]:
        total = total + ref[...].astype(jnp.float32)
    total = total.astype(jnp.bfloat16)
    capacity = out[0].shape[0] // 2
    for s in range(experts):
        for c in range(2):
            start = (c * experts + s) * capacity
            out[-1 - s][c * capacity : (c + 1) * capacity, :] = total[start : start + capacity]


def home_kernel(experts, capacity, maps, *refs):
    got, out = refs[:experts], refs[experts:]
    for c in range(2):
        here = slice(c * capacity, (c + 1) * capacity)
        rows = jnp.concatenate([ref[here, :] for ref in got[::-1]], axis=0)
        by_slot = dot(maps[c], rows).astype(jnp.bfloat16)
        for s in range(experts):
            out[-1 - s][here, :] = by_slot[s * capacity : (s + 1) * capacity]


def upstream_kernel(columns, experts, loss_scale, *refs):
    sums, teacher, out = refs[:columns], refs[columns:-1], refs[-1]
    total = sums[0][...]
    for ref in sums[1:]:
        total = total + ref[...].astype(jnp.float32)
    capacity = teacher[0].shape[0] // 2
    rows = jnp.concatenate(
        [
            teacher[-1 - s][c * capacity : (c + 1) * capacity, :]
            for c in range(2)
            for s in range(experts)
        ],
        axis=0,
    ).astype(jnp.float32)
    out[...] = ((total - rows) * loss_scale).astype(jnp.bfloat16)


def backward_kernel(columns, places, first, last, *refs):
    _, core, column = place()
    pieces, refs = refs[: len(places)], refs[len(places) :]
    hidden_t, w2, refs = refs[0], refs[1], refs[2:]
    if not first:
        sum_in, refs = refs[0], refs[2:]
    if last:
        flat_t, slope, grad_second, grad_first, held_first, held_second, sems = refs
    else:
        grad_second, sum_out, held_second, sems = refs
    piece = pieces[0].shape[1]
    width = w2.shape[1]
    hidden_grad = None if first else sum_in[...]
    copies = []

    def leave(source, target):
        copies.append(pltpu.make_async_copy(source, target, sems.at[len(copies)]))
        copies[-1].start()

    used = []
    for ref, (other, m) in zip(pieces, places):
        which = 1 - core if other else core
        start = which * (width // 2) + (column ^ m) * piece
        cols = pl.ds(pl.multiple_of(start, piece), piece)
        half = ref.shape[0] // 2
        rows = jnp.concatenate(
            [ref[pl.ds(pl.multiple_of(block * half, 16), half), :] for block in (core, 1 - core)],
            axis=0,
        )
        used.append((rows, cols))
        term = dot_nt(rows, w2[:, cols])
        hidden_grad = term if hidden_grad is None else hidden_grad + term
    if last:
        pre_grad = (hidden_grad * slope[...]).astype(jnp.bfloat16)
        step = 512
        for j in range(width // step):
            here = slice(j * step, (j + 1) * step)
            held_first[here, :] = dot(flat_t[here, :], pre_grad).astype(jnp.bfloat16)
            leave(held_first.at[here, :], grad_first.at[here, :])
    else:
        sum_out[...] = hidden_grad
    for i, (rows, cols) in enumerate(used):
        held_second[i] = dot(hidden_t[...], rows).astype(jnp.bfloat16)
        leave(held_second.at[i], grad_second.at[:, cols])
    for copy in copies:
        copy.wait()


def by_kernels(
    teacher_in,
    student_in,
    teacher_route,
    student_route,
    teacher_w1,
    teacher_w2,
    student_w1,
    student_w2,
):
    groups, columns, experts, row_count, width, capacity = sizes(teacher_in)
    plane_rows = groups * capacity
    loss_scale = 1.0 / math.sqrt(row_count)
    feat = width // columns
    piece = feat // 2
    hid = teacher_w1.shape[2]
    f32 = jnp.float32

    def after(value, *others):
        return lax.optimization_barrier((value, others))[0]

    def over_planes(sent):
        return [partner(value, "dp", (experts - 1 - i) << 1) for i, value in enumerate(sent)]

    def spread(mine):
        return [mine] + [partner(mine, "expert", m) for m in range(1, columns)]

    def across(value):
        return partner(value, "dp", 1)

    def load(*weights):
        return call(
            load_kernel,
            [shape(*w.shape) for w in weights],
            weights,
            in_specs=[ANY] * len(weights),
            name="load",
            scratch=[pltpu.SemaphoreType.DMA((len(weights),))],
        )

    def forward(flats, w1, w2, keep_pre, name, units=0):
        half, count = plane_rows // 2, len(flats)
        pre = [shape(half, hid, dtype=f32)] * count if keep_pre else []
        return call(
            lambda *refs: forward_kernel(columns, count, *refs),
            [shape(count, columns, half, piece)] + [shape(half, hid)] * count + pre,
            [*flats, w1, w2],
            flops=units * plane_rows * width * hid,
            name=name,
        )

    def keep(own, other, w2, state, outs):
        return call(
            lambda *refs: keep_kernel(columns, *refs),
            [shape(columns, plane_rows // 2, piece)] * 2 + outs,
            [own, other, w2, *state],
            flops=(64 if state else 8) * plane_rows * width * hid,
            name="keep_s" if state else "keep_t",
        )

    def pair(kept, got):
        return call(
            lambda *refs: pair_kernel(columns, *refs),
            [shape(plane_rows, piece, dtype=f32)] + [shape(plane_rows, piece)] * (columns - 1),
            [*kept, *got],
            name="pair",
        )

    def collect(mine, *out):
        return [mine] + [partner(value, "expert", m + 1) for m, value in enumerate(out)]

    route_t = teacher_route.reshape(1, row_count)
    route_s = student_route.reshape(1, row_count)
    def stay(values, route):
        return call(
            lambda *refs: stay_kernel(experts, capacity, *refs),
            [shape(capacity, width)],
            [values, route],
            name="stay",
        )[0]

    sent = call(
        lambda *refs: pack_kernel(experts, capacity, feat, *refs),
        [shape(capacity, 2 * feat)] * (experts - 1),
        [teacher_in, student_in, route_t, route_s],
        in_specs=[ANY] * 4,
        grant=(253 << 20) // 4,
        name="pack",
        scratch=[pltpu.VMEM((row_count, feat), jnp.bfloat16)] * 2
        + [pltpu.VMEM((1, row_count), jnp.int32)] * 2
        + [pltpu.SemaphoreType.DMA((4,))],
    )
    stay_t, stay_s = stay(teacher_in, route_t), stay(student_in, route_s)
    routes = jnp.concatenate([route_t, route_s], axis=0)
    other_routes = across(routes)
    w1_t, w2_t = load(teacher_w1[0], teacher_w2[0])
    moved = after(over_planes(sent), stay_t, stay_s, other_routes, w1_t)
    mine_t, mine_s = call(
        stack_kernel, [shape((experts - 1) * capacity, feat)] * 2, moved, name="stack"
    )
    got_t, got_s = spread(mine_t), spread(mine_s)
    w1_s, w2_s = load(student_w1[0], student_w2[0])
    (maps,) = call(
        lambda *refs: map_kernel(experts, capacity, *refs),
        [shape(2, experts * capacity, experts * capacity)],
        [routes, other_routes],
        name="maps",
    )

    def join(rows, got):
        return call(
            lambda *refs: join_kernel(columns, *refs),
            [shape(plane_rows // 2, width)],
            [rows, *got],
            name="join",
        )[0]

    flat_t_own = join(stay_t, after(got_t, maps))
    flat_t_other = across(flat_t_own)

    send, hidden_own = forward([flat_t_own], w1_t, w2_t, False, "forward_t", 24)
    got_own = across(send)
    send, hidden_other = forward([flat_t_other], w1_t, w2_t, False, "forward_t", 0)
    got_other = across(send)
    kept = keep(hidden_own, after(hidden_other, got_s, w1_s), w2_t, [], [])
    pieces_t = pair(kept, [got_own, got_other])
    sums_t = collect(*pieces_t)

    flat_own = join(stay_s, after(got_s, pieces_t[0]))
    flat_other = across(flat_own)
    send, hidden_own, hidden_other, pre_own, pre_other = forward(
        [flat_own, flat_other], w1_s, w2_s, True, "forward_s"
    )
    got = [across(send)]
    *kept, flat_t, hidden_t, slope = keep(
        hidden_own,
        hidden_other,
        w2_s,
        [pre_own, pre_other, flat_own, flat_other],
        [shape(width, plane_rows), shape(hid, plane_rows), shape(plane_rows, hid, dtype=f32)],
    )

    pieces_s = pair(kept, got)
    sums_s = collect(*pieces_s)

    home = call(
        lambda *refs: total_kernel(columns, experts, *refs),
        [shape(2 * capacity, piece)] * experts,
        after(sums_t, pieces_s[0]),
    )
    *sent, near, own = home
    home = [*over_planes([*sent, after(near, sums_s[1])]), own]
    slots = call(
        lambda *refs: home_kernel(experts, capacity, *refs),
        [shape(2 * capacity, piece)] * experts,
        [maps, *home],
        flops=0 * plane_rows * width * hid,
        name="home",
    )
    teachers = [*over_planes(slots[:-1]), slots[-1]]
    (upstream,) = call(
        lambda *refs: upstream_kernel(columns, experts, loss_scale, *refs),
        [shape(plane_rows, piece)],
        [*sums_s, *teachers],
    )
    def backward(pieces, state, last):
        first = state is None
        places = tuple(pieces)
        operands = [pieces[key] for key in places] + [hidden_t, w2_s]
        in_specs = [VMEM] * len(operands)
        aliases = {}
        if not first:
            operands += [state[1], state[0]]
            in_specs += [VMEM, ANY]
            aliases = {len(operands) - 1: 0}
        outs = [shape(hid, width)]
        scratch = [pltpu.VMEM((len(places), hid, piece), jnp.bfloat16)]
        copies = len(places)
        if last:
            operands += [flat_t, slope]
            in_specs += [VMEM, VMEM]
            outs += [shape(width, hid)]
            out_specs = [ANY, ANY]
            scratch = [pltpu.VMEM((width, hid), jnp.bfloat16)] + scratch
            copies += width // 512
        else:
            outs += [shape(plane_rows, hid, dtype=f32)]
            out_specs = [ANY, VMEM]
        return call(
            lambda *refs: backward_kernel(columns, places, first, last, *refs),
            outs,
            operands,
            out_specs=out_specs,
            in_specs=in_specs,
            scratch=scratch + [pltpu.SemaphoreType.DMA((copies,))],
            aliases=aliases,
        )

    grads = spread(upstream)
    state = backward({(0, 0): upstream, (1, 0): across(upstream)}, None, False)
    far = after(grads[3], state[1])
    state = backward({(0, 3): far}, state, False)
    near = after(grads[1:3], state[1])
    others = [across(value) for value in (*near, far)]
    state = backward({(0, m + 1): near[m] for m in range(2)}, state, False)
    grad_second, grad_first = backward(
        {(1, m + 1): value for m, value in enumerate(others)}, state, True
    )
    return (grad_first[None], grad_second[None])

def on_device(*arrays):
    _, columns, _, row_count, width, capacity = sizes(arrays[0])
    aligned = columns == 4 and capacity % 16 == 0 and row_count % 128 == 0 and width % (256 * columns) == 0
    return by_kernels(*arrays) if aligned else by_ops(*arrays)


def solution(mesh):
    return jax.shard_map(
        on_device,
        mesh=mesh,
        in_specs=(
            P("dp", None),
            P("dp", None),
            P("dp", None),
            P("dp", None),
            P("dp", None, "expert"),
            P("dp", "expert", None),
            P("dp", None, "expert"),
            P("dp", "expert", None),
        ),
        out_specs=(P("dp", None, "expert"), P("dp", "expert", None)),
        check_vma=False,
    )
```

```python
import math

import jax
import jax.numpy as jnp
from jax import lax
from jax.experimental import pallas as pl
from jax.experimental.pallas import tpu as pltpu
from jax.sharding import PartitionSpec as P

root_coef = math.sqrt(2.0 / math.pi)
cubic_coef = 0.044715


def partner(value, axis, mask):
    return lax.ppermute(value, axis, [(i, i ^ mask) for i in range(lax.axis_size(axis))])


def gelu_tanh(pre_act):
    inner_arg = root_coef * (pre_act + cubic_coef * pre_act * pre_act * pre_act)
    return 0.5 * pre_act * (1.0 + jnp.tanh(inner_arg))


def gelu_slope(pre_act):
    tangent = jnp.tanh(root_coef * (pre_act + cubic_coef * pre_act * pre_act * pre_act))
    return 0.5 * (1.0 + tangent) + 0.5 * pre_act * (1.0 - tangent * tangent) * root_coef * (
        1.0 + 3.0 * cubic_coef * pre_act * pre_act
    )


def dot(left, right):
    return jnp.dot(left, right, preferred_element_type=jnp.float32)


def ranks(routes, experts):
    onehot = (routes[..., None] == jnp.arange(experts, dtype=jnp.int32)).astype(jnp.int32)
    rank_table = jnp.cumsum(onehot, axis=1) - 1
    return jnp.sum(onehot * rank_table, axis=2)


def sizes(rows):
    groups = lax.axis_size("dp")
    experts = groups // 2
    row_count, width = rows.shape
    capacity = 2 * max(1, 3 * row_count // (4 * experts))
    return groups, lax.axis_size("expert"), experts, row_count, width, capacity


def by_ops(
    teacher_in,
    student_in,
    teacher_route,
    student_route,
    teacher_w1,
    teacher_w2,
    student_w1,
    student_w2,
):
    groups, columns, experts, row_count, width, capacity = sizes(teacher_in)
    plane_rows = groups * capacity
    dp = lax.axis_index("dp")
    column = lax.axis_index("expert")
    plane, core = dp // 2, dp % 2
    loss_scale = 1.0 / math.sqrt(row_count)
    feat = width // columns
    piece = feat // 2

    def dispatch(values, routes):
        position = ranks(routes[:, 0][None], experts)[0]
        slot = (routes[:, 0] ^ plane) * capacity + position
        placing = (
            jnp.arange(experts * capacity, dtype=jnp.int32)[:, None] == slot[None, :]
        ).astype(jnp.bfloat16)
        own_slice = lax.dynamic_slice(values, (0, column * feat), (row_count, feat))
        slots = dot(placing[capacity:], own_slice).astype(jnp.bfloat16)
        stay = dot(placing[:capacity], values).astype(jnp.bfloat16)
        moved = [
            partner(slots[(s - 1) * capacity : s * capacity], "dp", s << 1)
            for s in range(1, experts)
        ]
        mine = jnp.concatenate(moved, axis=0)
        buffer = jnp.concatenate([stay, jnp.zeros((mine.shape[0], width), jnp.bfloat16)], axis=0)
        for m in range(columns):
            got = partner(mine, "expert", m) if m else mine
            buffer = lax.dynamic_update_slice(buffer, got, (capacity, (column ^ m) * feat))
        other = partner(buffer, "dp", 1)
        first = jnp.where(core == 0, buffer, other)
        second = jnp.where(core == 0, other, buffer)
        return jnp.concatenate([first, second], axis=0)

    def forward(flat, w1, w2):
        pre = dot(flat, w1)
        hidden = gelu_tanh(pre).astype(jnp.bfloat16)
        part = dot(hidden, w2).astype(jnp.bfloat16).reshape(plane_rows, 2, columns, piece)
        part = part.transpose(1, 2, 0, 3)
        return pre, hidden, part

    def plane_sum(part):
        keep = lax.dynamic_index_in_dim(part, core, 0, keepdims=False)
        send = lax.dynamic_index_in_dim(part, 1 - core, 0, keepdims=False)
        pair = (
            keep.astype(jnp.float32) + partner(send, "dp", 1).astype(jnp.float32)
        ).astype(jnp.bfloat16)
        total = lax.dynamic_index_in_dim(pair, column, 0, keepdims=False).astype(jnp.float32)
        for m in range(1, columns):
            out = lax.dynamic_index_in_dim(pair, column ^ m, 0, keepdims=False)
            total = total + partner(out, "expert", m).astype(jnp.float32)
        return total

    routes = jnp.concatenate([teacher_route, student_route], axis=1)
    table = lax.all_gather(routes, "dp", axis=0, tiled=True).reshape(groups, row_count, 2)
    teacher_all, student_all = table[:, :, 0], table[:, :, 1]
    block = jnp.arange(groups, dtype=jnp.int32)[:, None]
    block_plane, block_core = block // 2, block % 2
    teacher_row = (
        (teacher_all ^ plane) * plane_rows
        + (block_core * experts + (block_plane ^ teacher_all)) * capacity
        + ranks(teacher_all, experts)
    )
    student_row = jnp.where(student_all == plane, ranks(student_all, experts), -1)
    hits = jnp.arange(capacity, dtype=jnp.int32)[None, :, None] == student_row[:, None, :]
    source = jnp.sum(jnp.where(hits, teacher_row[:, None, :] + 1, 0), axis=2) - 1
    source = source.reshape(experts, 2, capacity)
    source = source[jnp.arange(experts, dtype=jnp.int32) ^ plane].transpose(1, 0, 2)
    source = source.reshape(plane_rows)

    teacher_flat = dispatch(teacher_in, teacher_route)
    student_flat = dispatch(student_in, student_route)
    _, _, teacher_part = forward(teacher_flat, teacher_w1[0], teacher_w2[0])
    teacher_sum = plane_sum(teacher_part).astype(jnp.bfloat16)
    teacher_sums = jnp.concatenate(
        [teacher_sum] + [partner(teacher_sum, "dp", s << 1) for s in range(1, experts)], axis=0
    )
    student_pre, student_hidden, student_part = forward(
        student_flat, student_w1[0], student_w2[0]
    )
    pick = (
        source[:, None] == jnp.arange(experts * plane_rows, dtype=jnp.int32)[None, :]
    ).astype(jnp.bfloat16)
    teacher_rows = dot(pick, teacher_sums)
    student_sum = plane_sum(student_part)
    upstream = ((student_sum - teacher_rows) * loss_scale).astype(jnp.bfloat16)

    half = jnp.zeros((plane_rows, width // 2), jnp.bfloat16)
    for m in range(columns):
        got = partner(upstream, "expert", m) if m else upstream
        half = lax.dynamic_update_slice(half, got, (0, (column ^ m) * piece))
    other_half = partner(half, "dp", 1)
    grad_flat = jnp.concatenate(
        [jnp.where(core == 0, half, other_half), jnp.where(core == 0, other_half, half)], axis=1
    )
    hidden_grad = dot(grad_flat, student_w2[0].T)
    pre_grad = (hidden_grad * gelu_slope(student_pre)).astype(jnp.bfloat16)
    grad_second = dot(student_hidden.T, grad_flat).astype(jnp.bfloat16)
    grad_first = dot(student_flat.T, pre_grad).astype(jnp.bfloat16)
    return (grad_first[None], grad_second[None])


def plane_order(experts):
    return (*range(2, experts), 1, 0)


def place():
    dp = lax.axis_index("dp")
    return dp // 2, dp % 2, lax.axis_index("expert")


VMEM = pl.BlockSpec(memory_space=pltpu.VMEM)
ANY = pl.BlockSpec(memory_space=pl.ANY)


def call(kernel, outs, operands, out_specs=None, in_specs=None, scratch=(), aliases=None, grant=20 << 20, flops=0, name=None):
    return pl.pallas_call(
        kernel,
        name=name,
        out_shape=outs,
        in_specs=in_specs or [VMEM] * len(operands),
        out_specs=out_specs or [VMEM] * len(outs),
        scratch_shapes=list(scratch),
        input_output_aliases=aliases or {},
        compiler_params=pltpu.CompilerParams(vmem_limit_bytes=grant),
        cost_estimate=pl.CostEstimate(flops=flops, bytes_accessed=0, transcendentals=0),
    )(*operands)


def shape(*dims, dtype=jnp.bfloat16):
    return jax.ShapeDtypeStruct(dims, dtype)


def dot_tn(left, right):
    return lax.dot_general(
        left, right, (((0,), (0,)), ((), ())), preferred_element_type=jnp.float32
    )


def dot_nt(left, right):
    return lax.dot_general(
        left, right, (((1,), (1,)), ((), ())), preferred_element_type=jnp.float32
    )


def placing(route, experts, capacity, plane):
    rows = route.shape[1]
    known = lax.broadcasted_iota(jnp.int32, (16 * (-(-experts // 16)), rows), 0)
    onehot = jnp.where(known == route, 1.0, 0.0)
    upto = lax.broadcasted_iota(jnp.int32, (rows, rows), 0) <= lax.broadcasted_iota(
        jnp.int32, (rows, rows), 1
    )
    counts = dot(onehot.astype(jnp.bfloat16), jnp.where(upto, 1.0, 0.0).astype(jnp.bfloat16))
    position = jnp.sum(onehot * counts, axis=0, keepdims=True).astype(jnp.int32) - 1
    slot = (route ^ plane) * capacity + position
    slots = lax.broadcasted_iota(jnp.int32, (experts * capacity, rows), 0)
    return jnp.where(slots == slot, 1.0, 0.0).astype(jnp.bfloat16)


def pack_kernel(experts, capacity, feat, *refs):
    plane, _, column = place()
    values, routes, refs = refs[:2], refs[2:4], refs[4:]
    moved, refs = refs[: experts - 1], refs[experts - 1 :]
    slices, blocks, sems = refs[:2], refs[2:4], refs[4]
    cols = pl.ds(pl.multiple_of(column * feat, feat), feat)
    copies = [
        pltpu.make_async_copy(routes[0], blocks[0], sems.at[0]),
        pltpu.make_async_copy(routes[1], blocks[1], sems.at[1]),
        pltpu.make_async_copy(values[0].at[:, cols], slices[0], sems.at[2]),
        pltpu.make_async_copy(values[1].at[:, cols], slices[1], sems.at[3]),
    ]
    for copy in copies:
        copy.start()
    for i in range(2):
        copies[i].wait()
    places = [placing(block[...], experts, capacity, plane) for block in blocks]
    for i in range(2):
        copies[2 + i].wait()
    for i in range(2):
        sent = dot(places[i][capacity:], slices[i][...]).astype(jnp.bfloat16)
        for out, s in zip(moved, plane_order(experts)):
            out[:, i * feat : (i + 1) * feat] = sent[(s - 1) * capacity : s * capacity]


def stay_kernel(experts, capacity, values, route, stay):
    plane, _, _ = place()
    place_rows = placing(route[...], experts, capacity, plane)
    stay[...] = dot(place_rows[:capacity], values[...]).astype(jnp.bfloat16)


def map_kernel(experts, capacity, routes, other_routes, out):
    plane, core, _ = place()
    for c in range(2):
        block = jnp.where(core == c, routes[...], other_routes[...])
        source = placing(block[0:1], experts, capacity, plane)
        target = placing(block[1:2], experts, capacity, plane)
        out[c] = dot_nt(target, source).astype(jnp.bfloat16)


def load_kernel(*refs):
    count = len(refs) // 2
    copies = [
        pltpu.make_async_copy(refs[i], refs[count + i], refs[-1].at[i]) for i in range(count)
    ]
    for copy in copies:
        copy.start()
    for copy in copies:
        copy.wait()


def stack_kernel(*refs):
    moved, out = refs[:-2], refs[-2:]
    capacity, both = moved[0].shape
    for ref, s in zip(moved, plane_order(len(moved) + 1)):
        for i in range(2):
            out[i][(s - 1) * capacity : s * capacity, :] = ref[
                :, i * (both // 2) : (i + 1) * (both // 2)
            ]


def join_kernel(columns, stay, *refs):
    _, _, column = place()
    parts, flat = refs[:-1], refs[-1]
    capacity = stay.shape[0]
    feat = parts[0].shape[1]
    flat[:capacity, :] = stay[...]
    for m in range(columns):
        cols = pl.ds(pl.multiple_of((column ^ m) * feat, feat), feat)
        flat[capacity:, cols] = parts[m][...]


def part_pieces(hidden, w2, which, columns, out):
    half = w2.shape[1] // 2
    piece = half // columns
    for j in range(columns):
        cols = pl.ds(pl.multiple_of(which * half + j * piece, piece), piece)
        out[j] = dot(hidden, w2[:, cols]).astype(jnp.bfloat16)


def forward_kernel(columns, count, *refs):
    _, core, _ = place()
    flats, refs = refs[:count], refs[count:]
    w1, w2, send, refs = refs[0], refs[1], refs[2], refs[3:]
    for i in range(count):
        pre = dot(flats[i][...], w1[...])
        if len(refs) > count:
            refs[count + i][...] = pre
        hidden = gelu_tanh(pre).astype(jnp.bfloat16)
        refs[i][...] = hidden
        part_pieces(hidden, w2, 1 - core, columns, send.at[i])


def keep_kernel(columns, hidden_own, hidden_other, w2, *refs):
    _, core, _ = place()
    if len(refs) > 2:
        pre_own, pre_other, flat_own, flat_other, keep_own, keep_other = refs[:6]
        flat_t, hidden_t, slope = refs[6:]
    else:
        keep_own, keep_other = refs
    part_pieces(hidden_own[...], w2, core, columns, keep_own)
    part_pieces(hidden_other[...], w2, core, columns, keep_other)
    if len(refs) > 2:
        half = flat_own.shape[0]
        slope[:half, :] = gelu_slope(pre_own[...])
        slope[half:, :] = gelu_slope(pre_other[...])
        hidden_t[...] = jnp.concatenate([hidden_own[...], hidden_other[...]], axis=0).T
        step = 512
        for j in range(0, flat_own.shape[1], step):
            here = slice(j, j + step)
            both = jnp.concatenate([flat_own[:, here], flat_other[:, here]], axis=0)
            flat_t[here, :] = both.T


def pair_kernel(columns, keep_own, keep_other, *refs):
    _, core, column = place()
    half = keep_own.shape[1]
    got, (mine, *out) = refs[:-columns], refs[-columns:]
    got_own, got_other = got[0].at[0], got[-1].at[len(got) % 2]
    for m in range(columns):
        for which, keep, got in ((core, keep_own, got_other), (1 - core, keep_other, got_own)):
            rows = pl.ds(pl.multiple_of(which * half, 16), half)
            both = keep[column ^ m].astype(jnp.float32) + got[column ^ m].astype(jnp.float32)
            if m:
                out[m - 1][rows, :] = both.astype(jnp.bfloat16)
            else:
                mine[rows, :] = both


def total_kernel(columns, experts, *refs):
    sums, out = refs[:columns], refs[columns:]
    total = sums[0][...]
    for ref in sums[1:]:
        total = total + ref[...].astype(jnp.float32)
    total = total.astype(jnp.bfloat16)
    capacity = out[0].shape[0] // 2
    for ref, s in zip(out, plane_order(experts)):
        for c in range(2):
            start = (c * experts + s) * capacity
            ref[c * capacity : (c + 1) * capacity, :] = total[start : start + capacity]


def home_kernel(experts, capacity, maps, *refs):
    got, out = refs[:experts], refs[experts:]
    for c in range(2):
        here = slice(c * capacity, (c + 1) * capacity)
        by_plane = dict(zip(plane_order(experts), got))
        rows = jnp.concatenate([by_plane[s][here, :] for s in range(experts)], axis=0)
        by_slot = dot(maps[c], rows).astype(jnp.bfloat16)
        for ref, s in zip(out, plane_order(experts)):
            ref[here, :] = by_slot[s * capacity : (s + 1) * capacity]


def upstream_kernel(columns, experts, loss_scale, *refs):
    sums, teacher, out = refs[:columns], refs[columns:-1], refs[-1]
    total = sums[0][...]
    for ref in sums[1:]:
        total = total + ref[...].astype(jnp.float32)
    capacity = teacher[0].shape[0] // 2
    teacher = dict(zip(plane_order(experts), teacher))
    rows = jnp.concatenate(
        [
            teacher[s][c * capacity : (c + 1) * capacity, :]
            for c in range(2)
            for s in range(experts)
        ],
        axis=0,
    ).astype(jnp.float32)
    out[...] = ((total - rows) * loss_scale).astype(jnp.bfloat16)


def backward_kernel(columns, places, first, last, *refs):
    _, core, column = place()
    pieces, refs = refs[: len(places)], refs[len(places) :]
    hidden_t, w2, refs = refs[0], refs[1], refs[2:]
    if not first:
        sum_in, refs = refs[0], refs[2:]
    if last:
        flat_t, slope, grad_second, grad_first, held_first, held_second, sems = refs
    else:
        grad_second, sum_out, held_second, sems = refs
    piece = pieces[0].shape[1]
    width = w2.shape[1]
    hidden_grad = None if first else sum_in[...]
    copies = []

    def leave(source, target):
        copies.append(pltpu.make_async_copy(source, target, sems.at[len(copies)]))
        copies[-1].start()

    used = []
    for ref, (other, m) in zip(pieces, places):
        which = 1 - core if other else core
        start = which * (width // 2) + (column ^ m) * piece
        cols = pl.ds(pl.multiple_of(start, piece), piece)
        half = ref.shape[0] // 2
        rows = jnp.concatenate(
            [ref[pl.ds(pl.multiple_of(block * half, 16), half), :] for block in (core, 1 - core)],
            axis=0,
        )
        used.append((rows, cols))
        term = dot_nt(rows, w2[:, cols])
        hidden_grad = term if hidden_grad is None else hidden_grad + term
    if last:
        pre_grad = (hidden_grad * slope[...]).astype(jnp.bfloat16)
        step = 512
        for j in range(width // step):
            here = slice(j * step, (j + 1) * step)
            held_first[here, :] = dot(flat_t[here, :], pre_grad).astype(jnp.bfloat16)
            leave(held_first.at[here, :], grad_first.at[here, :])
    else:
        sum_out[...] = hidden_grad
    for i, (rows, cols) in enumerate(used):
        held_second[i] = dot(hidden_t[...], rows).astype(jnp.bfloat16)
        leave(held_second.at[i], grad_second.at[:, cols])
    for copy in copies:
        copy.wait()


def by_kernels(
    teacher_in,
    student_in,
    teacher_route,
    student_route,
    teacher_w1,
    teacher_w2,
    student_w1,
    student_w2,
):
    groups, columns, experts, row_count, width, capacity = sizes(teacher_in)
    plane_rows = groups * capacity
    loss_scale = 1.0 / math.sqrt(row_count)
    feat = width // columns
    piece = feat // 2
    hid = teacher_w1.shape[2]
    f32 = jnp.float32

    def after(value, *others):
        return lax.optimization_barrier((value, others))[0]

    def over_planes(sent):
        return [
            partner(value, "dp", s << 1) for value, s in zip(sent, plane_order(experts))
        ]

    def spread(mine):
        return [mine] + [partner(mine, "expert", m) for m in range(1, columns)]

    def across(value):
        return partner(value, "dp", 1)

    def load(*weights):
        return call(
            load_kernel,
            [shape(*w.shape) for w in weights],
            weights,
            in_specs=[ANY] * len(weights),
            name="load",
            scratch=[pltpu.SemaphoreType.DMA((len(weights),))],
        )

    def forward(flats, w1, w2, keep_pre, name, units=0):
        half, count = plane_rows // 2, len(flats)
        pre = [shape(half, hid, dtype=f32)] * count if keep_pre else []
        return call(
            lambda *refs: forward_kernel(columns, count, *refs),
            [shape(count, columns, half, piece)] + [shape(half, hid)] * count + pre,
            [*flats, w1, w2],
            flops=units * plane_rows * width * hid,
            name=name,
        )

    def keep(own, other, w2, state, outs):
        return call(
            lambda *refs: keep_kernel(columns, *refs),
            [shape(columns, plane_rows // 2, piece)] * 2 + outs,
            [own, other, w2, *state],
            flops=(64 if state else 8) * plane_rows * width * hid,
            name="keep_s" if state else "keep_t",
        )

    def pair(kept, got):
        return call(
            lambda *refs: pair_kernel(columns, *refs),
            [shape(plane_rows, piece, dtype=f32)] + [shape(plane_rows, piece)] * (columns - 1),
            [*kept, *got],
            name="pair",
        )

    def collect(mine, *out):
        return [mine] + [partner(value, "expert", m + 1) for m, value in enumerate(out)]

    route_t = teacher_route.reshape(1, row_count)
    route_s = student_route.reshape(1, row_count)
    def stay(values, route):
        return call(
            lambda *refs: stay_kernel(experts, capacity, *refs),
            [shape(capacity, width)],
            [values, route],
            name="stay",
        )[0]

    sent = call(
        lambda *refs: pack_kernel(experts, capacity, feat, *refs),
        [shape(capacity, 2 * feat)] * (experts - 1),
        [teacher_in, student_in, route_t, route_s],
        in_specs=[ANY] * 4,
        grant=(253 << 20) // 4,
        name="pack",
        scratch=[pltpu.VMEM((row_count, feat), jnp.bfloat16)] * 2
        + [pltpu.VMEM((1, row_count), jnp.int32)] * 2
        + [pltpu.SemaphoreType.DMA((4,))],
    )
    stay_t, stay_s = stay(teacher_in, route_t), stay(student_in, route_s)
    routes = jnp.concatenate([route_t, route_s], axis=0)
    other_routes = across(routes)
    w1_t, w2_t = load(teacher_w1[0], teacher_w2[0])
    moved = after(over_planes(sent), stay_t, stay_s, other_routes, w1_t)
    mine_t, mine_s = call(
        stack_kernel, [shape((experts - 1) * capacity, feat)] * 2, moved, name="stack"
    )
    got_t, got_s = spread(mine_t), spread(mine_s)
    w1_s, w2_s = load(student_w1[0], student_w2[0])
    (maps,) = call(
        lambda *refs: map_kernel(experts, capacity, *refs),
        [shape(2, experts * capacity, experts * capacity)],
        [routes, other_routes],
        name="maps",
    )

    def join(rows, got):
        return call(
            lambda *refs: join_kernel(columns, *refs),
            [shape(plane_rows // 2, width)],
            [rows, *got],
            name="join",
        )[0]

    flat_t_own = join(stay_t, after(got_t, maps))
    flat_t_other = across(flat_t_own)

    send, hidden_own = forward([flat_t_own], w1_t, w2_t, False, "forward_t", 24)
    got_own = across(send)
    send, hidden_other = forward([flat_t_other], w1_t, w2_t, False, "forward_t", 0)
    got_other = across(send)
    kept = keep(hidden_own, after(hidden_other, got_s, w1_s), w2_t, [], [])
    pieces_t = pair(kept, [got_own, got_other])
    sums_t = collect(*pieces_t)

    flat_own = join(stay_s, after(got_s, pieces_t[0]))
    flat_other = across(flat_own)
    send, hidden_own, hidden_other, pre_own, pre_other = forward(
        [flat_own, flat_other], w1_s, w2_s, True, "forward_s"
    )
    got = [across(send)]
    *kept, flat_t, hidden_t, slope = keep(
        hidden_own,
        hidden_other,
        w2_s,
        [pre_own, pre_other, flat_own, flat_other],
        [shape(width, plane_rows), shape(hid, plane_rows), shape(plane_rows, hid, dtype=f32)],
    )

    pieces_s = pair(kept, got)
    sums_s = collect(*pieces_s)

    home = call(
        lambda *refs: total_kernel(columns, experts, *refs),
        [shape(2 * capacity, piece)] * experts,
        after(sums_t, pieces_s[0]),
    )
    *sent, near, own = home
    home = [*over_planes([*sent, after(near, sums_s[1])]), own]
    slots = call(
        lambda *refs: home_kernel(experts, capacity, *refs),
        [shape(2 * capacity, piece)] * experts,
        [maps, *home],
        flops=0 * plane_rows * width * hid,
        name="home",
    )
    teachers = [*over_planes(slots[:-1]), slots[-1]]
    (upstream,) = call(
        lambda *refs: upstream_kernel(columns, experts, loss_scale, *refs),
        [shape(plane_rows, piece)],
        [*sums_s, *teachers],
    )
    def backward(pieces, state, last):
        first = state is None
        places = tuple(pieces)
        operands = [pieces[key] for key in places] + [hidden_t, w2_s]
        in_specs = [VMEM] * len(operands)
        aliases = {}
        if not first:
            operands += [state[1], state[0]]
            in_specs += [VMEM, ANY]
            aliases = {len(operands) - 1: 0}
        outs = [shape(hid, width)]
        scratch = [pltpu.VMEM((len(places), hid, piece), jnp.bfloat16)]
        copies = len(places)
        if last:
            operands += [flat_t, slope]
            in_specs += [VMEM, VMEM]
            outs += [shape(width, hid)]
            out_specs = [ANY, ANY]
            scratch = [pltpu.VMEM((width, hid), jnp.bfloat16)] + scratch
            copies += width // 512
        else:
            outs += [shape(plane_rows, hid, dtype=f32)]
            out_specs = [ANY, VMEM]
        return call(
            lambda *refs: backward_kernel(columns, places, first, last, *refs),
            outs,
            operands,
            out_specs=out_specs,
            in_specs=in_specs,
            scratch=scratch + [pltpu.SemaphoreType.DMA((copies,))],
            aliases=aliases,
        )

    grads = spread(upstream)
    state = backward({(0, 0): upstream, (1, 0): across(upstream)}, None, False)
    far = after(grads[3], state[1])
    state = backward({(0, 3): far}, state, False)
    near = after(grads[1:3], state[1])
    others = [across(value) for value in (*near, far)]
    state = backward({(0, m + 1): near[m] for m in range(2)}, state, False)
    grad_second, grad_first = backward(
        {(1, m + 1): value for m, value in enumerate(others)}, state, True
    )
    return (grad_first[None], grad_second[None])

def on_device(*arrays):
    _, columns, _, row_count, width, capacity = sizes(arrays[0])
    aligned = columns == 4 and capacity % 16 == 0 and row_count % 128 == 0 and width % (256 * columns) == 0
    return by_kernels(*arrays) if aligned else by_ops(*arrays)


def solution(mesh):
    return jax.shard_map(
        on_device,
        mesh=mesh,
        in_specs=(
            P("dp", None),
            P("dp", None),
            P("dp", None),
            P("dp", None),
            P("dp", None, "expert"),
            P("dp", "expert", None),
            P("dp", None, "expert"),
            P("dp", "expert", None),
        ),
        out_specs=(P("dp", None, "expert"), P("dp", "expert", None)),
        check_vma=False,
    )
```

```python
import math

import jax
import jax.numpy as jnp
from jax import lax
from jax.experimental import pallas as pl
from jax.experimental.pallas import tpu as pltpu
from jax.sharding import PartitionSpec as P

root_coef = math.sqrt(2.0 / math.pi)
cubic_coef = 0.044715


def partner(value, axis, mask):
    return lax.ppermute(value, axis, [(i, i ^ mask) for i in range(lax.axis_size(axis))])


def gelu_tanh(pre_act):
    inner_arg = root_coef * (pre_act + cubic_coef * pre_act * pre_act * pre_act)
    return 0.5 * pre_act * (1.0 + jnp.tanh(inner_arg))


def gelu_slope(pre_act):
    tangent = jnp.tanh(root_coef * (pre_act + cubic_coef * pre_act * pre_act * pre_act))
    return 0.5 * (1.0 + tangent) + 0.5 * pre_act * (1.0 - tangent * tangent) * root_coef * (
        1.0 + 3.0 * cubic_coef * pre_act * pre_act
    )


def dot(left, right):
    return jnp.dot(left, right, preferred_element_type=jnp.float32)


def ranks(routes, experts):
    onehot = (routes[..., None] == jnp.arange(experts, dtype=jnp.int32)).astype(jnp.int32)
    rank_table = jnp.cumsum(onehot, axis=1) - 1
    return jnp.sum(onehot * rank_table, axis=2)


def sizes(rows):
    groups = lax.axis_size("dp")
    experts = groups // 2
    row_count, width = rows.shape
    capacity = 2 * max(1, 3 * row_count // (4 * experts))
    return groups, lax.axis_size("expert"), experts, row_count, width, capacity


def by_ops(
    teacher_in,
    student_in,
    teacher_route,
    student_route,
    teacher_w1,
    teacher_w2,
    student_w1,
    student_w2,
):
    groups, columns, experts, row_count, width, capacity = sizes(teacher_in)
    plane_rows = groups * capacity
    dp = lax.axis_index("dp")
    column = lax.axis_index("expert")
    plane, core = dp // 2, dp % 2
    loss_scale = 1.0 / math.sqrt(row_count)
    feat = width // columns
    piece = feat // 2

    def dispatch(values, routes):
        position = ranks(routes[:, 0][None], experts)[0]
        slot = (routes[:, 0] ^ plane) * capacity + position
        placing = (
            jnp.arange(experts * capacity, dtype=jnp.int32)[:, None] == slot[None, :]
        ).astype(jnp.bfloat16)
        own_slice = lax.dynamic_slice(values, (0, column * feat), (row_count, feat))
        slots = dot(placing[capacity:], own_slice).astype(jnp.bfloat16)
        stay = dot(placing[:capacity], values).astype(jnp.bfloat16)
        moved = [
            partner(slots[(s - 1) * capacity : s * capacity], "dp", s << 1)
            for s in range(1, experts)
        ]
        mine = jnp.concatenate(moved, axis=0)
        buffer = jnp.concatenate([stay, jnp.zeros((mine.shape[0], width), jnp.bfloat16)], axis=0)
        for m in range(columns):
            got = partner(mine, "expert", m) if m else mine
            buffer = lax.dynamic_update_slice(buffer, got, (capacity, (column ^ m) * feat))
        other = partner(buffer, "dp", 1)
        first = jnp.where(core == 0, buffer, other)
        second = jnp.where(core == 0, other, buffer)
        return jnp.concatenate([first, second], axis=0)

    def forward(flat, w1, w2):
        pre = dot(flat, w1)
        hidden = gelu_tanh(pre).astype(jnp.bfloat16)
        part = dot(hidden, w2).astype(jnp.bfloat16).reshape(plane_rows, 2, columns, piece)
        part = part.transpose(1, 2, 0, 3)
        return pre, hidden, part

    def plane_sum(part):
        keep = lax.dynamic_index_in_dim(part, core, 0, keepdims=False)
        send = lax.dynamic_index_in_dim(part, 1 - core, 0, keepdims=False)
        pair = (
            keep.astype(jnp.float32) + partner(send, "dp", 1).astype(jnp.float32)
        ).astype(jnp.bfloat16)
        total = lax.dynamic_index_in_dim(pair, column, 0, keepdims=False).astype(jnp.float32)
        for m in range(1, columns):
            out = lax.dynamic_index_in_dim(pair, column ^ m, 0, keepdims=False)
            total = total + partner(out, "expert", m).astype(jnp.float32)
        return total

    routes = jnp.concatenate([teacher_route, student_route], axis=1)
    table = lax.all_gather(routes, "dp", axis=0, tiled=True).reshape(groups, row_count, 2)
    teacher_all, student_all = table[:, :, 0], table[:, :, 1]
    block = jnp.arange(groups, dtype=jnp.int32)[:, None]
    block_plane, block_core = block // 2, block % 2
    teacher_row = (
        (teacher_all ^ plane) * plane_rows
        + (block_core * experts + (block_plane ^ teacher_all)) * capacity
        + ranks(teacher_all, experts)
    )
    student_row = jnp.where(student_all == plane, ranks(student_all, experts), -1)
    hits = jnp.arange(capacity, dtype=jnp.int32)[None, :, None] == student_row[:, None, :]
    source = jnp.sum(jnp.where(hits, teacher_row[:, None, :] + 1, 0), axis=2) - 1
    source = source.reshape(experts, 2, capacity)
    source = source[jnp.arange(experts, dtype=jnp.int32) ^ plane].transpose(1, 0, 2)
    source = source.reshape(plane_rows)

    teacher_flat = dispatch(teacher_in, teacher_route)
    student_flat = dispatch(student_in, student_route)
    _, _, teacher_part = forward(teacher_flat, teacher_w1[0], teacher_w2[0])
    teacher_sum = plane_sum(teacher_part).astype(jnp.bfloat16)
    teacher_sums = jnp.concatenate(
        [teacher_sum] + [partner(teacher_sum, "dp", s << 1) for s in range(1, experts)], axis=0
    )
    student_pre, student_hidden, student_part = forward(
        student_flat, student_w1[0], student_w2[0]
    )
    pick = (
        source[:, None] == jnp.arange(experts * plane_rows, dtype=jnp.int32)[None, :]
    ).astype(jnp.bfloat16)
    teacher_rows = dot(pick, teacher_sums)
    student_sum = plane_sum(student_part)
    upstream = ((student_sum - teacher_rows) * loss_scale).astype(jnp.bfloat16)

    half = jnp.zeros((plane_rows, width // 2), jnp.bfloat16)
    for m in range(columns):
        got = partner(upstream, "expert", m) if m else upstream
        half = lax.dynamic_update_slice(half, got, (0, (column ^ m) * piece))
    other_half = partner(half, "dp", 1)
    grad_flat = jnp.concatenate(
        [jnp.where(core == 0, half, other_half), jnp.where(core == 0, other_half, half)], axis=1
    )
    hidden_grad = dot(grad_flat, student_w2[0].T)
    pre_grad = (hidden_grad * gelu_slope(student_pre)).astype(jnp.bfloat16)
    grad_second = dot(student_hidden.T, grad_flat).astype(jnp.bfloat16)
    grad_first = dot(student_flat.T, pre_grad).astype(jnp.bfloat16)
    return (grad_first[None], grad_second[None])


def plane_order(experts):
    return (*range(2, experts), 1, 0)


def place():
    dp = lax.axis_index("dp")
    return dp // 2, dp % 2, lax.axis_index("expert")


VMEM = pl.BlockSpec(memory_space=pltpu.VMEM)
ANY = pl.BlockSpec(memory_space=pl.ANY)


def call(kernel, outs, operands, out_specs=None, in_specs=None, scratch=(), grant=20 << 20, flops=0, name=None):
    return pl.pallas_call(
        kernel,
        name=name,
        out_shape=outs,
        in_specs=in_specs or [VMEM] * len(operands),
        out_specs=out_specs or [VMEM] * len(outs),
        scratch_shapes=list(scratch),
        compiler_params=pltpu.CompilerParams(vmem_limit_bytes=grant),
        cost_estimate=pl.CostEstimate(flops=flops, bytes_accessed=0, transcendentals=0),
    )(*operands)


def shape(*dims, dtype=jnp.bfloat16):
    return jax.ShapeDtypeStruct(dims, dtype)


def dot_tn(left, right):
    return lax.dot_general(
        left, right, (((0,), (0,)), ((), ())), preferred_element_type=jnp.float32
    )


def dot_nt(left, right):
    return lax.dot_general(
        left, right, (((1,), (1,)), ((), ())), preferred_element_type=jnp.float32
    )


def placing(route, experts, capacity, plane):
    rows = route.shape[1]
    known = lax.broadcasted_iota(jnp.int32, (16 * (-(-experts // 16)), rows), 0)
    onehot = jnp.where(known == route, 1.0, 0.0)
    upto = lax.broadcasted_iota(jnp.int32, (rows, rows), 0) <= lax.broadcasted_iota(
        jnp.int32, (rows, rows), 1
    )
    counts = dot(onehot.astype(jnp.bfloat16), jnp.where(upto, 1.0, 0.0).astype(jnp.bfloat16))
    position = jnp.sum(onehot * counts, axis=0, keepdims=True).astype(jnp.int32) - 1
    slot = (route ^ plane) * capacity + position
    slots = lax.broadcasted_iota(jnp.int32, (experts * capacity, rows), 0)
    return jnp.where(slots == slot, 1.0, 0.0).astype(jnp.bfloat16)


def pack_kernel(experts, capacity, feat, *refs):
    plane, _, column = place()
    values, routes, refs = refs[:2], refs[2:4], refs[4:]
    moved, refs = refs[: experts - 1], refs[experts - 1 :]
    slices, blocks, sems = refs[:2], refs[2:4], refs[4]
    cols = pl.ds(pl.multiple_of(column * feat, feat), feat)
    copies = [
        pltpu.make_async_copy(routes[0], blocks[0], sems.at[0]),
        pltpu.make_async_copy(routes[1], blocks[1], sems.at[1]),
        pltpu.make_async_copy(values[0].at[:, cols], slices[0], sems.at[2]),
        pltpu.make_async_copy(values[1].at[:, cols], slices[1], sems.at[3]),
    ]
    for copy in copies:
        copy.start()
    for i in range(2):
        copies[i].wait()
    places = [placing(block[...], experts, capacity, plane) for block in blocks]
    for i in range(2):
        copies[2 + i].wait()
    for i in range(2):
        sent = dot(places[i][capacity:], slices[i][...]).astype(jnp.bfloat16)
        for out, s in zip(moved, plane_order(experts)):
            out[:, i * feat : (i + 1) * feat] = sent[(s - 1) * capacity : s * capacity]


def stay_kernel(experts, capacity, values, route, stay):
    plane, _, _ = place()
    place_rows = placing(route[...], experts, capacity, plane)
    stay[...] = dot(place_rows[:capacity], values[...]).astype(jnp.bfloat16)


def map_kernel(experts, capacity, routes, other_routes, out):
    plane, core, _ = place()
    for c in range(2):
        block = jnp.where(core == c, routes[...], other_routes[...])
        source = placing(block[0:1], experts, capacity, plane)
        target = placing(block[1:2], experts, capacity, plane)
        out[c] = dot_nt(target, source).astype(jnp.bfloat16)


def load_kernel(*refs):
    count = len(refs) // 2
    copies = [
        pltpu.make_async_copy(refs[i], refs[count + i], refs[-1].at[i]) for i in range(count)
    ]
    for copy in copies:
        copy.start()
    for copy in copies:
        copy.wait()


def stack_kernel(*refs):
    moved, out = refs[:-2], refs[-2:]
    capacity, both = moved[0].shape
    for ref, s in zip(moved, plane_order(len(moved) + 1)):
        for i in range(2):
            out[i][(s - 1) * capacity : s * capacity, :] = ref[
                :, i * (both // 2) : (i + 1) * (both // 2)
            ]


def join_kernel(columns, stay, *refs):
    _, _, column = place()
    parts, flat = refs[:-1], refs[-1]
    capacity = stay.shape[0]
    feat = parts[0].shape[1]
    flat[:capacity, :] = stay[...]
    for m in range(columns):
        cols = pl.ds(pl.multiple_of((column ^ m) * feat, feat), feat)
        flat[capacity:, cols] = parts[m][...]


def part_pieces(hidden, w2, which, columns, out):
    half = w2.shape[1] // 2
    piece = half // columns
    for j in range(columns):
        cols = pl.ds(pl.multiple_of(which * half + j * piece, piece), piece)
        out[j] = dot(hidden, w2[:, cols]).astype(jnp.bfloat16)


def forward_kernel(columns, count, *refs):
    _, core, _ = place()
    flats, refs = refs[:count], refs[count:]
    w1, w2, send, refs = refs[0], refs[1], refs[2], refs[3:]
    for i in range(count):
        pre = dot(flats[i][...], w1[...])
        if len(refs) > count:
            refs[count + i][...] = pre
        hidden = gelu_tanh(pre).astype(jnp.bfloat16)
        refs[i][...] = hidden
        part_pieces(hidden, w2, 1 - core, columns, send.at[i])


def keep_kernel(columns, hidden_own, hidden_other, w2, *refs):
    _, core, _ = place()
    if len(refs) > 2:
        pre_own, pre_other, flat_own, flat_other, keep_own, keep_other = refs[:6]
        flat_t, hidden_t, slope = refs[6:]
    else:
        keep_own, keep_other = refs
    part_pieces(hidden_own[...], w2, core, columns, keep_own)
    part_pieces(hidden_other[...], w2, core, columns, keep_other)
    if len(refs) > 2:
        half = flat_own.shape[0]
        slope[:half, :] = gelu_slope(pre_own[...])
        slope[half:, :] = gelu_slope(pre_other[...])
        hidden_t[...] = jnp.concatenate([hidden_own[...], hidden_other[...]], axis=0).T
        step = 512
        for j in range(0, flat_own.shape[1], step):
            here = slice(j, j + step)
            both = jnp.concatenate([flat_own[:, here], flat_other[:, here]], axis=0)
            flat_t[here, :] = both.T


def pair_kernel(columns, keep_own, keep_other, *refs):
    _, core, column = place()
    half = keep_own.shape[1]
    got, (mine, *out) = refs[:-columns], refs[-columns:]
    got_own, got_other = got[0].at[0], got[-1].at[len(got) % 2]
    for m in range(columns):
        for which, keep, got in ((core, keep_own, got_other), (1 - core, keep_other, got_own)):
            rows = pl.ds(pl.multiple_of(which * half, 16), half)
            both = keep[column ^ m].astype(jnp.float32) + got[column ^ m].astype(jnp.float32)
            if m:
                out[m - 1][rows, :] = both.astype(jnp.bfloat16)
            else:
                mine[rows, :] = both


def total_kernel(columns, experts, *refs):
    sums, out = refs[:columns], refs[columns:]
    total = sums[0][...]
    for ref in sums[1:]:
        total = total + ref[...].astype(jnp.float32)
    total = total.astype(jnp.bfloat16)
    capacity = out[0].shape[0] // 2
    for ref, s in zip(out, plane_order(experts)):
        for c in range(2):
            start = (c * experts + s) * capacity
            ref[c * capacity : (c + 1) * capacity, :] = total[start : start + capacity]


def home_kernel(experts, capacity, maps, *refs):
    got, out = refs[:experts], refs[experts:]
    for c in range(2):
        here = slice(c * capacity, (c + 1) * capacity)
        by_plane = dict(zip(plane_order(experts), got))
        rows = jnp.concatenate([by_plane[s][here, :] for s in range(experts)], axis=0)
        by_slot = dot(maps[c], rows).astype(jnp.bfloat16)
        for ref, s in zip(out, plane_order(experts)):
            ref[here, :] = by_slot[s * capacity : (s + 1) * capacity]


def upstream_kernel(columns, experts, loss_scale, *refs):
    sums, teacher, out = refs[:columns], refs[columns:-1], refs[-1]
    total = sums[0][...]
    for ref in sums[1:]:
        total = total + ref[...].astype(jnp.float32)
    capacity = teacher[0].shape[0] // 2
    teacher = dict(zip(plane_order(experts), teacher))
    rows = jnp.concatenate(
        [
            teacher[s][c * capacity : (c + 1) * capacity, :]
            for c in range(2)
            for s in range(experts)
        ],
        axis=0,
    ).astype(jnp.float32)
    out[...] = ((total - rows) * loss_scale).astype(jnp.bfloat16)


def piece_columns(which, width, piece):
    _, core, column = place()
    other, m = which
    start = (1 - core if other else core) * (width // 2) + (column ^ m) * piece
    return pl.ds(pl.multiple_of(start, piece), piece)


def use_piece(ref, cols, hidden_t, w2, hidden_grad):
    _, core, _ = place()
    half = ref.shape[0] // 2
    rows = jnp.concatenate(
        [ref[pl.ds(pl.multiple_of(block * half, 16), half), :] for block in (core, 1 - core)],
        axis=0,
    )
    term = dot_nt(rows, w2[:, cols])
    hidden_grad = term if hidden_grad is None else hidden_grad + term
    return hidden_grad, rows


def early_kernel(places, first, *refs):
    count = len(places)
    pieces, (hidden_t, w2), refs = refs[:count], refs[count : count + 2], refs[count + 2 :]
    hidden_grad = None if first else refs[0][...]
    sum_out, *grads = refs if first else refs[1:]
    piece, width = pieces[0].shape[1], w2.shape[1]
    for ref, which, out in zip(pieces, places, grads):
        cols = piece_columns(which, width, piece)
        hidden_grad, rows = use_piece(ref, cols, hidden_t, w2, hidden_grad)
        out[...] = dot(hidden_t[...], rows).astype(jnp.bfloat16)
    sum_out[...] = hidden_grad


def last_kernel(places, early, *refs):
    count = len(places)
    pieces, refs = refs[:count], refs[count:]
    done, refs = refs[: len(early)], refs[len(early) :]
    hidden_t, w2, sum_in, flat_t, slope, grad_first, grad_second, held_first, held_second, sems = refs
    piece, width = pieces[0].shape[1], w2.shape[1]
    copies = []

    def leave(source, target):
        copies.append(pltpu.make_async_copy(source, target, sems.at[len(copies)]))
        copies[-1].start()

    for ref, which in zip(done, early):
        leave(ref, grad_second.at[:, piece_columns(which, width, piece)])
    hidden_grad = sum_in[...]
    used = []
    for ref, which in zip(pieces, places):
        cols = piece_columns(which, width, piece)
        hidden_grad, rows = use_piece(ref, cols, hidden_t, w2, hidden_grad)
        used.append((cols, rows))
    pre_grad = (hidden_grad * slope[...]).astype(jnp.bfloat16)
    step = 512
    for j in range(width // step):
        here = slice(j * step, (j + 1) * step)
        held_first[here, :] = dot(flat_t[here, :], pre_grad).astype(jnp.bfloat16)
        leave(held_first.at[here, :], grad_first.at[here, :])
    for i, (cols, rows) in enumerate(used):
        held_second[i] = dot(hidden_t[...], rows).astype(jnp.bfloat16)
        leave(held_second.at[i], grad_second.at[:, cols])
    for copy in copies:
        copy.wait()


def by_kernels(
    teacher_in,
    student_in,
    teacher_route,
    student_route,
    teacher_w1,
    teacher_w2,
    student_w1,
    student_w2,
):
    groups, columns, experts, row_count, width, capacity = sizes(teacher_in)
    plane_rows = groups * capacity
    loss_scale = 1.0 / math.sqrt(row_count)
    feat = width // columns
    piece = feat // 2
    hid = teacher_w1.shape[2]
    f32 = jnp.float32

    def after(value, *others):
        return lax.optimization_barrier((value, others))[0]

    def over_planes(sent):
        return [
            partner(value, "dp", s << 1) for value, s in zip(sent, plane_order(experts))
        ]

    def spread(mine):
        return [mine] + [partner(mine, "expert", m) for m in range(1, columns)]

    def across(value):
        return partner(value, "dp", 1)

    def load(*weights):
        return call(
            load_kernel,
            [shape(*w.shape) for w in weights],
            weights,
            in_specs=[ANY] * len(weights),
            name="load",
            scratch=[pltpu.SemaphoreType.DMA((len(weights),))],
        )

    def forward(flats, w1, w2, keep_pre, name, units=0):
        half, count = plane_rows // 2, len(flats)
        pre = [shape(half, hid, dtype=f32)] * count if keep_pre else []
        return call(
            lambda *refs: forward_kernel(columns, count, *refs),
            [shape(count, columns, half, piece)] + [shape(half, hid)] * count + pre,
            [*flats, w1, w2],
            flops=units * plane_rows * width * hid,
            name=name,
        )

    def keep(own, other, w2, state, outs):
        return call(
            lambda *refs: keep_kernel(columns, *refs),
            [shape(columns, plane_rows // 2, piece)] * 2 + outs,
            [own, other, w2, *state],
            flops=(64 if state else 8) * plane_rows * width * hid,
            name="keep_s" if state else "keep_t",
        )

    def pair(kept, got):
        return call(
            lambda *refs: pair_kernel(columns, *refs),
            [shape(plane_rows, piece, dtype=f32)] + [shape(plane_rows, piece)] * (columns - 1),
            [*kept, *got],
            name="pair",
        )

    def collect(mine, *out):
        return [mine] + [partner(value, "expert", m + 1) for m, value in enumerate(out)]

    route_t = teacher_route.reshape(1, row_count)
    route_s = student_route.reshape(1, row_count)
    def stay(values, route):
        return call(
            lambda *refs: stay_kernel(experts, capacity, *refs),
            [shape(capacity, width)],
            [values, route],
            name="stay",
        )[0]

    sent = call(
        lambda *refs: pack_kernel(experts, capacity, feat, *refs),
        [shape(capacity, 2 * feat)] * (experts - 1),
        [teacher_in, student_in, route_t, route_s],
        in_specs=[ANY] * 4,
        grant=(253 << 20) // 4,
        name="pack",
        scratch=[pltpu.VMEM((row_count, feat), jnp.bfloat16)] * 2
        + [pltpu.VMEM((1, row_count), jnp.int32)] * 2
        + [pltpu.SemaphoreType.DMA((4,))],
    )
    stay_t, stay_s = stay(teacher_in, route_t), stay(student_in, route_s)
    routes = jnp.concatenate([route_t, route_s], axis=0)
    other_routes = across(routes)
    w1_t, w2_t = load(teacher_w1[0], teacher_w2[0])
    moved = after(over_planes(sent), stay_t, other_routes, w1_t)
    mine_t, mine_s = call(
        stack_kernel, [shape((experts - 1) * capacity, feat)] * 2, moved, name="stack"
    )
    got_t, got_s = spread(mine_t), spread(mine_s)
    w1_s, w2_s = load(student_w1[0], student_w2[0])
    (maps,) = call(
        lambda *refs: map_kernel(experts, capacity, *refs),
        [shape(2, experts * capacity, experts * capacity)],
        [routes, other_routes],
        name="maps",
    )

    def join(rows, got):
        return call(
            lambda *refs: join_kernel(columns, *refs),
            [shape(plane_rows // 2, width)],
            [rows, *got],
            name="join",
        )[0]

    flat_t_own = join(stay_t, after(got_t, maps))
    flat_t_other = across(flat_t_own)

    send, hidden_own = forward([flat_t_own], w1_t, w2_t, False, "forward_t", 24)
    got_own = across(send)
    send, hidden_other = forward([flat_t_other], w1_t, w2_t, False, "forward_t", 0)
    got_other = across(send)
    kept = keep(hidden_own, after(hidden_other, got_s, w1_s, stay_s), w2_t, [], [])
    pieces_t = pair(kept, [got_own, got_other])
    sums_t = collect(*pieces_t)

    flat_own = join(stay_s, after(got_s, pieces_t[0]))
    flat_other = across(flat_own)
    send, hidden_own, hidden_other, pre_own, pre_other = forward(
        [flat_own, flat_other], w1_s, w2_s, True, "forward_s"
    )
    got = [across(send)]
    *kept, flat_t, hidden_t, slope = keep(
        hidden_own,
        hidden_other,
        w2_s,
        [pre_own, pre_other, flat_own, flat_other],
        [shape(width, plane_rows), shape(hid, plane_rows), shape(plane_rows, hid, dtype=f32)],
    )

    pieces_s = pair(kept, got)
    sums_s = collect(*pieces_s)

    home = call(
        lambda *refs: total_kernel(columns, experts, *refs),
        [shape(2 * capacity, piece)] * experts,
        after(sums_t, pieces_s[0]),
    )
    *sent, near, own = home
    home = [*over_planes([*sent, after(near, sums_s[1])]), own]
    slots = call(
        lambda *refs: home_kernel(experts, capacity, *refs),
        [shape(2 * capacity, piece)] * experts,
        [maps, *home],
        flops=4 * plane_rows * width * hid,
        name="home",
    )
    teachers = [*over_planes(slots[:-1]), slots[-1]]
    (upstream,) = call(
        lambda *refs: upstream_kernel(columns, experts, loss_scale, *refs),
        [shape(plane_rows, piece)],
        [*sums_s, *teachers],
    )
    early = {}

    def backward(pieces, total):
        first = total is None
        places = tuple(pieces)
        total, *done = call(
            lambda *refs: early_kernel(places, first, *refs),
            [shape(plane_rows, hid, dtype=f32)] + [shape(hid, piece)] * len(places),
            [*pieces.values(), hidden_t, w2_s] + ([] if first else [total]),
            name="early",
        )
        early.update(zip(places, done))
        return total

    def finish(pieces, total):
        places, kept_places = tuple(pieces), tuple(early)
        return call(
            lambda *refs: last_kernel(places, kept_places, *refs),
            [shape(width, hid), shape(hid, width)],
            [*pieces.values(), *early.values(), hidden_t, w2_s, total, flat_t, slope],
            out_specs=[ANY, ANY],
            scratch=[
                pltpu.VMEM((width, hid), jnp.bfloat16),
                pltpu.VMEM((len(places), hid, piece), jnp.bfloat16),
                pltpu.SemaphoreType.DMA((len(places) + len(early) + width // 512,)),
            ],
            name="last",
        )

    grads = spread(upstream)
    total = backward({(0, 0): upstream, (1, 0): across(upstream)}, None)
    far = after(grads[3], total)
    total = backward({(0, 3): far}, total)
    near = after(grads[1:3], total)
    other_far = across(far)
    others = [across(value) for value in near]
    total = backward({(0, 1): near[0], (0, 2): near[1], (1, 3): other_far}, total)
    grad_first, grad_second = finish({(1, 1): others[0], (1, 2): others[1]}, total)
    return (grad_first[None], grad_second[None])

def on_device(*arrays):
    _, columns, _, row_count, width, capacity = sizes(arrays[0])
    aligned = columns == 4 and capacity % 16 == 0 and row_count % 128 == 0 and width % (256 * columns) == 0
    return by_kernels(*arrays) if aligned else by_ops(*arrays)


def solution(mesh):
    return jax.shard_map(
        on_device,
        mesh=mesh,
        in_specs=(
            P("dp", None),
            P("dp", None),
            P("dp", None),
            P("dp", None),
            P("dp", None, "expert"),
            P("dp", "expert", None),
            P("dp", None, "expert"),
            P("dp", "expert", None),
        ),
        out_specs=(P("dp", None, "expert"), P("dp", "expert", None)),
        check_vma=False,
    )
```

```python
import math

import jax
import jax.numpy as jnp
from jax import lax
from jax.experimental import pallas as pl
from jax.experimental.pallas import tpu as pltpu
from jax.sharding import PartitionSpec as P

root_coef = math.sqrt(2.0 / math.pi)
cubic_coef = 0.044715


def partner(value, axis, mask):
    return lax.ppermute(value, axis, [(i, i ^ mask) for i in range(lax.axis_size(axis))])


def gelu_tanh(pre_act):
    inner_arg = root_coef * (pre_act + cubic_coef * pre_act * pre_act * pre_act)
    return 0.5 * pre_act * (1.0 + jnp.tanh(inner_arg))


def gelu_slope(pre_act):
    tangent = jnp.tanh(root_coef * (pre_act + cubic_coef * pre_act * pre_act * pre_act))
    return 0.5 * (1.0 + tangent) + 0.5 * pre_act * (1.0 - tangent * tangent) * root_coef * (
        1.0 + 3.0 * cubic_coef * pre_act * pre_act
    )


def dot(left, right):
    return jnp.dot(left, right, preferred_element_type=jnp.float32)


def ranks(routes, experts):
    onehot = (routes[..., None] == jnp.arange(experts, dtype=jnp.int32)).astype(jnp.int32)
    rank_table = jnp.cumsum(onehot, axis=1) - 1
    return jnp.sum(onehot * rank_table, axis=2)


def sizes(rows):
    groups = lax.axis_size("dp")
    experts = groups // 2
    row_count, width = rows.shape
    capacity = 2 * max(1, 3 * row_count // (4 * experts))
    return groups, lax.axis_size("expert"), experts, row_count, width, capacity


def by_ops(
    teacher_in,
    student_in,
    teacher_route,
    student_route,
    teacher_w1,
    teacher_w2,
    student_w1,
    student_w2,
):
    groups, columns, experts, row_count, width, capacity = sizes(teacher_in)
    plane_rows = groups * capacity
    dp = lax.axis_index("dp")
    column = lax.axis_index("expert")
    plane, core = dp // 2, dp % 2
    loss_scale = 1.0 / math.sqrt(row_count)
    feat = width // columns
    piece = feat // 2

    def dispatch(values, routes):
        position = ranks(routes[:, 0][None], experts)[0]
        slot = (routes[:, 0] ^ plane) * capacity + position
        placing = (
            jnp.arange(experts * capacity, dtype=jnp.int32)[:, None] == slot[None, :]
        ).astype(jnp.bfloat16)
        own_slice = lax.dynamic_slice(values, (0, column * feat), (row_count, feat))
        slots = dot(placing[capacity:], own_slice).astype(jnp.bfloat16)
        stay = dot(placing[:capacity], values).astype(jnp.bfloat16)
        moved = [
            partner(slots[(s - 1) * capacity : s * capacity], "dp", s << 1)
            for s in range(1, experts)
        ]
        mine = jnp.concatenate(moved, axis=0)
        buffer = jnp.concatenate([stay, jnp.zeros((mine.shape[0], width), jnp.bfloat16)], axis=0)
        for m in range(columns):
            got = partner(mine, "expert", m) if m else mine
            buffer = lax.dynamic_update_slice(buffer, got, (capacity, (column ^ m) * feat))
        other = partner(buffer, "dp", 1)
        first = jnp.where(core == 0, buffer, other)
        second = jnp.where(core == 0, other, buffer)
        return jnp.concatenate([first, second], axis=0)

    def forward(flat, w1, w2):
        pre = dot(flat, w1)
        hidden = gelu_tanh(pre).astype(jnp.bfloat16)
        part = dot(hidden, w2).astype(jnp.bfloat16).reshape(plane_rows, 2, columns, piece)
        part = part.transpose(1, 2, 0, 3)
        return pre, hidden, part

    def plane_sum(part):
        keep = lax.dynamic_index_in_dim(part, core, 0, keepdims=False)
        send = lax.dynamic_index_in_dim(part, 1 - core, 0, keepdims=False)
        pair = (
            keep.astype(jnp.float32) + partner(send, "dp", 1).astype(jnp.float32)
        ).astype(jnp.bfloat16)
        total = lax.dynamic_index_in_dim(pair, column, 0, keepdims=False).astype(jnp.float32)
        for m in range(1, columns):
            out = lax.dynamic_index_in_dim(pair, column ^ m, 0, keepdims=False)
            total = total + partner(out, "expert", m).astype(jnp.float32)
        return total

    routes = jnp.concatenate([teacher_route, student_route], axis=1)
    table = lax.all_gather(routes, "dp", axis=0, tiled=True).reshape(groups, row_count, 2)
    teacher_all, student_all = table[:, :, 0], table[:, :, 1]
    block = jnp.arange(groups, dtype=jnp.int32)[:, None]
    block_plane, block_core = block // 2, block % 2
    teacher_row = (
        (teacher_all ^ plane) * plane_rows
        + (block_core * experts + (block_plane ^ teacher_all)) * capacity
        + ranks(teacher_all, experts)
    )
    student_row = jnp.where(student_all == plane, ranks(student_all, experts), -1)
    hits = jnp.arange(capacity, dtype=jnp.int32)[None, :, None] == student_row[:, None, :]
    source = jnp.sum(jnp.where(hits, teacher_row[:, None, :] + 1, 0), axis=2) - 1
    source = source.reshape(experts, 2, capacity)
    source = source[jnp.arange(experts, dtype=jnp.int32) ^ plane].transpose(1, 0, 2)
    source = source.reshape(plane_rows)

    teacher_flat = dispatch(teacher_in, teacher_route)
    student_flat = dispatch(student_in, student_route)
    _, _, teacher_part = forward(teacher_flat, teacher_w1[0], teacher_w2[0])
    teacher_sum = plane_sum(teacher_part).astype(jnp.bfloat16)
    teacher_sums = jnp.concatenate(
        [teacher_sum] + [partner(teacher_sum, "dp", s << 1) for s in range(1, experts)], axis=0
    )
    student_pre, student_hidden, student_part = forward(
        student_flat, student_w1[0], student_w2[0]
    )
    pick = (
        source[:, None] == jnp.arange(experts * plane_rows, dtype=jnp.int32)[None, :]
    ).astype(jnp.bfloat16)
    teacher_rows = dot(pick, teacher_sums)
    student_sum = plane_sum(student_part)
    upstream = ((student_sum - teacher_rows) * loss_scale).astype(jnp.bfloat16)

    half = jnp.zeros((plane_rows, width // 2), jnp.bfloat16)
    for m in range(columns):
        got = partner(upstream, "expert", m) if m else upstream
        half = lax.dynamic_update_slice(half, got, (0, (column ^ m) * piece))
    other_half = partner(half, "dp", 1)
    grad_flat = jnp.concatenate(
        [jnp.where(core == 0, half, other_half), jnp.where(core == 0, other_half, half)], axis=1
    )
    hidden_grad = dot(grad_flat, student_w2[0].T)
    pre_grad = (hidden_grad * gelu_slope(student_pre)).astype(jnp.bfloat16)
    grad_second = dot(student_hidden.T, grad_flat).astype(jnp.bfloat16)
    grad_first = dot(student_flat.T, pre_grad).astype(jnp.bfloat16)
    return (grad_first[None], grad_second[None])


def plane_order(experts):
    return (*range(2, experts), 1, 0)


def place():
    dp = lax.axis_index("dp")
    return dp // 2, dp % 2, lax.axis_index("expert")


VMEM = pl.BlockSpec(memory_space=pltpu.VMEM)
ANY = pl.BlockSpec(memory_space=pl.ANY)


def call(kernel, outs, operands, out_specs=None, in_specs=None, scratch=(), grant=20 << 20, flops=0, name=None):
    return pl.pallas_call(
        kernel,
        name=name,
        out_shape=outs,
        in_specs=in_specs or [VMEM] * len(operands),
        out_specs=out_specs or [VMEM] * len(outs),
        scratch_shapes=list(scratch),
        compiler_params=pltpu.CompilerParams(vmem_limit_bytes=grant),
        cost_estimate=pl.CostEstimate(flops=flops, bytes_accessed=0, transcendentals=0),
    )(*operands)


def shape(*dims, dtype=jnp.bfloat16):
    return jax.ShapeDtypeStruct(dims, dtype)


def dot_tn(left, right):
    return lax.dot_general(
        left, right, (((0,), (0,)), ((), ())), preferred_element_type=jnp.float32
    )


def dot_nt(left, right):
    return lax.dot_general(
        left, right, (((1,), (1,)), ((), ())), preferred_element_type=jnp.float32
    )


def placing(route, experts, capacity, plane):
    rows = route.shape[1]
    known = lax.broadcasted_iota(jnp.int32, (16 * (-(-experts // 16)), rows), 0)
    onehot = jnp.where(known == route, 1.0, 0.0)
    upto = lax.broadcasted_iota(jnp.int32, (rows, rows), 0) <= lax.broadcasted_iota(
        jnp.int32, (rows, rows), 1
    )
    counts = dot(onehot.astype(jnp.bfloat16), jnp.where(upto, 1.0, 0.0).astype(jnp.bfloat16))
    position = jnp.sum(onehot * counts, axis=0, keepdims=True).astype(jnp.int32) - 1
    slot = (route ^ plane) * capacity + position
    slots = lax.broadcasted_iota(jnp.int32, (experts * capacity, rows), 0)
    return jnp.where(slots == slot, 1.0, 0.0).astype(jnp.bfloat16)


def pack_kernel(experts, capacity, feat, *refs):
    plane, _, column = place()
    values, routes, refs = refs[:2], refs[2:4], refs[4:]
    moved, refs = refs[: experts - 1], refs[experts - 1 :]
    slices, blocks, sems = refs[:2], refs[2:4], refs[4]
    cols = pl.ds(pl.multiple_of(column * feat, feat), feat)
    copies = [
        pltpu.make_async_copy(routes[0], blocks[0], sems.at[0]),
        pltpu.make_async_copy(routes[1], blocks[1], sems.at[1]),
        pltpu.make_async_copy(values[0].at[:, cols], slices[0], sems.at[2]),
        pltpu.make_async_copy(values[1].at[:, cols], slices[1], sems.at[3]),
    ]
    for copy in copies:
        copy.start()
    for i in range(2):
        copies[i].wait()
    places = [placing(block[...], experts, capacity, plane) for block in blocks]
    for i in range(2):
        copies[2 + i].wait()
    for i in range(2):
        sent = dot(places[i][capacity:], slices[i][...]).astype(jnp.bfloat16)
        for out, s in zip(moved, plane_order(experts)):
            out[:, i * feat : (i + 1) * feat] = sent[(s - 1) * capacity : s * capacity]


def stay_kernel(experts, capacity, values, route, stay):
    plane, _, _ = place()
    place_rows = placing(route[...], experts, capacity, plane)
    stay[...] = dot(place_rows[:capacity], values[...]).astype(jnp.bfloat16)


def map_kernel(experts, capacity, routes, other_routes, out):
    plane, core, _ = place()
    for c in range(2):
        block = jnp.where(core == c, routes[...], other_routes[...])
        source = placing(block[0:1], experts, capacity, plane)
        target = placing(block[1:2], experts, capacity, plane)
        out[c] = dot_nt(target, source).astype(jnp.bfloat16)


def load_kernel(*refs):
    count = len(refs) // 2
    copies = [
        pltpu.make_async_copy(refs[i], refs[count + i], refs[-1].at[i]) for i in range(count)
    ]
    for copy in copies:
        copy.start()
    for copy in copies:
        copy.wait()


def stack_kernel(*refs):
    moved, out = refs[:-2], refs[-2:]
    capacity, both = moved[0].shape
    for ref, s in zip(moved, plane_order(len(moved) + 1)):
        for i in range(2):
            out[i][(s - 1) * capacity : s * capacity, :] = ref[
                :, i * (both // 2) : (i + 1) * (both // 2)
            ]


def join_kernel(columns, stay, *refs):
    _, _, column = place()
    parts, flat = refs[:-1], refs[-1]
    capacity = stay.shape[0]
    feat = parts[0].shape[1]
    flat[:capacity, :] = stay[...]
    for m in range(columns):
        cols = pl.ds(pl.multiple_of((column ^ m) * feat, feat), feat)
        flat[capacity:, cols] = parts[m][...]


def part_pieces(hidden, w2, which, columns, out):
    half = w2.shape[1] // 2
    piece = half // columns
    for j in range(columns):
        cols = pl.ds(pl.multiple_of(which * half + j * piece, piece), piece)
        out[j] = dot(hidden, w2[:, cols]).astype(jnp.bfloat16)


def forward_kernel(columns, count, *refs):
    _, core, _ = place()
    flats, refs = refs[:count], refs[count:]
    w1, w2, send, refs = refs[0], refs[1], refs[2], refs[3:]
    for i in range(count):
        pre = dot(flats[i][...], w1[...])
        if len(refs) > count:
            refs[count + i][...] = pre
        hidden = gelu_tanh(pre).astype(jnp.bfloat16)
        refs[i][...] = hidden
        part_pieces(hidden, w2, 1 - core, columns, send.at[i])


def keep_kernel(columns, hidden_own, hidden_other, w2, *refs):
    _, core, _ = place()
    if len(refs) > 2:
        pre_own, pre_other, flat_own, flat_other, keep_own, keep_other = refs[:6]
        flat_t, hidden_t, slope = refs[6:]
    else:
        keep_own, keep_other = refs
    part_pieces(hidden_own[...], w2, core, columns, keep_own)
    part_pieces(hidden_other[...], w2, core, columns, keep_other)
    if len(refs) > 2:
        half = flat_own.shape[0]
        slope[:half, :] = gelu_slope(pre_own[...])
        slope[half:, :] = gelu_slope(pre_other[...])
        hidden_t[...] = jnp.concatenate([hidden_own[...], hidden_other[...]], axis=0).T
        step = 512
        for j in range(0, flat_own.shape[1], step):
            here = slice(j, j + step)
            both = jnp.concatenate([flat_own[:, here], flat_other[:, here]], axis=0)
            flat_t[here, :] = both.T


def pair_kernel(columns, keep_own, keep_other, *refs):
    _, core, column = place()
    half = keep_own.shape[1]
    got, (mine, *out) = refs[:-columns], refs[-columns:]
    got = [ref for ref in got if ref.dtype != jnp.int32]
    got_own, got_other = got[0].at[0], got[-1].at[len(got) % 2]
    for m in range(columns):
        for which, keep, got in ((core, keep_own, got_other), (1 - core, keep_other, got_own)):
            rows = pl.ds(pl.multiple_of(which * half, 16), half)
            both = keep[column ^ m].astype(jnp.float32) + got[column ^ m].astype(jnp.float32)
            if m:
                out[m - 1][rows, :] = both.astype(jnp.bfloat16)
            else:
                mine[rows, :] = both


def total_kernel(columns, experts, *refs):
    sums, out = refs[:columns], refs[columns:]
    total = sums[0][...]
    for ref in sums[1:]:
        total = total + ref[...].astype(jnp.float32)
    total = total.astype(jnp.bfloat16)
    capacity = out[0].shape[0] // 2
    for ref, s in zip(out, plane_order(experts)):
        for c in range(2):
            start = (c * experts + s) * capacity
            ref[c * capacity : (c + 1) * capacity, :] = total[start : start + capacity]


def home_kernel(experts, capacity, maps, *refs):
    got, out = refs[:experts], refs[experts:]
    for c in range(2):
        here = slice(c * capacity, (c + 1) * capacity)
        by_plane = dict(zip(plane_order(experts), got))
        rows = jnp.concatenate([by_plane[s][here, :] for s in range(experts)], axis=0)
        by_slot = dot(maps[c], rows).astype(jnp.bfloat16)
        for ref, s in zip(out, plane_order(experts)):
            ref[here, :] = by_slot[s * capacity : (s + 1) * capacity]


def upstream_kernel(columns, experts, loss_scale, *refs):
    sums, teacher, out = refs[:columns], refs[columns:-1], refs[-1]
    total = sums[0][...]
    for ref in sums[1:]:
        total = total + ref[...].astype(jnp.float32)
    capacity = teacher[0].shape[0] // 2
    teacher = dict(zip(plane_order(experts), teacher))
    rows = jnp.concatenate(
        [
            teacher[s][c * capacity : (c + 1) * capacity, :]
            for c in range(2)
            for s in range(experts)
        ],
        axis=0,
    ).astype(jnp.float32)
    out[...] = ((total - rows) * loss_scale).astype(jnp.bfloat16)


def piece_columns(which, width, piece):
    _, core, column = place()
    other, m = which
    start = (1 - core if other else core) * (width // 2) + (column ^ m) * piece
    return pl.ds(pl.multiple_of(start, piece), piece)


def use_piece(ref, cols, hidden_t, w2, hidden_grad):
    _, core, _ = place()
    half = ref.shape[0] // 2
    rows = jnp.concatenate(
        [ref[pl.ds(pl.multiple_of(block * half, 16), half), :] for block in (core, 1 - core)],
        axis=0,
    )
    term = dot_nt(rows, w2[:, cols])
    hidden_grad = term if hidden_grad is None else hidden_grad + term
    return hidden_grad, rows


def early_kernel(places, first, *refs):
    count = len(places)
    pieces, (hidden_t, w2), refs = refs[:count], refs[count : count + 2], refs[count + 2 :]
    hidden_grad = None if first else refs[0][...]
    sum_out, *grads = refs if first else refs[1:]
    piece, width = pieces[0].shape[1], w2.shape[1]
    for ref, which, out in zip(pieces, places, grads):
        cols = piece_columns(which, width, piece)
        hidden_grad, rows = use_piece(ref, cols, hidden_t, w2, hidden_grad)
        out[...] = dot(hidden_t[...], rows).astype(jnp.bfloat16)
    sum_out[...] = hidden_grad


def last_kernel(places, early, *refs):
    count = len(places)
    pieces, refs = refs[:count], refs[count:]
    done, refs = refs[: len(early)], refs[len(early) :]
    hidden_t, w2, sum_in, flat_t, slope, grad_first, grad_second, held_first, held_second, sems = refs
    piece, width = pieces[0].shape[1], w2.shape[1]
    copies = []

    def leave(source, target):
        copies.append(pltpu.make_async_copy(source, target, sems.at[len(copies)]))
        copies[-1].start()

    for ref, which in zip(done, early):
        leave(ref, grad_second.at[:, piece_columns(which, width, piece)])
    hidden_grad = sum_in[...]
    used = []
    for ref, which in zip(pieces, places):
        cols = piece_columns(which, width, piece)
        hidden_grad, rows = use_piece(ref, cols, hidden_t, w2, hidden_grad)
        used.append((cols, rows))
    pre_grad = (hidden_grad * slope[...]).astype(jnp.bfloat16)
    step = 512
    for j in range(width // step):
        here = slice(j * step, (j + 1) * step)
        held_first[here, :] = dot(flat_t[here, :], pre_grad).astype(jnp.bfloat16)
        leave(held_first.at[here, :], grad_first.at[here, :])
    for i, (cols, rows) in enumerate(used):
        held_second[i] = dot(hidden_t[...], rows).astype(jnp.bfloat16)
        leave(held_second.at[i], grad_second.at[:, cols])
    for copy in copies:
        copy.wait()


def by_kernels(
    teacher_in,
    student_in,
    teacher_route,
    student_route,
    teacher_w1,
    teacher_w2,
    student_w1,
    student_w2,
):
    groups, columns, experts, row_count, width, capacity = sizes(teacher_in)
    plane_rows = groups * capacity
    loss_scale = 1.0 / math.sqrt(row_count)
    feat = width // columns
    piece = feat // 2
    hid = teacher_w1.shape[2]
    f32 = jnp.float32

    def after(value, *others):
        return lax.optimization_barrier((value, others))[0]

    def over_planes(sent):
        return [
            partner(value, "dp", s << 1) for value, s in zip(sent, plane_order(experts))
        ]

    def spread(mine):
        return [mine] + [partner(mine, "expert", m) for m in range(1, columns)]

    def across(value):
        return partner(value, "dp", 1)

    def load(*weights):
        return call(
            load_kernel,
            [shape(*w.shape) for w in weights],
            weights,
            in_specs=[ANY] * len(weights),
            name="load",
            scratch=[pltpu.SemaphoreType.DMA((len(weights),))],
        )

    def forward(flats, w1, w2, keep_pre, name, units=0):
        half, count = plane_rows // 2, len(flats)
        pre = [shape(half, hid, dtype=f32)] * count if keep_pre else []
        return call(
            lambda *refs: forward_kernel(columns, count, *refs),
            [shape(count, columns, half, piece)] + [shape(half, hid)] * count + pre,
            [*flats, w1, w2],
            flops=units * plane_rows * width * hid,
            name=name,
        )

    def keep(own, other, w2, state, outs):
        return call(
            lambda *refs: keep_kernel(columns, *refs),
            [shape(columns, plane_rows // 2, piece)] * 2 + outs,
            [own, other, w2, *state],
            flops=(64 if state else 0) * plane_rows * width * hid,
            name="keep_s" if state else "keep_t",
        )

    def pair(kept, got, marks=()):
        return call(
            lambda *refs: pair_kernel(columns, *refs),
            [shape(plane_rows, piece, dtype=f32)] + [shape(plane_rows, piece)] * (columns - 1),
            [*kept, *marks, *got],
            name="pair",
        )

    def collect(mine, *out):
        return [mine] + [partner(value, "expert", m + 1) for m, value in enumerate(out)]

    route_t = teacher_route.reshape(1, row_count)
    route_s = student_route.reshape(1, row_count)
    def stay(values, route):
        return call(
            lambda *refs: stay_kernel(experts, capacity, *refs),
            [shape(capacity, width)],
            [values, route],
            name="stay",
        )[0]

    sent = call(
        lambda *refs: pack_kernel(experts, capacity, feat, *refs),
        [shape(capacity, 2 * feat)] * (experts - 1),
        [teacher_in, student_in, route_t, route_s],
        in_specs=[ANY] * 4,
        grant=(253 << 20) // 4,
        name="pack",
        scratch=[pltpu.VMEM((row_count, feat), jnp.bfloat16)] * 2
        + [pltpu.VMEM((1, row_count), jnp.int32)] * 2
        + [pltpu.SemaphoreType.DMA((4,))],
    )
    stay_t, stay_s = stay(teacher_in, route_t), stay(student_in, route_s)
    routes = jnp.concatenate([route_t, route_s], axis=0)
    other_routes = across(routes)
    w1_t, w2_t = load(teacher_w1[0], teacher_w2[0])
    moved = after(over_planes(sent), stay_t, other_routes, w1_t)
    mine_t, mine_s = call(
        stack_kernel, [shape((experts - 1) * capacity, feat)] * 2, moved, name="stack"
    )
    got_t, got_s = spread(mine_t), spread(mine_s)
    w1_s, w2_s = load(student_w1[0], student_w2[0])
    (maps,) = call(
        lambda *refs: map_kernel(experts, capacity, *refs),
        [shape(2, experts * capacity, experts * capacity)],
        [routes, other_routes],
        name="maps",
    )

    def join(rows, got):
        return call(
            lambda *refs: join_kernel(columns, *refs),
            [shape(plane_rows // 2, width)],
            [rows, *got],
            name="join",
        )[0]

    flat_t_own = join(stay_t, got_t)
    flat_t_other = across(flat_t_own)

    send, hidden_own = forward([flat_t_own], w1_t, w2_t, False, "forward_t", 24)
    got_own = across(send)
    send, hidden_other = forward([flat_t_other], w1_t, w2_t, False, "forward_t", 0)
    got_other = across(send)
    kept = keep(hidden_own, hidden_other, w2_t, [], [])
    (mark,) = call(
        lambda source, out: out.__setitem__(Ellipsis, source[...]),
        [shape(1, row_count, dtype=jnp.int32)],
        [after(route_t, got_s, w1_s, stay_s, kept[0])],
        flops=8 * plane_rows * width * hid,
        name="mark",
    )
    pieces_t = pair(kept, [got_own, got_other], [mark])
    sums_t = collect(*pieces_t)

    flat_own = join(stay_s, after(got_s, pieces_t[0]))
    flat_other = across(flat_own)
    send, hidden_own, hidden_other, pre_own, pre_other = forward(
        [flat_own, flat_other], w1_s, w2_s, True, "forward_s"
    )
    got = [across(send)]
    *kept, flat_t, hidden_t, slope = keep(
        hidden_own,
        hidden_other,
        w2_s,
        [pre_own, pre_other, flat_own, flat_other],
        [shape(width, plane_rows), shape(hid, plane_rows), shape(plane_rows, hid, dtype=f32)],
    )

    pieces_s = pair(kept, got)
    sums_s = collect(*pieces_s)

    home = call(
        lambda *refs: total_kernel(columns, experts, *refs),
        [shape(2 * capacity, piece)] * experts,
        after(sums_t, pieces_s[0], maps),
    )
    *sent, near, own = home
    home = [*over_planes([*sent, after(near, sums_s[1])]), own]
    slots = call(
        lambda *refs: home_kernel(experts, capacity, *refs),
        [shape(2 * capacity, piece)] * experts,
        [maps, *home],
        flops=5 * plane_rows * width * hid,
        name="home",
    )
    teachers = [*over_planes(slots[:-1]), slots[-1]]
    (upstream,) = call(
        lambda *refs: upstream_kernel(columns, experts, loss_scale, *refs),
        [shape(plane_rows, piece)],
        [*sums_s, *teachers],
    )
    early = {}

    def backward(pieces, total):
        first = total is None
        places = tuple(pieces)
        total, *done = call(
            lambda *refs: early_kernel(places, first, *refs),
            [shape(plane_rows, hid, dtype=f32)] + [shape(hid, piece)] * len(places),
            [*pieces.values(), hidden_t, w2_s] + ([] if first else [total]),
            name="early",
        )
        early.update(zip(places, done))
        return total

    def finish(pieces, total):
        places, kept_places = tuple(pieces), tuple(early)
        return call(
            lambda *refs: last_kernel(places, kept_places, *refs),
            [shape(width, hid), shape(hid, width)],
            [*pieces.values(), *early.values(), hidden_t, w2_s, total, flat_t, slope],
            out_specs=[ANY, ANY],
            scratch=[
                pltpu.VMEM((width, hid), jnp.bfloat16),
                pltpu.VMEM((len(places), hid, piece), jnp.bfloat16),
                pltpu.SemaphoreType.DMA((len(places) + len(early) + width // 512,)),
            ],
            name="last",
        )

    grads = spread(upstream)
    total = backward({(0, 0): upstream, (1, 0): across(upstream)}, None)
    far = after(grads[3], total)
    total = backward({(0, 3): far}, total)
    near = after(grads[1:3], total)
    other_far = across(far)
    others = [across(value) for value in near]
    total = backward({(0, 1): near[0], (0, 2): near[1], (1, 3): other_far}, total)
    grad_first, grad_second = finish({(1, 1): others[0], (1, 2): others[1]}, total)
    return (grad_first[None], grad_second[None])

def on_device(*arrays):
    _, columns, _, row_count, width, capacity = sizes(arrays[0])
    aligned = columns == 4 and capacity % 16 == 0 and row_count % 128 == 0 and width % (256 * columns) == 0
    return by_kernels(*arrays) if aligned else by_ops(*arrays)


def solution(mesh):
    return jax.shard_map(
        on_device,
        mesh=mesh,
        in_specs=(
            P("dp", None),
            P("dp", None),
            P("dp", None),
            P("dp", None),
            P("dp", None, "expert"),
            P("dp", "expert", None),
            P("dp", None, "expert"),
            P("dp", "expert", None),
        ),
        out_specs=(P("dp", None, "expert"), P("dp", "expert", None)),
        check_vma=False,
    )
```

```python
import math

import jax
import jax.numpy as jnp
from jax import lax
from jax.experimental import pallas as pl
from jax.experimental.pallas import tpu as pltpu
from jax.sharding import PartitionSpec as P

root_coef = math.sqrt(2.0 / math.pi)
cubic_coef = 0.044715


def partner(value, axis, mask):
    return lax.ppermute(value, axis, [(i, i ^ mask) for i in range(lax.axis_size(axis))])


def gelu_tanh(pre_act):
    inner_arg = root_coef * (pre_act + cubic_coef * pre_act * pre_act * pre_act)
    return 0.5 * pre_act * (1.0 + jnp.tanh(inner_arg))


def gelu_slope(pre_act):
    tangent = jnp.tanh(root_coef * (pre_act + cubic_coef * pre_act * pre_act * pre_act))
    return 0.5 * (1.0 + tangent) + 0.5 * pre_act * (1.0 - tangent * tangent) * root_coef * (
        1.0 + 3.0 * cubic_coef * pre_act * pre_act
    )


def dot(left, right):
    return jnp.dot(left, right, preferred_element_type=jnp.float32)


def ranks(routes, experts):
    onehot = (routes[..., None] == jnp.arange(experts, dtype=jnp.int32)).astype(jnp.int32)
    rank_table = jnp.cumsum(onehot, axis=1) - 1
    return jnp.sum(onehot * rank_table, axis=2)


def sizes(rows):
    groups = lax.axis_size("dp")
    experts = groups // 2
    row_count, width = rows.shape
    capacity = 2 * max(1, 3 * row_count // (4 * experts))
    return groups, lax.axis_size("expert"), experts, row_count, width, capacity


def by_ops(
    teacher_in,
    student_in,
    teacher_route,
    student_route,
    teacher_w1,
    teacher_w2,
    student_w1,
    student_w2,
):
    groups, columns, experts, row_count, width, capacity = sizes(teacher_in)
    plane_rows = groups * capacity
    dp = lax.axis_index("dp")
    column = lax.axis_index("expert")
    plane, core = dp // 2, dp % 2
    loss_scale = 1.0 / math.sqrt(row_count)
    feat = width // columns
    piece = feat // 2

    def dispatch(values, routes):
        position = ranks(routes[:, 0][None], experts)[0]
        slot = (routes[:, 0] ^ plane) * capacity + position
        placing = (
            jnp.arange(experts * capacity, dtype=jnp.int32)[:, None] == slot[None, :]
        ).astype(jnp.bfloat16)
        own_slice = lax.dynamic_slice(values, (0, column * feat), (row_count, feat))
        slots = dot(placing[capacity:], own_slice).astype(jnp.bfloat16)
        stay = dot(placing[:capacity], values).astype(jnp.bfloat16)
        moved = [
            partner(slots[(s - 1) * capacity : s * capacity], "dp", s << 1)
            for s in range(1, experts)
        ]
        mine = jnp.concatenate(moved, axis=0)
        buffer = jnp.concatenate([stay, jnp.zeros((mine.shape[0], width), jnp.bfloat16)], axis=0)
        for m in range(columns):
            got = partner(mine, "expert", m) if m else mine
            buffer = lax.dynamic_update_slice(buffer, got, (capacity, (column ^ m) * feat))
        other = partner(buffer, "dp", 1)
        first = jnp.where(core == 0, buffer, other)
        second = jnp.where(core == 0, other, buffer)
        return jnp.concatenate([first, second], axis=0)

    def forward(flat, w1, w2):
        pre = dot(flat, w1)
        hidden = gelu_tanh(pre).astype(jnp.bfloat16)
        part = dot(hidden, w2).astype(jnp.bfloat16).reshape(plane_rows, 2, columns, piece)
        part = part.transpose(1, 2, 0, 3)
        return pre, hidden, part

    def plane_sum(part):
        keep = lax.dynamic_index_in_dim(part, core, 0, keepdims=False)
        send = lax.dynamic_index_in_dim(part, 1 - core, 0, keepdims=False)
        pair = (
            keep.astype(jnp.float32) + partner(send, "dp", 1).astype(jnp.float32)
        ).astype(jnp.bfloat16)
        total = lax.dynamic_index_in_dim(pair, column, 0, keepdims=False).astype(jnp.float32)
        for m in range(1, columns):
            out = lax.dynamic_index_in_dim(pair, column ^ m, 0, keepdims=False)
            total = total + partner(out, "expert", m).astype(jnp.float32)
        return total

    routes = jnp.concatenate([teacher_route, student_route], axis=1)
    table = lax.all_gather(routes, "dp", axis=0, tiled=True).reshape(groups, row_count, 2)
    teacher_all, student_all = table[:, :, 0], table[:, :, 1]
    block = jnp.arange(groups, dtype=jnp.int32)[:, None]
    block_plane, block_core = block // 2, block % 2
    teacher_row = (
        (teacher_all ^ plane) * plane_rows
        + (block_core * experts + (block_plane ^ teacher_all)) * capacity
        + ranks(teacher_all, experts)
    )
    student_row = jnp.where(student_all == plane, ranks(student_all, experts), -1)
    hits = jnp.arange(capacity, dtype=jnp.int32)[None, :, None] == student_row[:, None, :]
    source = jnp.sum(jnp.where(hits, teacher_row[:, None, :] + 1, 0), axis=2) - 1
    source = source.reshape(experts, 2, capacity)
    source = source[jnp.arange(experts, dtype=jnp.int32) ^ plane].transpose(1, 0, 2)
    source = source.reshape(plane_rows)

    teacher_flat = dispatch(teacher_in, teacher_route)
    student_flat = dispatch(student_in, student_route)
    _, _, teacher_part = forward(teacher_flat, teacher_w1[0], teacher_w2[0])
    teacher_sum = plane_sum(teacher_part).astype(jnp.bfloat16)
    teacher_sums = jnp.concatenate(
        [teacher_sum] + [partner(teacher_sum, "dp", s << 1) for s in range(1, experts)], axis=0
    )
    student_pre, student_hidden, student_part = forward(
        student_flat, student_w1[0], student_w2[0]
    )
    pick = (
        source[:, None] == jnp.arange(experts * plane_rows, dtype=jnp.int32)[None, :]
    ).astype(jnp.bfloat16)
    teacher_rows = dot(pick, teacher_sums)
    student_sum = plane_sum(student_part)
    upstream = ((student_sum - teacher_rows) * loss_scale).astype(jnp.bfloat16)

    half = jnp.zeros((plane_rows, width // 2), jnp.bfloat16)
    for m in range(columns):
        got = partner(upstream, "expert", m) if m else upstream
        half = lax.dynamic_update_slice(half, got, (0, (column ^ m) * piece))
    other_half = partner(half, "dp", 1)
    grad_flat = jnp.concatenate(
        [jnp.where(core == 0, half, other_half), jnp.where(core == 0, other_half, half)], axis=1
    )
    hidden_grad = dot(grad_flat, student_w2[0].T)
    pre_grad = (hidden_grad * gelu_slope(student_pre)).astype(jnp.bfloat16)
    grad_second = dot(student_hidden.T, grad_flat).astype(jnp.bfloat16)
    grad_first = dot(student_flat.T, pre_grad).astype(jnp.bfloat16)
    return (grad_first[None], grad_second[None])


def plane_order(experts):
    return (*range(2, experts), 1, 0)


def place():
    dp = lax.axis_index("dp")
    return dp // 2, dp % 2, lax.axis_index("expert")


VMEM = pl.BlockSpec(memory_space=pltpu.VMEM)
ANY = pl.BlockSpec(memory_space=pl.ANY)


def call(kernel, outs, operands, out_specs=None, in_specs=None, scratch=(), grant=20 << 20, flops=0, name=None):
    return pl.pallas_call(
        kernel,
        name=name,
        out_shape=outs,
        in_specs=in_specs or [VMEM] * len(operands),
        out_specs=out_specs or [VMEM] * len(outs),
        scratch_shapes=list(scratch),
        compiler_params=pltpu.CompilerParams(vmem_limit_bytes=grant),
        cost_estimate=pl.CostEstimate(flops=flops, bytes_accessed=0, transcendentals=0),
    )(*operands)


def shape(*dims, dtype=jnp.bfloat16):
    return jax.ShapeDtypeStruct(dims, dtype)


def dot_tn(left, right):
    return lax.dot_general(
        left, right, (((0,), (0,)), ((), ())), preferred_element_type=jnp.float32
    )


def dot_nt(left, right):
    return lax.dot_general(
        left, right, (((1,), (1,)), ((), ())), preferred_element_type=jnp.float32
    )


def placing(route, experts, capacity, plane):
    rows = route.shape[1]
    known = lax.broadcasted_iota(jnp.int32, (16 * (-(-experts // 16)), rows), 0)
    onehot = jnp.where(known == route, 1.0, 0.0)
    upto = lax.broadcasted_iota(jnp.int32, (rows, rows), 0) <= lax.broadcasted_iota(
        jnp.int32, (rows, rows), 1
    )
    counts = dot(onehot.astype(jnp.bfloat16), jnp.where(upto, 1.0, 0.0).astype(jnp.bfloat16))
    position = jnp.sum(onehot * counts, axis=0, keepdims=True).astype(jnp.int32) - 1
    slot = (route ^ plane) * capacity + position
    slots = lax.broadcasted_iota(jnp.int32, (experts * capacity, rows), 0)
    return jnp.where(slots == slot, 1.0, 0.0).astype(jnp.bfloat16)


def pack_kernel(experts, capacity, feat, *refs):
    plane, _, column = place()
    values, routes, refs = refs[:2], refs[2:4], refs[4:]
    moved, refs = refs[: 2 * (experts - 1)], refs[2 * (experts - 1) :]
    slices, blocks, sems = refs[:2], refs[2:4], refs[4]
    cols = pl.ds(pl.multiple_of(column * feat, feat), feat)
    copies = [
        pltpu.make_async_copy(routes[0], blocks[0], sems.at[0]),
        pltpu.make_async_copy(routes[1], blocks[1], sems.at[1]),
        pltpu.make_async_copy(values[0].at[:, cols], slices[0], sems.at[2]),
        pltpu.make_async_copy(values[1].at[:, cols], slices[1], sems.at[3]),
    ]
    for copy in copies:
        copy.start()
    for i in range(2):
        copies[i].wait()
    places = [placing(block[...], experts, capacity, plane) for block in blocks]
    for i in range(2):
        copies[2 + i].wait()
    for i in range(2):
        sent = dot(places[i][capacity:], slices[i][...]).astype(jnp.bfloat16)
        for out, s in zip(moved[i * (experts - 1) :], plane_order(experts)[:-1]):
            out[...] = sent[(s - 1) * capacity : s * capacity]


def stay_kernel(experts, capacity, values, route, stay):
    plane, _, _ = place()
    place_rows = placing(route[...], experts, capacity, plane)
    stay[...] = dot(place_rows[:capacity], values[...]).astype(jnp.bfloat16)


def map_kernel(experts, capacity, routes, other_routes, out):
    plane, core, _ = place()
    for c in range(2):
        block = jnp.where(core == c, routes[...], other_routes[...])
        source = placing(block[0:1], experts, capacity, plane)
        target = placing(block[1:2], experts, capacity, plane)
        out[c] = dot_nt(target, source).astype(jnp.bfloat16)


def load_kernel(*refs):
    count = len(refs) // 2
    copies = [
        pltpu.make_async_copy(refs[i], refs[count + i], refs[-1].at[i]) for i in range(count)
    ]
    for copy in copies:
        copy.start()
    for copy in copies:
        copy.wait()


def stack_kernel(*refs):
    moved, out = refs[:-1], refs[-1]
    capacity = moved[0].shape[0]
    for ref, s in zip(moved, plane_order(len(moved) + 1)):
        out[(s - 1) * capacity : s * capacity, :] = ref[...]


def join_kernel(columns, stay, *refs):
    _, _, column = place()
    parts, flat = refs[:-1], refs[-1]
    capacity = stay.shape[0]
    feat = parts[0].shape[1]
    flat[:capacity, :] = stay[...]
    for m in range(columns):
        cols = pl.ds(pl.multiple_of((column ^ m) * feat, feat), feat)
        flat[capacity:, cols] = parts[m][...]


def part_pieces(hidden, w2, which, columns, out):
    half = w2.shape[1] // 2
    piece = half // columns
    for j in range(columns):
        cols = pl.ds(pl.multiple_of(which * half + j * piece, piece), piece)
        out[j] = dot(hidden, w2[:, cols]).astype(jnp.bfloat16)


def forward_kernel(columns, count, *refs):
    _, core, _ = place()
    flats, refs = refs[:count], refs[count:]
    w1, w2, send, refs = refs[0], refs[1], refs[2], refs[3:]
    for i in range(count):
        pre = dot(flats[i][...], w1[...])
        if len(refs) > count:
            refs[count + i][...] = pre
        hidden = gelu_tanh(pre).astype(jnp.bfloat16)
        refs[i][...] = hidden
        part_pieces(hidden, w2, 1 - core, columns, send.at[i])


def keep_kernel(columns, hidden_own, hidden_other, w2, *refs):
    _, core, _ = place()
    if len(refs) > 2:
        pre_own, pre_other, flat_own, flat_other, keep_own, keep_other = refs[:6]
        flat_t, hidden_t, slope = refs[6:]
    else:
        keep_own, keep_other = refs
    part_pieces(hidden_own[...], w2, core, columns, keep_own)
    part_pieces(hidden_other[...], w2, core, columns, keep_other)
    if len(refs) > 2:
        half = flat_own.shape[0]
        slope[:half, :] = gelu_slope(pre_own[...])
        slope[half:, :] = gelu_slope(pre_other[...])
        hidden_t[...] = jnp.concatenate([hidden_own[...], hidden_other[...]], axis=0).T
        step = 512
        for j in range(0, flat_own.shape[1], step):
            here = slice(j, j + step)
            both = jnp.concatenate([flat_own[:, here], flat_other[:, here]], axis=0)
            flat_t[here, :] = both.T


def pair_kernel(columns, keep_own, keep_other, *refs):
    _, core, column = place()
    half = keep_own.shape[1]
    got, (mine, *out) = refs[:-columns], refs[-columns:]
    got = [ref for ref in got if ref.dtype != jnp.int32]
    got_own, got_other = got[0].at[0], got[-1].at[len(got) % 2]
    for m in range(columns):
        for which, keep, got in ((core, keep_own, got_other), (1 - core, keep_other, got_own)):
            rows = pl.ds(pl.multiple_of(which * half, 16), half)
            both = keep[column ^ m].astype(jnp.float32) + got[column ^ m].astype(jnp.float32)
            if m:
                out[m - 1][rows, :] = both.astype(jnp.bfloat16)
            else:
                mine[rows, :] = both


def total_kernel(columns, experts, *refs):
    sums, out = refs[:columns], refs[columns:]
    total = sums[0][...]
    for ref in sums[1:]:
        total = total + ref[...].astype(jnp.float32)
    total = total.astype(jnp.bfloat16)
    capacity = out[0].shape[0] // 2
    for ref, s in zip(out, plane_order(experts)):
        for c in range(2):
            start = (c * experts + s) * capacity
            ref[c * capacity : (c + 1) * capacity, :] = total[start : start + capacity]


def home_kernel(experts, capacity, maps, *refs):
    got, out = refs[:experts], refs[experts:]
    for c in range(2):
        here = slice(c * capacity, (c + 1) * capacity)
        by_plane = dict(zip(plane_order(experts), got))
        rows = jnp.concatenate([by_plane[s][here, :] for s in range(experts)], axis=0)
        by_slot = dot(maps[c], rows).astype(jnp.bfloat16)
        for ref, s in zip(out, plane_order(experts)):
            ref[here, :] = by_slot[s * capacity : (s + 1) * capacity]


def upstream_kernel(columns, experts, loss_scale, *refs):
    sums, teacher, out = refs[:columns], refs[columns:-1], refs[-1]
    total = sums[0][...]
    for ref in sums[1:]:
        total = total + ref[...].astype(jnp.float32)
    capacity = teacher[0].shape[0] // 2
    teacher = dict(zip(plane_order(experts), teacher))
    rows = jnp.concatenate(
        [
            teacher[s][c * capacity : (c + 1) * capacity, :]
            for c in range(2)
            for s in range(experts)
        ],
        axis=0,
    ).astype(jnp.float32)
    out[...] = ((total - rows) * loss_scale).astype(jnp.bfloat16)


def piece_columns(which, width, piece):
    _, core, column = place()
    other, m = which
    start = (1 - core if other else core) * (width // 2) + (column ^ m) * piece
    return pl.ds(pl.multiple_of(start, piece), piece)


def use_piece(ref, cols, hidden_t, w2, hidden_grad):
    _, core, _ = place()
    half = ref.shape[0] // 2
    rows = jnp.concatenate(
        [ref[pl.ds(pl.multiple_of(block * half, 16), half), :] for block in (core, 1 - core)],
        axis=0,
    )
    term = dot_nt(rows, w2[:, cols])
    hidden_grad = term if hidden_grad is None else hidden_grad + term
    return hidden_grad, rows


def early_kernel(places, first, *refs):
    count = len(places)
    pieces, (hidden_t, w2), refs = refs[:count], refs[count : count + 2], refs[count + 2 :]
    hidden_grad = None if first else refs[0][...]
    sum_out, *grads = refs if first else refs[1:]
    piece, width = pieces[0].shape[1], w2.shape[1]
    for ref, which, out in zip(pieces, places, grads):
        cols = piece_columns(which, width, piece)
        hidden_grad, rows = use_piece(ref, cols, hidden_t, w2, hidden_grad)
        out[...] = dot(hidden_t[...], rows).astype(jnp.bfloat16)
    sum_out[...] = hidden_grad


def last_kernel(places, early, *refs):
    count = len(places)
    pieces, refs = refs[:count], refs[count:]
    done, refs = refs[: len(early)], refs[len(early) :]
    hidden_t, w2, sum_in, flat_t, slope, grad_first, grad_second, held_first, held_second, sems = refs
    piece, width = pieces[0].shape[1], w2.shape[1]
    copies = []

    def leave(source, target):
        copies.append(pltpu.make_async_copy(source, target, sems.at[len(copies)]))
        copies[-1].start()

    for ref, which in zip(done, early):
        leave(ref, grad_second.at[:, piece_columns(which, width, piece)])
    hidden_grad = sum_in[...]
    used = []
    for ref, which in zip(pieces, places):
        cols = piece_columns(which, width, piece)
        hidden_grad, rows = use_piece(ref, cols, hidden_t, w2, hidden_grad)
        used.append((cols, rows))
    pre_grad = (hidden_grad * slope[...]).astype(jnp.bfloat16)
    step = 512
    for j in range(width // step):
        here = slice(j * step, (j + 1) * step)
        held_first[here, :] = dot(flat_t[here, :], pre_grad).astype(jnp.bfloat16)
        leave(held_first.at[here, :], grad_first.at[here, :])
    for i, (cols, rows) in enumerate(used):
        held_second[i] = dot(hidden_t[...], rows).astype(jnp.bfloat16)
        leave(held_second.at[i], grad_second.at[:, cols])
    for copy in copies:
        copy.wait()


def by_kernels(
    teacher_in,
    student_in,
    teacher_route,
    student_route,
    teacher_w1,
    teacher_w2,
    student_w1,
    student_w2,
):
    groups, columns, experts, row_count, width, capacity = sizes(teacher_in)
    plane_rows = groups * capacity
    loss_scale = 1.0 / math.sqrt(row_count)
    feat = width // columns
    piece = feat // 2
    hid = teacher_w1.shape[2]
    f32 = jnp.float32

    def after(value, *others):
        return lax.optimization_barrier((value, others))[0]

    def over_planes(sent):
        return [
            partner(value, "dp", s << 1) for value, s in zip(sent, plane_order(experts))
        ]

    def spread(mine):
        return [mine] + [partner(mine, "expert", m) for m in range(1, columns)]

    def across(value):
        return partner(value, "dp", 1)

    def load(*weights):
        return call(
            load_kernel,
            [shape(*w.shape) for w in weights],
            weights,
            in_specs=[ANY] * len(weights),
            name="load",
            scratch=[pltpu.SemaphoreType.DMA((len(weights),))],
        )

    def forward(flats, w1, w2, keep_pre, name, units=0):
        half, count = plane_rows // 2, len(flats)
        pre = [shape(half, hid, dtype=f32)] * count if keep_pre else []
        return call(
            lambda *refs: forward_kernel(columns, count, *refs),
            [shape(count, columns, half, piece)] + [shape(half, hid)] * count + pre,
            [*flats, w1, w2],
            flops=units * plane_rows * width * hid,
            name=name,
        )

    def keep(own, other, w2, state, outs):
        return call(
            lambda *refs: keep_kernel(columns, *refs),
            [shape(columns, plane_rows // 2, piece)] * 2 + outs,
            [own, other, w2, *state],
            flops=(64 if state else 0) * plane_rows * width * hid,
            name="keep_s" if state else "keep_t",
        )

    def pair(kept, got, marks=()):
        return call(
            lambda *refs: pair_kernel(columns, *refs),
            [shape(plane_rows, piece, dtype=f32)] + [shape(plane_rows, piece)] * (columns - 1),
            [*kept, *marks, *got],
            name="pair",
        )

    def collect(mine, *out):
        return [mine] + [partner(value, "expert", m + 1) for m, value in enumerate(out)]

    route_t = teacher_route.reshape(1, row_count)
    route_s = student_route.reshape(1, row_count)
    def stay(values, route):
        return call(
            lambda *refs: stay_kernel(experts, capacity, *refs),
            [shape(capacity, width)],
            [values, route],
            name="stay",
        )[0]

    sent = call(
        lambda *refs: pack_kernel(experts, capacity, feat, *refs),
        [shape(capacity, feat)] * (2 * (experts - 1)),
        [teacher_in, student_in, route_t, route_s],
        in_specs=[ANY] * 4,
        grant=(253 << 20) // 4,
        name="pack",
        scratch=[pltpu.VMEM((row_count, feat), jnp.bfloat16)] * 2
        + [pltpu.VMEM((1, row_count), jnp.int32)] * 2
        + [pltpu.SemaphoreType.DMA((4,))],
    )
    stay_t, stay_s = stay(teacher_in, route_t), stay(student_in, route_s)
    routes = jnp.concatenate([route_t, route_s], axis=0)
    other_routes = across(routes)
    def stack(moved, units=0):
        return call(
            stack_kernel,
            [shape((experts - 1) * capacity, feat)],
            moved,
            flops=units * plane_rows * width * hid,
            name="stack",
        )[0]

    sent_t, sent_s = sent[: experts - 1], sent[experts - 1 :]
    moved_t = after(over_planes(sent_t), stay_t)
    moved_s = over_planes(sent_s)
    mine_t, mine_s = stack(moved_t, 0), stack(moved_s, 8)
    w1_t, w2_t = load(*after((teacher_w1[0], teacher_w2[0]), mine_s))
    got_t, got_s = spread(mine_t), spread(mine_s)
    w1_s, w2_s = load(student_w1[0], student_w2[0])
    (maps,) = call(
        lambda *refs: map_kernel(experts, capacity, *refs),
        [shape(2, experts * capacity, experts * capacity)],
        [routes, other_routes],
        name="maps",
    )

    def join(rows, got):
        return call(
            lambda *refs: join_kernel(columns, *refs),
            [shape(plane_rows // 2, width)],
            [rows, *got],
            name="join",
        )[0]

    flat_t_own = join(stay_t, after(got_t, w1_t))
    flat_t_other = across(flat_t_own)

    send, hidden_own = forward([flat_t_own], w1_t, w2_t, False, "forward_t", 24)
    got_own = across(send)
    send, hidden_other = forward([flat_t_other], w1_t, w2_t, False, "forward_t", 0)
    got_other = across(send)
    kept = keep(hidden_own, hidden_other, w2_t, [], [])
    (mark,) = call(
        lambda source, out: out.__setitem__(Ellipsis, source[...]),
        [shape(1, row_count, dtype=jnp.int32)],
        [after(route_t, got_s, w1_s, stay_s, kept[0])],
        flops=8 * plane_rows * width * hid,
        name="mark",
    )
    pieces_t = pair(kept, [got_own, got_other], [mark])
    sums_t = collect(*pieces_t)

    flat_own = join(stay_s, after(got_s, pieces_t[0]))
    flat_other = across(flat_own)
    send, hidden_own, hidden_other, pre_own, pre_other = forward(
        [flat_own, flat_other], w1_s, w2_s, True, "forward_s"
    )
    got = [across(send)]
    *kept, flat_t, hidden_t, slope = keep(
        hidden_own,
        hidden_other,
        w2_s,
        [pre_own, pre_other, flat_own, flat_other],
        [shape(width, plane_rows), shape(hid, plane_rows), shape(plane_rows, hid, dtype=f32)],
    )

    pieces_s = pair(kept, got)
    sums_s = collect(*pieces_s)

    home = call(
        lambda *refs: total_kernel(columns, experts, *refs),
        [shape(2 * capacity, piece)] * experts,
        after(sums_t, pieces_s[0], maps),
    )
    *sent, near, own = home
    home = [*over_planes([*sent, after(near, sums_s[1])]), own]
    slots = call(
        lambda *refs: home_kernel(experts, capacity, *refs),
        [shape(2 * capacity, piece)] * experts,
        [maps, *home],
        flops=4 * plane_rows * width * hid,
        name="home",
    )
    teachers = [*over_planes(slots[:-1]), slots[-1]]
    (upstream,) = call(
        lambda *refs: upstream_kernel(columns, experts, loss_scale, *refs),
        [shape(plane_rows, piece)],
        [*sums_s, *teachers],
    )
    early = {}

    def backward(pieces, total):
        first = total is None
        places = tuple(pieces)
        total, *done = call(
            lambda *refs: early_kernel(places, first, *refs),
            [shape(plane_rows, hid, dtype=f32)] + [shape(hid, piece)] * len(places),
            [*pieces.values(), hidden_t, w2_s] + ([] if first else [total]),
            name="early",
        )
        early.update(zip(places, done))
        return total

    def finish(pieces, total):
        places, kept_places = tuple(pieces), tuple(early)
        return call(
            lambda *refs: last_kernel(places, kept_places, *refs),
            [shape(width, hid), shape(hid, width)],
            [*pieces.values(), *early.values(), hidden_t, w2_s, total, flat_t, slope],
            out_specs=[ANY, ANY],
            scratch=[
                pltpu.VMEM((width, hid), jnp.bfloat16),
                pltpu.VMEM((len(places), hid, piece), jnp.bfloat16),
                pltpu.SemaphoreType.DMA((len(places) + len(early) + width // 512,)),
            ],
            name="last",
        )

    grads = spread(upstream)
    total = backward({(0, 0): upstream, (1, 0): across(upstream)}, None)
    far = after(grads[3], total)
    total = backward({(0, 3): far}, total)
    near = after(grads[1:3], total)
    other_far = across(far)
    others = [across(value) for value in near]
    total = backward({(0, 1): near[0], (0, 2): near[1], (1, 3): other_far}, total)
    grad_first, grad_second = finish({(1, 1): others[0], (1, 2): others[1]}, total)
    return (grad_first[None], grad_second[None])

def on_device(*arrays):
    _, columns, _, row_count, width, capacity = sizes(arrays[0])
    aligned = columns == 4 and capacity % 16 == 0 and row_count % 128 == 0 and width % (256 * columns) == 0
    return by_kernels(*arrays) if aligned else by_ops(*arrays)


def solution(mesh):
    return jax.shard_map(
        on_device,
        mesh=mesh,
        in_specs=(
            P("dp", None),
            P("dp", None),
            P("dp", None),
            P("dp", None),
            P("dp", None, "expert"),
            P("dp", "expert", None),
            P("dp", None, "expert"),
            P("dp", "expert", None),
        ),
        out_specs=(P("dp", None, "expert"), P("dp", "expert", None)),
        check_vma=False,
    )
```

```python
import math

import jax
import jax.numpy as jnp
from jax import lax
from jax.experimental import pallas as pl
from jax.experimental.pallas import tpu as pltpu
from jax.sharding import PartitionSpec as P

root_coef = math.sqrt(2.0 / math.pi)
cubic_coef = 0.044715


def partner(value, axis, mask):
    return lax.ppermute(value, axis, [(i, i ^ mask) for i in range(lax.axis_size(axis))])


def gelu_tanh(pre_act):
    inner_arg = root_coef * (pre_act + cubic_coef * pre_act * pre_act * pre_act)
    return 0.5 * pre_act * (1.0 + jnp.tanh(inner_arg))


def gelu_slope(pre_act):
    tangent = jnp.tanh(root_coef * (pre_act + cubic_coef * pre_act * pre_act * pre_act))
    return 0.5 * (1.0 + tangent) + 0.5 * pre_act * (1.0 - tangent * tangent) * root_coef * (
        1.0 + 3.0 * cubic_coef * pre_act * pre_act
    )


def dot(left, right):
    return jnp.dot(left, right, preferred_element_type=jnp.float32)


def ranks(routes, experts):
    onehot = (routes[..., None] == jnp.arange(experts, dtype=jnp.int32)).astype(jnp.int32)
    rank_table = jnp.cumsum(onehot, axis=1) - 1
    return jnp.sum(onehot * rank_table, axis=2)


def sizes(rows):
    groups = lax.axis_size("dp")
    experts = groups // 2
    row_count, width = rows.shape
    capacity = 2 * max(1, 3 * row_count // (4 * experts))
    return groups, lax.axis_size("expert"), experts, row_count, width, capacity


def by_ops(
    teacher_in,
    student_in,
    teacher_route,
    student_route,
    teacher_w1,
    teacher_w2,
    student_w1,
    student_w2,
):
    groups, columns, experts, row_count, width, capacity = sizes(teacher_in)
    plane_rows = groups * capacity
    dp = lax.axis_index("dp")
    column = lax.axis_index("expert")
    plane, core = dp // 2, dp % 2
    loss_scale = 1.0 / math.sqrt(row_count)
    feat = width // columns
    piece = feat // 2

    def dispatch(values, routes):
        position = ranks(routes[:, 0][None], experts)[0]
        slot = (routes[:, 0] ^ plane) * capacity + position
        placing = (
            jnp.arange(experts * capacity, dtype=jnp.int32)[:, None] == slot[None, :]
        ).astype(jnp.bfloat16)
        own_slice = lax.dynamic_slice(values, (0, column * feat), (row_count, feat))
        slots = dot(placing[capacity:], own_slice).astype(jnp.bfloat16)
        stay = dot(placing[:capacity], values).astype(jnp.bfloat16)
        moved = [
            partner(slots[(s - 1) * capacity : s * capacity], "dp", s << 1)
            for s in range(1, experts)
        ]
        mine = jnp.concatenate(moved, axis=0)
        buffer = jnp.concatenate([stay, jnp.zeros((mine.shape[0], width), jnp.bfloat16)], axis=0)
        for m in range(columns):
            got = partner(mine, "expert", m) if m else mine
            buffer = lax.dynamic_update_slice(buffer, got, (capacity, (column ^ m) * feat))
        other = partner(buffer, "dp", 1)
        first = jnp.where(core == 0, buffer, other)
        second = jnp.where(core == 0, other, buffer)
        return jnp.concatenate([first, second], axis=0)

    def forward(flat, w1, w2):
        pre = dot(flat, w1)
        hidden = gelu_tanh(pre).astype(jnp.bfloat16)
        part = dot(hidden, w2).astype(jnp.bfloat16).reshape(plane_rows, 2, columns, piece)
        part = part.transpose(1, 2, 0, 3)
        return pre, hidden, part

    def plane_sum(part):
        keep = lax.dynamic_index_in_dim(part, core, 0, keepdims=False)
        send = lax.dynamic_index_in_dim(part, 1 - core, 0, keepdims=False)
        pair = (
            keep.astype(jnp.float32) + partner(send, "dp", 1).astype(jnp.float32)
        ).astype(jnp.bfloat16)
        total = lax.dynamic_index_in_dim(pair, column, 0, keepdims=False).astype(jnp.float32)
        for m in range(1, columns):
            out = lax.dynamic_index_in_dim(pair, column ^ m, 0, keepdims=False)
            total = total + partner(out, "expert", m).astype(jnp.float32)
        return total

    routes = jnp.concatenate([teacher_route, student_route], axis=1)
    table = lax.all_gather(routes, "dp", axis=0, tiled=True).reshape(groups, row_count, 2)
    teacher_all, student_all = table[:, :, 0], table[:, :, 1]
    block = jnp.arange(groups, dtype=jnp.int32)[:, None]
    block_plane, block_core = block // 2, block % 2
    teacher_row = (
        (teacher_all ^ plane) * plane_rows
        + (block_core * experts + (block_plane ^ teacher_all)) * capacity
        + ranks(teacher_all, experts)
    )
    student_row = jnp.where(student_all == plane, ranks(student_all, experts), -1)
    hits = jnp.arange(capacity, dtype=jnp.int32)[None, :, None] == student_row[:, None, :]
    source = jnp.sum(jnp.where(hits, teacher_row[:, None, :] + 1, 0), axis=2) - 1
    source = source.reshape(experts, 2, capacity)
    source = source[jnp.arange(experts, dtype=jnp.int32) ^ plane].transpose(1, 0, 2)
    source = source.reshape(plane_rows)

    teacher_flat = dispatch(teacher_in, teacher_route)
    student_flat = dispatch(student_in, student_route)
    _, _, teacher_part = forward(teacher_flat, teacher_w1[0], teacher_w2[0])
    teacher_sum = plane_sum(teacher_part).astype(jnp.bfloat16)
    teacher_sums = jnp.concatenate(
        [teacher_sum] + [partner(teacher_sum, "dp", s << 1) for s in range(1, experts)], axis=0
    )
    student_pre, student_hidden, student_part = forward(
        student_flat, student_w1[0], student_w2[0]
    )
    pick = (
        source[:, None] == jnp.arange(experts * plane_rows, dtype=jnp.int32)[None, :]
    ).astype(jnp.bfloat16)
    teacher_rows = dot(pick, teacher_sums)
    student_sum = plane_sum(student_part)
    upstream = ((student_sum - teacher_rows) * loss_scale).astype(jnp.bfloat16)

    half = jnp.zeros((plane_rows, width // 2), jnp.bfloat16)
    for m in range(columns):
        got = partner(upstream, "expert", m) if m else upstream
        half = lax.dynamic_update_slice(half, got, (0, (column ^ m) * piece))
    other_half = partner(half, "dp", 1)
    grad_flat = jnp.concatenate(
        [jnp.where(core == 0, half, other_half), jnp.where(core == 0, other_half, half)], axis=1
    )
    hidden_grad = dot(grad_flat, student_w2[0].T)
    pre_grad = (hidden_grad * gelu_slope(student_pre)).astype(jnp.bfloat16)
    grad_second = dot(student_hidden.T, grad_flat).astype(jnp.bfloat16)
    grad_first = dot(student_flat.T, pre_grad).astype(jnp.bfloat16)
    return (grad_first[None], grad_second[None])


def plane_order(experts):
    return (*range(2, experts), 1, 0)


def place():
    dp = lax.axis_index("dp")
    return dp // 2, dp % 2, lax.axis_index("expert")


VMEM = pl.BlockSpec(memory_space=pltpu.VMEM)
ANY = pl.BlockSpec(memory_space=pl.ANY)


def call(kernel, outs, operands, out_specs=None, in_specs=None, scratch=(), grant=20 << 20, flops=0, name=None):
    return pl.pallas_call(
        kernel,
        name=name,
        out_shape=outs,
        in_specs=in_specs or [VMEM] * len(operands),
        out_specs=out_specs or [VMEM] * len(outs),
        scratch_shapes=list(scratch),
        compiler_params=pltpu.CompilerParams(vmem_limit_bytes=grant),
        cost_estimate=pl.CostEstimate(flops=flops, bytes_accessed=0, transcendentals=0),
    )(*operands)


def shape(*dims, dtype=jnp.bfloat16):
    return jax.ShapeDtypeStruct(dims, dtype)


def dot_tn(left, right):
    return lax.dot_general(
        left, right, (((0,), (0,)), ((), ())), preferred_element_type=jnp.float32
    )


def dot_nt(left, right):
    return lax.dot_general(
        left, right, (((1,), (1,)), ((), ())), preferred_element_type=jnp.float32
    )


def placing(route, experts, capacity, plane):
    rows = route.shape[1]
    known = lax.broadcasted_iota(jnp.int32, (16 * (-(-experts // 16)), rows), 0)
    onehot = jnp.where(known == route, 1.0, 0.0)
    upto = lax.broadcasted_iota(jnp.int32, (rows, rows), 0) <= lax.broadcasted_iota(
        jnp.int32, (rows, rows), 1
    )
    counts = dot(onehot.astype(jnp.bfloat16), jnp.where(upto, 1.0, 0.0).astype(jnp.bfloat16))
    position = jnp.sum(onehot * counts, axis=0, keepdims=True).astype(jnp.int32) - 1
    slot = (route ^ plane) * capacity + position
    slots = lax.broadcasted_iota(jnp.int32, (experts * capacity, rows), 0)
    return jnp.where(slots == slot, 1.0, 0.0).astype(jnp.bfloat16)


def pack_kernel(experts, capacity, feat, *refs):
    plane, _, column = place()
    values, routes, refs = refs[:2], refs[2:4], refs[4:]
    moved, refs = refs[: 2 * (experts - 1)], refs[2 * (experts - 1) :]
    slices, blocks, sems = refs[:2], refs[2:4], refs[4]
    cols = pl.ds(pl.multiple_of(column * feat, feat), feat)
    copies = [
        pltpu.make_async_copy(routes[0], blocks[0], sems.at[0]),
        pltpu.make_async_copy(routes[1], blocks[1], sems.at[1]),
        pltpu.make_async_copy(values[0].at[:, cols], slices[0], sems.at[2]),
        pltpu.make_async_copy(values[1].at[:, cols], slices[1], sems.at[3]),
    ]
    for copy in copies:
        copy.start()
    for i in range(2):
        copies[i].wait()
    places = [placing(block[...], experts, capacity, plane) for block in blocks]
    for i in range(2):
        copies[2 + i].wait()
    for i in range(2):
        sent = dot(places[i][capacity:], slices[i][...]).astype(jnp.bfloat16)
        for out, s in zip(moved[i * (experts - 1) :], plane_order(experts)[:-1]):
            out[...] = sent[(s - 1) * capacity : s * capacity]


def stay_kernel(experts, capacity, values, route, stay):
    plane, _, _ = place()
    place_rows = placing(route[...], experts, capacity, plane)
    stay[...] = dot(place_rows[:capacity], values[...]).astype(jnp.bfloat16)


def map_kernel(experts, capacity, routes, other_routes, out):
    plane, core, _ = place()
    for c in range(2):
        block = jnp.where(core == c, routes[...], other_routes[...])
        source = placing(block[0:1], experts, capacity, plane)
        target = placing(block[1:2], experts, capacity, plane)
        out[c] = dot_nt(target, source).astype(jnp.bfloat16)


def load_kernel(*refs):
    count = len(refs) // 2
    copies = [
        pltpu.make_async_copy(refs[i], refs[count + i], refs[-1].at[i]) for i in range(count)
    ]
    for copy in copies:
        copy.start()
    for copy in copies:
        copy.wait()


def stack_kernel(*refs):
    moved, out = refs[:-1], refs[-1]
    capacity = moved[0].shape[0]
    for ref, s in zip(moved, plane_order(len(moved) + 1)):
        out[(s - 1) * capacity : s * capacity, :] = ref[...]


def join_kernel(columns, stay, *refs):
    _, _, column = place()
    parts, flat = refs[:-1], refs[-1]
    capacity = stay.shape[0]
    feat = parts[0].shape[1]
    flat[:capacity, :] = stay[...]
    for m in range(columns):
        cols = pl.ds(pl.multiple_of((column ^ m) * feat, feat), feat)
        flat[capacity:, cols] = parts[m][...]


def part_pieces(hidden, w2, which, columns, out):
    half = w2.shape[1] // 2
    piece = half // columns
    for j in range(columns):
        cols = pl.ds(pl.multiple_of(which * half + j * piece, piece), piece)
        out[j] = dot(hidden, w2[:, cols]).astype(jnp.bfloat16)


def forward_kernel(columns, count, *refs):
    _, core, _ = place()
    flats, refs = refs[:count], refs[count:]
    w1, w2, send, refs = refs[0], refs[1], refs[2], refs[3:]
    for i in range(count):
        pre = dot(flats[i][...], w1[...])
        if len(refs) > count:
            refs[count + i][...] = pre
        hidden = gelu_tanh(pre).astype(jnp.bfloat16)
        refs[i][...] = hidden
        part_pieces(hidden, w2, 1 - core, columns, send.at[i])


def keep_kernel(columns, hidden_own, hidden_other, w2, *refs):
    _, core, _ = place()
    if len(refs) > 2:
        pre_own, pre_other, flat_own, flat_other, keep_own, keep_other = refs[:6]
        flat_t, hidden_t, slope = refs[6:]
    else:
        keep_own, keep_other = refs
    part_pieces(hidden_own[...], w2, core, columns, keep_own)
    part_pieces(hidden_other[...], w2, core, columns, keep_other)
    if len(refs) > 2:
        half = flat_own.shape[0]
        slope[:half, :] = gelu_slope(pre_own[...])
        slope[half:, :] = gelu_slope(pre_other[...])
        hidden_t[...] = jnp.concatenate([hidden_own[...], hidden_other[...]], axis=0).T
        step = 512
        for j in range(0, flat_own.shape[1], step):
            here = slice(j, j + step)
            both = jnp.concatenate([flat_own[:, here], flat_other[:, here]], axis=0)
            flat_t[here, :] = both.T


def pair_kernel(columns, keep_own, keep_other, *refs):
    _, core, column = place()
    half = keep_own.shape[1]
    got, (mine, *out) = refs[:-columns], refs[-columns:]
    got = [ref for ref in got if ref.dtype != jnp.int32]
    got_own, got_other = got[0].at[0], got[-1].at[len(got) % 2]
    for m in range(columns):
        for which, keep, got in ((core, keep_own, got_other), (1 - core, keep_other, got_own)):
            rows = pl.ds(pl.multiple_of(which * half, 16), half)
            both = keep[column ^ m].astype(jnp.float32) + got[column ^ m].astype(jnp.float32)
            if m:
                out[m - 1][rows, :] = both.astype(jnp.bfloat16)
            else:
                mine[rows, :] = both


def total_kernel(columns, experts, *refs):
    sums, out = refs[:columns], refs[columns:]
    total = sums[0][...]
    for ref in sums[1:]:
        total = total + ref[...].astype(jnp.float32)
    total = total.astype(jnp.bfloat16)
    capacity = out[0].shape[0] // 2
    for ref, s in zip(out, plane_order(experts)):
        for c in range(2):
            start = (c * experts + s) * capacity
            ref[c * capacity : (c + 1) * capacity, :] = total[start : start + capacity]


def home_kernel(experts, capacity, maps, *refs):
    got, out = refs[:experts], refs[experts:]
    for c in range(2):
        here = slice(c * capacity, (c + 1) * capacity)
        by_plane = dict(zip(plane_order(experts), got))
        rows = jnp.concatenate([by_plane[s][here, :] for s in range(experts)], axis=0)
        by_slot = dot(maps[c], rows).astype(jnp.bfloat16)
        for ref, s in zip(out, plane_order(experts)):
            ref[here, :] = by_slot[s * capacity : (s + 1) * capacity]


def upstream_kernel(columns, experts, loss_scale, *refs):
    sums, teacher, out = refs[:columns], refs[columns:-1], refs[-1]
    total = sums[0][...]
    for ref in sums[1:]:
        total = total + ref[...].astype(jnp.float32)
    capacity = teacher[0].shape[0] // 2
    teacher = dict(zip(plane_order(experts), teacher))
    rows = jnp.concatenate(
        [
            teacher[s][c * capacity : (c + 1) * capacity, :]
            for c in range(2)
            for s in range(experts)
        ],
        axis=0,
    ).astype(jnp.float32)
    out[...] = ((total - rows) * loss_scale).astype(jnp.bfloat16)


def piece_columns(which, width, piece):
    _, core, column = place()
    other, m = which
    start = (1 - core if other else core) * (width // 2) + (column ^ m) * piece
    return pl.ds(pl.multiple_of(start, piece), piece)


def use_piece(ref, cols, hidden_t, w2, hidden_grad):
    _, core, _ = place()
    half = ref.shape[0] // 2
    rows = jnp.concatenate(
        [ref[pl.ds(pl.multiple_of(block * half, 16), half), :] for block in (core, 1 - core)],
        axis=0,
    )
    term = dot_nt(rows, w2[:, cols])
    hidden_grad = term if hidden_grad is None else hidden_grad + term
    return hidden_grad, rows


def early_kernel(places, first, *refs):
    count = len(places)
    pieces, (hidden_t, w2), refs = refs[:count], refs[count : count + 2], refs[count + 2 :]
    hidden_grad = None if first else refs[0][...]
    sum_out, *grads = refs if first else refs[1:]
    piece, width = pieces[0].shape[1], w2.shape[1]
    for ref, which, out in zip(pieces, places, grads):
        cols = piece_columns(which, width, piece)
        hidden_grad, rows = use_piece(ref, cols, hidden_t, w2, hidden_grad)
        out[...] = dot(hidden_t[...], rows).astype(jnp.bfloat16)
    sum_out[...] = hidden_grad


def last_kernel(places, early, *refs):
    count = len(places)
    pieces, refs = refs[:count], refs[count:]
    done, refs = refs[: len(early)], refs[len(early) :]
    hidden_t, w2, sum_in, flat_t, slope, grad_first, grad_second, held_first, held_second, sems = refs
    piece, width = pieces[0].shape[1], w2.shape[1]
    copies = []

    def leave(source, target):
        copies.append(pltpu.make_async_copy(source, target, sems.at[len(copies)]))
        copies[-1].start()

    for ref, which in zip(done, early):
        leave(ref, grad_second.at[:, piece_columns(which, width, piece)])
    hidden_grad = sum_in[...]
    used = []
    for ref, which in zip(pieces, places):
        cols = piece_columns(which, width, piece)
        hidden_grad, rows = use_piece(ref, cols, hidden_t, w2, hidden_grad)
        used.append((cols, rows))
    pre_grad = (hidden_grad * slope[...]).astype(jnp.bfloat16)
    step = 512
    for j in range(width // step):
        here = slice(j * step, (j + 1) * step)
        held_first[here, :] = dot(flat_t[here, :], pre_grad).astype(jnp.bfloat16)
        leave(held_first.at[here, :], grad_first.at[here, :])
    for i, (cols, rows) in enumerate(used):
        held_second[i] = dot(hidden_t[...], rows).astype(jnp.bfloat16)
        leave(held_second.at[i], grad_second.at[:, cols])
    for copy in copies:
        copy.wait()


def by_kernels(
    teacher_in,
    student_in,
    teacher_route,
    student_route,
    teacher_w1,
    teacher_w2,
    student_w1,
    student_w2,
):
    groups, columns, experts, row_count, width, capacity = sizes(teacher_in)
    plane_rows = groups * capacity
    loss_scale = 1.0 / math.sqrt(row_count)
    feat = width // columns
    piece = feat // 2
    hid = teacher_w1.shape[2]
    f32 = jnp.float32

    def after(value, *others):
        return lax.optimization_barrier((value, others))[0]

    def over_planes(sent):
        return [
            partner(value, "dp", s << 1) for value, s in zip(sent, plane_order(experts))
        ]

    def spread(mine):
        return [mine] + [partner(mine, "expert", m) for m in range(1, columns)]

    def across(value):
        return partner(value, "dp", 1)

    def load(*weights):
        return call(
            load_kernel,
            [shape(*w.shape) for w in weights],
            weights,
            in_specs=[ANY] * len(weights),
            name="load",
            scratch=[pltpu.SemaphoreType.DMA((len(weights),))],
        )

    def forward(flats, w1, w2, keep_pre, name, units=0):
        half, count = plane_rows // 2, len(flats)
        pre = [shape(half, hid, dtype=f32)] * count if keep_pre else []
        return call(
            lambda *refs: forward_kernel(columns, count, *refs),
            [shape(count, columns, half, piece)] + [shape(half, hid)] * count + pre,
            [*flats, w1, w2],
            flops=units * plane_rows * width * hid,
            name=name,
        )

    def keep(own, other, w2, state, outs):
        return call(
            lambda *refs: keep_kernel(columns, *refs),
            [shape(columns, plane_rows // 2, piece)] * 2 + outs,
            [own, other, w2, *state],
            flops=(64 if state else 0) * plane_rows * width * hid,
            name="keep_s" if state else "keep_t",
        )

    def pair(kept, got, marks=()):
        return call(
            lambda *refs: pair_kernel(columns, *refs),
            [shape(plane_rows, piece, dtype=f32)] + [shape(plane_rows, piece)] * (columns - 1),
            [*kept, *marks, *got],
            name="pair",
        )

    def collect(mine, *out):
        return [mine] + [partner(value, "expert", m + 1) for m, value in enumerate(out)]

    route_t = teacher_route.reshape(1, row_count)
    route_s = student_route.reshape(1, row_count)
    def stay(values, route):
        return call(
            lambda *refs: stay_kernel(experts, capacity, *refs),
            [shape(capacity, width)],
            [values, route],
            name="stay",
        )[0]

    sent = call(
        lambda *refs: pack_kernel(experts, capacity, feat, *refs),
        [shape(capacity, feat)] * (2 * (experts - 1)),
        [teacher_in, student_in, route_t, route_s],
        in_specs=[ANY] * 4,
        grant=(253 << 20) // 4,
        name="pack",
        scratch=[pltpu.VMEM((row_count, feat), jnp.bfloat16)] * 2
        + [pltpu.VMEM((1, row_count), jnp.int32)] * 2
        + [pltpu.SemaphoreType.DMA((4,))],
    )
    stay_s = stay(student_in, route_s)
    routes = jnp.concatenate([route_t, route_s], axis=0)
    other_routes = across(routes)
    def stack(moved, units=0):
        return call(
            stack_kernel,
            [shape((experts - 1) * capacity, feat)],
            moved,
            flops=units * plane_rows * width * hid,
            name="stack",
        )[0]

    sent_t, sent_s = sent[: experts - 1], sent[experts - 1 :]
    moved_t = over_planes(sent_t)
    moved_s = over_planes(sent_s)
    mine_t, mine_s = stack(moved_t, 0), stack(moved_s, 8)
    w1_t, w2_t = load(*after((teacher_w1[0], teacher_w2[0]), mine_s))
    stay_t = stay(after(teacher_in, mine_s), route_t)
    got_t, got_s = spread(mine_t), spread(mine_s)
    w1_s, w2_s = load(student_w1[0], student_w2[0])
    (maps,) = call(
        lambda *refs: map_kernel(experts, capacity, *refs),
        [shape(2, experts * capacity, experts * capacity)],
        [routes, other_routes],
        name="maps",
    )

    def join(rows, got):
        return call(
            lambda *refs: join_kernel(columns, *refs),
            [shape(plane_rows // 2, width)],
            [rows, *got],
            name="join",
        )[0]

    flat_t_own = join(stay_t, after(got_t, w1_t))
    flat_t_other = across(flat_t_own)

    send, hidden_own = forward([flat_t_own], w1_t, w2_t, False, "forward_t", 24)
    got_own = across(send)
    send, hidden_other = forward([flat_t_other], w1_t, w2_t, False, "forward_t", 0)
    got_other = across(send)
    kept = keep(hidden_own, hidden_other, w2_t, [], [])
    (mark,) = call(
        lambda source, out: out.__setitem__(Ellipsis, source[...]),
        [shape(1, row_count, dtype=jnp.int32)],
        [after(route_t, got_s, w1_s, stay_s, kept[0])],
        flops=8 * plane_rows * width * hid,
        name="mark",
    )
    pieces_t = pair(kept, [got_own, got_other], [mark])
    sums_t = collect(*pieces_t)

    flat_own = join(stay_s, after(got_s, pieces_t[0]))
    flat_other = across(flat_own)
    send, hidden_own, hidden_other, pre_own, pre_other = forward(
        [flat_own, flat_other], w1_s, w2_s, True, "forward_s"
    )
    got = [across(send)]
    *kept, flat_t, hidden_t, slope = keep(
        hidden_own,
        hidden_other,
        w2_s,
        [pre_own, pre_other, flat_own, flat_other],
        [shape(width, plane_rows), shape(hid, plane_rows), shape(plane_rows, hid, dtype=f32)],
    )

    pieces_s = pair(kept, got)
    sums_s = collect(*pieces_s)

    home = call(
        lambda *refs: total_kernel(columns, experts, *refs),
        [shape(2 * capacity, piece)] * experts,
        after(sums_t, pieces_s[0], maps),
    )
    *sent, near, own = home
    home = [*over_planes([*sent, after(near, sums_s[1])]), own]
    slots = call(
        lambda *refs: home_kernel(experts, capacity, *refs),
        [shape(2 * capacity, piece)] * experts,
        [maps, *home],
        flops=4 * plane_rows * width * hid,
        name="home",
    )
    teachers = [*over_planes(slots[:-1]), slots[-1]]
    (upstream,) = call(
        lambda *refs: upstream_kernel(columns, experts, loss_scale, *refs),
        [shape(plane_rows, piece)],
        [*sums_s, *teachers],
    )
    early = {}

    def backward(pieces, total):
        first = total is None
        places = tuple(pieces)
        total, *done = call(
            lambda *refs: early_kernel(places, first, *refs),
            [shape(plane_rows, hid, dtype=f32)] + [shape(hid, piece)] * len(places),
            [*pieces.values(), hidden_t, w2_s] + ([] if first else [total]),
            name="early",
        )
        early.update(zip(places, done))
        return total

    def finish(pieces, total):
        places, kept_places = tuple(pieces), tuple(early)
        return call(
            lambda *refs: last_kernel(places, kept_places, *refs),
            [shape(width, hid), shape(hid, width)],
            [*pieces.values(), *early.values(), hidden_t, w2_s, total, flat_t, slope],
            out_specs=[ANY, ANY],
            scratch=[
                pltpu.VMEM((width, hid), jnp.bfloat16),
                pltpu.VMEM((len(places), hid, piece), jnp.bfloat16),
                pltpu.SemaphoreType.DMA((len(places) + len(early) + width // 512,)),
            ],
            name="last",
        )

    grads = spread(upstream)
    total = backward({(0, 0): upstream, (1, 0): across(upstream)}, None)
    far = after(grads[3], total)
    total = backward({(0, 3): far}, total)
    near = after(grads[1:3], total)
    other_far = across(far)
    others = [across(value) for value in near]
    total = backward({(0, 1): near[0], (0, 2): near[1], (1, 3): other_far}, total)
    grad_first, grad_second = finish({(1, 1): others[0], (1, 2): others[1]}, total)
    return (grad_first[None], grad_second[None])

def on_device(*arrays):
    _, columns, _, row_count, width, capacity = sizes(arrays[0])
    aligned = columns == 4 and capacity % 16 == 0 and row_count % 128 == 0 and width % (256 * columns) == 0
    return by_kernels(*arrays) if aligned else by_ops(*arrays)


def solution(mesh):
    return jax.shard_map(
        on_device,
        mesh=mesh,
        in_specs=(
            P("dp", None),
            P("dp", None),
            P("dp", None),
            P("dp", None),
            P("dp", None, "expert"),
            P("dp", "expert", None),
            P("dp", None, "expert"),
            P("dp", "expert", None),
        ),
        out_specs=(P("dp", None, "expert"), P("dp", "expert", None)),
        check_vma=False,
    )
```

```python
import math

import jax
import jax.numpy as jnp
from jax import lax
from jax.experimental import pallas as pl
from jax.experimental.pallas import tpu as pltpu
from jax.sharding import PartitionSpec as P

root_coef = math.sqrt(2.0 / math.pi)
cubic_coef = 0.044715


def partner(value, axis, mask):
    return lax.ppermute(value, axis, [(i, i ^ mask) for i in range(lax.axis_size(axis))])


def gelu_tanh(pre_act):
    inner_arg = root_coef * (pre_act + cubic_coef * pre_act * pre_act * pre_act)
    return 0.5 * pre_act * (1.0 + jnp.tanh(inner_arg))


def gelu_slope(pre_act):
    tangent = jnp.tanh(root_coef * (pre_act + cubic_coef * pre_act * pre_act * pre_act))
    return 0.5 * (1.0 + tangent) + 0.5 * pre_act * (1.0 - tangent * tangent) * root_coef * (
        1.0 + 3.0 * cubic_coef * pre_act * pre_act
    )


def dot(left, right):
    return jnp.dot(left, right, preferred_element_type=jnp.float32)


def ranks(routes, experts):
    onehot = (routes[..., None] == jnp.arange(experts, dtype=jnp.int32)).astype(jnp.int32)
    rank_table = jnp.cumsum(onehot, axis=1) - 1
    return jnp.sum(onehot * rank_table, axis=2)


def sizes(rows):
    groups = lax.axis_size("dp")
    experts = groups // 2
    row_count, width = rows.shape
    capacity = 2 * max(1, 3 * row_count // (4 * experts))
    return groups, lax.axis_size("expert"), experts, row_count, width, capacity


def by_ops(
    teacher_in,
    student_in,
    teacher_route,
    student_route,
    teacher_w1,
    teacher_w2,
    student_w1,
    student_w2,
):
    groups, columns, experts, row_count, width, capacity = sizes(teacher_in)
    plane_rows = groups * capacity
    dp = lax.axis_index("dp")
    column = lax.axis_index("expert")
    plane, core = dp // 2, dp % 2
    loss_scale = 1.0 / math.sqrt(row_count)
    feat = width // columns
    piece = feat // 2

    def dispatch(values, routes):
        position = ranks(routes[:, 0][None], experts)[0]
        slot = (routes[:, 0] ^ plane) * capacity + position
        placing = (
            jnp.arange(experts * capacity, dtype=jnp.int32)[:, None] == slot[None, :]
        ).astype(jnp.bfloat16)
        own_slice = lax.dynamic_slice(values, (0, column * feat), (row_count, feat))
        slots = dot(placing[capacity:], own_slice).astype(jnp.bfloat16)
        stay = dot(placing[:capacity], values).astype(jnp.bfloat16)
        moved = [
            partner(slots[(s - 1) * capacity : s * capacity], "dp", s << 1)
            for s in range(1, experts)
        ]
        mine = jnp.concatenate(moved, axis=0)
        buffer = jnp.concatenate([stay, jnp.zeros((mine.shape[0], width), jnp.bfloat16)], axis=0)
        for m in range(columns):
            got = partner(mine, "expert", m) if m else mine
            buffer = lax.dynamic_update_slice(buffer, got, (capacity, (column ^ m) * feat))
        other = partner(buffer, "dp", 1)
        first = jnp.where(core == 0, buffer, other)
        second = jnp.where(core == 0, other, buffer)
        return jnp.concatenate([first, second], axis=0)

    def forward(flat, w1, w2):
        pre = dot(flat, w1)
        hidden = gelu_tanh(pre).astype(jnp.bfloat16)
        part = dot(hidden, w2).astype(jnp.bfloat16).reshape(plane_rows, 2, columns, piece)
        part = part.transpose(1, 2, 0, 3)
        return pre, hidden, part

    def plane_sum(part):
        keep = lax.dynamic_index_in_dim(part, core, 0, keepdims=False)
        send = lax.dynamic_index_in_dim(part, 1 - core, 0, keepdims=False)
        pair = (
            keep.astype(jnp.float32) + partner(send, "dp", 1).astype(jnp.float32)
        ).astype(jnp.bfloat16)
        total = lax.dynamic_index_in_dim(pair, column, 0, keepdims=False).astype(jnp.float32)
        for m in range(1, columns):
            out = lax.dynamic_index_in_dim(pair, column ^ m, 0, keepdims=False)
            total = total + partner(out, "expert", m).astype(jnp.float32)
        return total

    routes = jnp.concatenate([teacher_route, student_route], axis=1)
    table = lax.all_gather(routes, "dp", axis=0, tiled=True).reshape(groups, row_count, 2)
    teacher_all, student_all = table[:, :, 0], table[:, :, 1]
    block = jnp.arange(groups, dtype=jnp.int32)[:, None]
    block_plane, block_core = block // 2, block % 2
    teacher_row = (
        (teacher_all ^ plane) * plane_rows
        + (block_core * experts + (block_plane ^ teacher_all)) * capacity
        + ranks(teacher_all, experts)
    )
    student_row = jnp.where(student_all == plane, ranks(student_all, experts), -1)
    hits = jnp.arange(capacity, dtype=jnp.int32)[None, :, None] == student_row[:, None, :]
    source = jnp.sum(jnp.where(hits, teacher_row[:, None, :] + 1, 0), axis=2) - 1
    source = source.reshape(experts, 2, capacity)
    source = source[jnp.arange(experts, dtype=jnp.int32) ^ plane].transpose(1, 0, 2)
    source = source.reshape(plane_rows)

    teacher_flat = dispatch(teacher_in, teacher_route)
    student_flat = dispatch(student_in, student_route)
    _, _, teacher_part = forward(teacher_flat, teacher_w1[0], teacher_w2[0])
    teacher_sum = plane_sum(teacher_part).astype(jnp.bfloat16)
    teacher_sums = jnp.concatenate(
        [teacher_sum] + [partner(teacher_sum, "dp", s << 1) for s in range(1, experts)], axis=0
    )
    student_pre, student_hidden, student_part = forward(
        student_flat, student_w1[0], student_w2[0]
    )
    pick = (
        source[:, None] == jnp.arange(experts * plane_rows, dtype=jnp.int32)[None, :]
    ).astype(jnp.bfloat16)
    teacher_rows = dot(pick, teacher_sums)
    student_sum = plane_sum(student_part)
    upstream = ((student_sum - teacher_rows) * loss_scale).astype(jnp.bfloat16)

    half = jnp.zeros((plane_rows, width // 2), jnp.bfloat16)
    for m in range(columns):
        got = partner(upstream, "expert", m) if m else upstream
        half = lax.dynamic_update_slice(half, got, (0, (column ^ m) * piece))
    other_half = partner(half, "dp", 1)
    grad_flat = jnp.concatenate(
        [jnp.where(core == 0, half, other_half), jnp.where(core == 0, other_half, half)], axis=1
    )
    hidden_grad = dot(grad_flat, student_w2[0].T)
    pre_grad = (hidden_grad * gelu_slope(student_pre)).astype(jnp.bfloat16)
    grad_second = dot(student_hidden.T, grad_flat).astype(jnp.bfloat16)
    grad_first = dot(student_flat.T, pre_grad).astype(jnp.bfloat16)
    return (grad_first[None], grad_second[None])


def plane_order(experts, near_first=False):
    return (*range(1, experts), 0) if near_first else (*range(2, experts), 1, 0)


def place():
    dp = lax.axis_index("dp")
    return dp // 2, dp % 2, lax.axis_index("expert")


VMEM = pl.BlockSpec(memory_space=pltpu.VMEM)
ANY = pl.BlockSpec(memory_space=pl.ANY)


def call(kernel, outs, operands, out_specs=None, in_specs=None, scratch=(), grant=20 << 20, flops=0, name=None):
    return pl.pallas_call(
        kernel,
        name=name,
        out_shape=outs,
        in_specs=in_specs or [VMEM] * len(operands),
        out_specs=out_specs or [VMEM] * len(outs),
        scratch_shapes=list(scratch),
        compiler_params=pltpu.CompilerParams(vmem_limit_bytes=grant),
        cost_estimate=pl.CostEstimate(flops=flops, bytes_accessed=0, transcendentals=0),
    )(*operands)


def shape(*dims, dtype=jnp.bfloat16):
    return jax.ShapeDtypeStruct(dims, dtype)


def dot_tn(left, right):
    return lax.dot_general(
        left, right, (((0,), (0,)), ((), ())), preferred_element_type=jnp.float32
    )


def dot_nt(left, right):
    return lax.dot_general(
        left, right, (((1,), (1,)), ((), ())), preferred_element_type=jnp.float32
    )


def placing(route, experts, capacity, plane):
    rows = route.shape[1]
    known = lax.broadcasted_iota(jnp.int32, (16 * (-(-experts // 16)), rows), 0)
    onehot = jnp.where(known == route, 1.0, 0.0)
    upto = lax.broadcasted_iota(jnp.int32, (rows, rows), 0) <= lax.broadcasted_iota(
        jnp.int32, (rows, rows), 1
    )
    counts = dot(onehot.astype(jnp.bfloat16), jnp.where(upto, 1.0, 0.0).astype(jnp.bfloat16))
    position = jnp.sum(onehot * counts, axis=0, keepdims=True).astype(jnp.int32) - 1
    slot = (route ^ plane) * capacity + position
    slots = lax.broadcasted_iota(jnp.int32, (experts * capacity, rows), 0)
    return jnp.where(slots == slot, 1.0, 0.0).astype(jnp.bfloat16)


def pack_kernel(experts, capacity, feat, *refs):
    plane, _, column = place()
    values, routes, refs = refs[:2], refs[2:4], refs[4:]
    moved, refs = refs[: 2 * (experts - 1)], refs[2 * (experts - 1) :]
    slices, blocks, sems = refs[:2], refs[2:4], refs[4]
    cols = pl.ds(pl.multiple_of(column * feat, feat), feat)
    copies = [
        pltpu.make_async_copy(routes[0], blocks[0], sems.at[0]),
        pltpu.make_async_copy(routes[1], blocks[1], sems.at[1]),
        pltpu.make_async_copy(values[0].at[:, cols], slices[0], sems.at[2]),
        pltpu.make_async_copy(values[1].at[:, cols], slices[1], sems.at[3]),
    ]
    for copy in copies:
        copy.start()
    for i in range(2):
        copies[i].wait()
    places = [placing(block[...], experts, capacity, plane) for block in blocks]
    for i in range(2):
        copies[2 + i].wait()
    for i in range(2):
        sent = dot(places[i][capacity:], slices[i][...]).astype(jnp.bfloat16)
        for out, s in zip(moved[i * (experts - 1) :], plane_order(experts, i)[:-1]):
            out[...] = sent[(s - 1) * capacity : s * capacity]


def stay_kernel(experts, capacity, values, route, stay):
    plane, _, _ = place()
    place_rows = placing(route[...], experts, capacity, plane)
    stay[...] = dot(place_rows[:capacity], values[...]).astype(jnp.bfloat16)


def map_kernel(experts, capacity, routes, other_routes, out):
    plane, core, _ = place()
    for c in range(2):
        block = jnp.where(core == c, routes[...], other_routes[...])
        source = placing(block[0:1], experts, capacity, plane)
        target = placing(block[1:2], experts, capacity, plane)
        out[c] = dot_nt(target, source).astype(jnp.bfloat16)


def load_kernel(*refs):
    count = len(refs) // 2
    copies = [
        pltpu.make_async_copy(refs[i], refs[count + i], refs[-1].at[i]) for i in range(count)
    ]
    for copy in copies:
        copy.start()
    for copy in copies:
        copy.wait()


def stack_kernel(near_first, *refs):
    moved, out = refs[:-1], refs[-1]
    capacity = moved[0].shape[0]
    for ref, s in zip(moved, plane_order(len(moved) + 1, near_first)):
        out[(s - 1) * capacity : s * capacity, :] = ref[...]


def join_kernel(columns, stay, *refs):
    _, _, column = place()
    parts, flat = refs[:-1], refs[-1]
    capacity = stay.shape[0]
    feat = parts[0].shape[1]
    flat[:capacity, :] = stay[...]
    for m in range(columns):
        cols = pl.ds(pl.multiple_of((column ^ m) * feat, feat), feat)
        flat[capacity:, cols] = parts[m][...]


def part_pieces(hidden, w2, which, columns, out):
    half = w2.shape[1] // 2
    piece = half // columns
    for j in range(columns):
        cols = pl.ds(pl.multiple_of(which * half + j * piece, piece), piece)
        out[j] = dot(hidden, w2[:, cols]).astype(jnp.bfloat16)


def forward_kernel(columns, count, *refs):
    _, core, _ = place()
    flats, refs = refs[:count], refs[count:]
    w1, w2, send, refs = refs[0], refs[1], refs[2], refs[3:]
    for i in range(count):
        pre = dot(flats[i][...], w1[...])
        if len(refs) > count:
            refs[count + i][...] = pre
        hidden = gelu_tanh(pre).astype(jnp.bfloat16)
        refs[i][...] = hidden
        part_pieces(hidden, w2, 1 - core, columns, send.at[i])


def keep_kernel(columns, hidden_own, hidden_other, w2, *refs):
    _, core, _ = place()
    if len(refs) > 2:
        pre_own, pre_other, flat_own, flat_other, keep_own, keep_other = refs[:6]
        flat_t, hidden_t, slope = refs[6:]
    else:
        keep_own, keep_other = refs
    part_pieces(hidden_own[...], w2, core, columns, keep_own)
    part_pieces(hidden_other[...], w2, core, columns, keep_other)
    if len(refs) > 2:
        half = flat_own.shape[0]
        slope[:half, :] = gelu_slope(pre_own[...])
        slope[half:, :] = gelu_slope(pre_other[...])
        hidden_t[...] = jnp.concatenate([hidden_own[...], hidden_other[...]], axis=0).T
        step = 512
        for j in range(0, flat_own.shape[1], step):
            here = slice(j, j + step)
            both = jnp.concatenate([flat_own[:, here], flat_other[:, here]], axis=0)
            flat_t[here, :] = both.T


def pair_kernel(columns, keep_own, keep_other, *refs):
    _, core, column = place()
    half = keep_own.shape[1]
    got, (mine, *out) = refs[:-columns], refs[-columns:]
    got = [ref for ref in got if ref.dtype != jnp.int32]
    got_own, got_other = got[0].at[0], got[-1].at[len(got) % 2]
    for m in range(columns):
        for which, keep, got in ((core, keep_own, got_other), (1 - core, keep_other, got_own)):
            rows = pl.ds(pl.multiple_of(which * half, 16), half)
            both = keep[column ^ m].astype(jnp.float32) + got[column ^ m].astype(jnp.float32)
            if m:
                out[-m][rows, :] = both.astype(jnp.bfloat16)
            else:
                mine[rows, :] = both


def total_kernel(columns, experts, *refs):
    sums, out = refs[:columns], refs[columns:]
    total = sums[0][...]
    for ref in sums[1:]:
        total = total + ref[...].astype(jnp.float32)
    total = total.astype(jnp.bfloat16)
    capacity = out[0].shape[0] // 2
    for ref, s in zip(out, plane_order(experts)):
        for c in range(2):
            start = (c * experts + s) * capacity
            ref[c * capacity : (c + 1) * capacity, :] = total[start : start + capacity]


def home_kernel(experts, capacity, maps, *refs):
    got, out = refs[:experts], refs[experts:]
    for c in range(2):
        here = slice(c * capacity, (c + 1) * capacity)
        by_plane = dict(zip(plane_order(experts), got))
        rows = jnp.concatenate([by_plane[s][here, :] for s in range(experts)], axis=0)
        by_slot = dot(maps[c], rows).astype(jnp.bfloat16)
        for ref, s in zip(out, plane_order(experts)):
            ref[here, :] = by_slot[s * capacity : (s + 1) * capacity]


def upstream_kernel(columns, experts, loss_scale, *refs):
    sums, teacher, out = refs[:columns], refs[columns:-1], refs[-1]
    total = sums[0][...]
    for ref in sums[1:]:
        total = total + ref[...].astype(jnp.float32)
    capacity = teacher[0].shape[0] // 2
    teacher = dict(zip(plane_order(experts), teacher))
    rows = jnp.concatenate(
        [
            teacher[s][c * capacity : (c + 1) * capacity, :]
            for c in range(2)
            for s in range(experts)
        ],
        axis=0,
    ).astype(jnp.float32)
    out[...] = ((total - rows) * loss_scale).astype(jnp.bfloat16)


def piece_columns(which, width, piece):
    _, core, column = place()
    other, m = which
    start = (1 - core if other else core) * (width // 2) + (column ^ m) * piece
    return pl.ds(pl.multiple_of(start, piece), piece)


def use_piece(ref, cols, hidden_t, w2, hidden_grad):
    _, core, _ = place()
    half = ref.shape[0] // 2
    rows = jnp.concatenate(
        [ref[pl.ds(pl.multiple_of(block * half, 16), half), :] for block in (core, 1 - core)],
        axis=0,
    )
    term = dot_nt(rows, w2[:, cols])
    hidden_grad = term if hidden_grad is None else hidden_grad + term
    return hidden_grad, rows


def early_kernel(places, first, *refs):
    count = len(places)
    pieces, (hidden_t, w2), refs = refs[:count], refs[count : count + 2], refs[count + 2 :]
    hidden_grad = None if first else refs[0][...]
    sum_out, *grads = refs if first else refs[1:]
    piece, width = pieces[0].shape[1], w2.shape[1]
    for ref, which, out in zip(pieces, places, grads):
        cols = piece_columns(which, width, piece)
        hidden_grad, rows = use_piece(ref, cols, hidden_t, w2, hidden_grad)
        out[...] = dot(hidden_t[...], rows).astype(jnp.bfloat16)
    sum_out[...] = hidden_grad


def last_kernel(places, early, *refs):
    count = len(places)
    pieces, refs = refs[:count], refs[count:]
    done, refs = refs[: len(early)], refs[len(early) :]
    hidden_t, w2, sum_in, flat_t, slope, grad_first, grad_second, held_first, held_second, sems = refs
    piece, width = pieces[0].shape[1], w2.shape[1]
    copies = []

    def leave(source, target):
        copies.append(pltpu.make_async_copy(source, target, sems.at[len(copies)]))
        copies[-1].start()

    for ref, which in zip(done, early):
        leave(ref, grad_second.at[:, piece_columns(which, width, piece)])
    hidden_grad = sum_in[...]
    used = []
    for ref, which in zip(pieces, places):
        cols = piece_columns(which, width, piece)
        hidden_grad, rows = use_piece(ref, cols, hidden_t, w2, hidden_grad)
        used.append((cols, rows))
    pre_grad = (hidden_grad * slope[...]).astype(jnp.bfloat16)
    step = 512
    for j in range(width // step):
        here = slice(j * step, (j + 1) * step)
        held_first[here, :] = dot(flat_t[here, :], pre_grad).astype(jnp.bfloat16)
        leave(held_first.at[here, :], grad_first.at[here, :])
    for i, (cols, rows) in enumerate(used):
        held_second[i] = dot(hidden_t[...], rows).astype(jnp.bfloat16)
        leave(held_second.at[i], grad_second.at[:, cols])
    for copy in copies:
        copy.wait()


def by_kernels(
    teacher_in,
    student_in,
    teacher_route,
    student_route,
    teacher_w1,
    teacher_w2,
    student_w1,
    student_w2,
):
    groups, columns, experts, row_count, width, capacity = sizes(teacher_in)
    plane_rows = groups * capacity
    loss_scale = 1.0 / math.sqrt(row_count)
    feat = width // columns
    piece = feat // 2
    hid = teacher_w1.shape[2]
    f32 = jnp.float32

    def after(value, *others):
        return lax.optimization_barrier((value, others))[0]

    def over_planes(sent, near_first=False):
        return [
            partner(value, "dp", s << 1) for value, s in zip(sent, plane_order(experts, near_first))
        ]

    def spread(mine):
        return [mine] + [partner(mine, "expert", m) for m in range(1, columns)]

    def across(value):
        return partner(value, "dp", 1)

    def load(*weights):
        return call(
            load_kernel,
            [shape(*w.shape) for w in weights],
            weights,
            in_specs=[ANY] * len(weights),
            name="load",
            scratch=[pltpu.SemaphoreType.DMA((len(weights),))],
        )

    def forward(flats, w1, w2, keep_pre, name, units=0):
        half, count = plane_rows // 2, len(flats)
        pre = [shape(half, hid, dtype=f32)] * count if keep_pre else []
        return call(
            lambda *refs: forward_kernel(columns, count, *refs),
            [shape(count, columns, half, piece)] + [shape(half, hid)] * count + pre,
            [*flats, w1, w2],
            flops=units * plane_rows * width * hid,
            name=name,
        )

    def keep(own, other, w2, state, outs):
        return call(
            lambda *refs: keep_kernel(columns, *refs),
            [shape(columns, plane_rows // 2, piece)] * 2 + outs,
            [own, other, w2, *state],
            flops=(64 if state else 0) * plane_rows * width * hid,
            name="keep_s" if state else "keep_t",
        )

    def pair(kept, got, marks=()):
        return call(
            lambda *refs: pair_kernel(columns, *refs),
            [shape(plane_rows, piece, dtype=f32)] + [shape(plane_rows, piece)] * (columns - 1),
            [*kept, *marks, *got],
            name="pair",
        )

    def collect(mine, *out):
        return [mine] + [
            partner(value, "expert", columns - 1 - i) for i, value in enumerate(out)
        ]

    route_t = teacher_route.reshape(1, row_count)
    route_s = student_route.reshape(1, row_count)
    def stay(values, route):
        return call(
            lambda *refs: stay_kernel(experts, capacity, *refs),
            [shape(capacity, width)],
            [values, route],
            name="stay",
        )[0]

    sent = call(
        lambda *refs: pack_kernel(experts, capacity, feat, *refs),
        [shape(capacity, feat)] * (2 * (experts - 1)),
        [teacher_in, student_in, route_t, route_s],
        in_specs=[ANY] * 4,
        grant=(253 << 20) // 4,
        name="pack",
        scratch=[pltpu.VMEM((row_count, feat), jnp.bfloat16)] * 2
        + [pltpu.VMEM((1, row_count), jnp.int32)] * 2
        + [pltpu.SemaphoreType.DMA((4,))],
    )
    stay_s = stay(student_in, route_s)
    routes = jnp.concatenate([route_t, route_s], axis=0)
    other_routes = across(routes)
    def stack(moved, near_first, units=0):
        return call(
            lambda *refs: stack_kernel(near_first, *refs),
            [shape((experts - 1) * capacity, feat)],
            moved,
            flops=units * plane_rows * width * hid,
            name="stack",
        )[0]

    sent_t, sent_s = sent[: experts - 1], sent[experts - 1 :]
    moved_t = over_planes(sent_t)
    moved_s = over_planes(sent_s, True)
    mine_t, mine_s = stack(moved_t, False, 0), stack(moved_s, True, 8)
    w1_t, w2_t = load(*after((teacher_w1[0], teacher_w2[0]), mine_s))
    stay_t = stay(after(teacher_in, mine_s), route_t)
    got_t, got_s = spread(mine_t), spread(mine_s)
    w1_s, w2_s = load(student_w1[0], student_w2[0])
    (maps,) = call(
        lambda *refs: map_kernel(experts, capacity, *refs),
        [shape(2, experts * capacity, experts * capacity)],
        [routes, other_routes],
        name="maps",
    )

    def join(rows, got):
        return call(
            lambda *refs: join_kernel(columns, *refs),
            [shape(plane_rows // 2, width)],
            [rows, *got],
            name="join",
        )[0]

    flat_t_own = join(stay_t, after(got_t, w1_t))
    flat_t_other = across(flat_t_own)

    send, hidden_own = forward([flat_t_own], w1_t, w2_t, False, "forward_t", 24)
    got_own = across(send)
    send, hidden_other = forward([flat_t_other], w1_t, w2_t, False, "forward_t", 0)
    got_other = across(send)
    kept = keep(hidden_own, hidden_other, w2_t, [], [])
    (mark,) = call(
        lambda source, out: out.__setitem__(Ellipsis, source[...]),
        [shape(1, row_count, dtype=jnp.int32)],
        [after(route_t, got_s, w1_s, stay_s, kept[0])],
        flops=8 * plane_rows * width * hid,
        name="mark",
    )
    pieces_t = pair(kept, [got_own, got_other], [mark])
    sums_t = collect(*pieces_t)

    flat_own = join(stay_s, after(got_s, pieces_t[0]))
    flat_other = across(flat_own)
    send, hidden_own, hidden_other, pre_own, pre_other = forward(
        [flat_own, flat_other], w1_s, w2_s, True, "forward_s"
    )
    got = [across(send)]
    *kept, flat_t, hidden_t, slope = keep(
        hidden_own,
        hidden_other,
        w2_s,
        [pre_own, pre_other, flat_own, flat_other],
        [shape(width, plane_rows), shape(hid, plane_rows), shape(plane_rows, hid, dtype=f32)],
    )

    pieces_s = pair(kept, got)
    sums_s = collect(*pieces_s)

    home = call(
        lambda *refs: total_kernel(columns, experts, *refs),
        [shape(2 * capacity, piece)] * experts,
        after(sums_t, pieces_s[0], maps),
    )
    *sent, near, own = home
    home = [*over_planes([*sent, after(near, sums_s[1])]), own]
    slots = call(
        lambda *refs: home_kernel(experts, capacity, *refs),
        [shape(2 * capacity, piece)] * experts,
        [maps, *home],
        flops=4 * plane_rows * width * hid,
        name="home",
    )
    teachers = [*over_planes(slots[:-1]), slots[-1]]
    (upstream,) = call(
        lambda *refs: upstream_kernel(columns, experts, loss_scale, *refs),
        [shape(plane_rows, piece)],
        [*sums_s, *teachers],
    )
    early = {}

    def backward(pieces, total):
        first = total is None
        places = tuple(pieces)
        total, *done = call(
            lambda *refs: early_kernel(places, first, *refs),
            [shape(plane_rows, hid, dtype=f32)] + [shape(hid, piece)] * len(places),
            [*pieces.values(), hidden_t, w2_s] + ([] if first else [total]),
            name="early",
        )
        early.update(zip(places, done))
        return total

    def finish(pieces, total):
        places, kept_places = tuple(pieces), tuple(early)
        return call(
            lambda *refs: last_kernel(places, kept_places, *refs),
            [shape(width, hid), shape(hid, width)],
            [*pieces.values(), *early.values(), hidden_t, w2_s, total, flat_t, slope],
            out_specs=[ANY, ANY],
            scratch=[
                pltpu.VMEM((width, hid), jnp.bfloat16),
                pltpu.VMEM((len(places), hid, piece), jnp.bfloat16),
                pltpu.SemaphoreType.DMA((len(places) + len(early) + width // 512,)),
            ],
            name="last",
        )

    grads = spread(upstream)
    total = backward({(0, 0): upstream, (1, 0): across(upstream)}, None)
    far = after(grads[3], total)
    total = backward({(0, 3): far}, total)
    near = after(grads[1:3], total)
    other_far = across(far)
    others = [across(value) for value in near]
    total = backward({(0, 1): near[0], (0, 2): near[1], (1, 3): other_far}, total)
    grad_first, grad_second = finish({(1, 1): others[0], (1, 2): others[1]}, total)
    return (grad_first[None], grad_second[None])

def on_device(*arrays):
    _, columns, _, row_count, width, capacity = sizes(arrays[0])
    aligned = columns == 4 and capacity % 16 == 0 and row_count % 128 == 0 and width % (256 * columns) == 0
    return by_kernels(*arrays) if aligned else by_ops(*arrays)


def solution(mesh):
    return jax.shard_map(
        on_device,
        mesh=mesh,
        in_specs=(
            P("dp", None),
            P("dp", None),
            P("dp", None),
            P("dp", None),
            P("dp", None, "expert"),
            P("dp", "expert", None),
            P("dp", None, "expert"),
            P("dp", "expert", None),
        ),
        out_specs=(P("dp", None, "expert"), P("dp", "expert", None)),
        check_vma=False,
    )
```

```python
import math

import jax
import jax.numpy as jnp
from jax import lax
from jax.experimental import pallas as pl
from jax.experimental.pallas import tpu as pltpu
from jax.sharding import PartitionSpec as P

root_coef = math.sqrt(2.0 / math.pi)
cubic_coef = 0.044715


def partner(value, axis, mask):
    return lax.ppermute(value, axis, [(i, i ^ mask) for i in range(lax.axis_size(axis))])


def gelu_tanh(pre_act):
    inner_arg = root_coef * (pre_act + cubic_coef * pre_act * pre_act * pre_act)
    return 0.5 * pre_act * (1.0 + jnp.tanh(inner_arg))


def gelu_slope(pre_act):
    tangent = jnp.tanh(root_coef * (pre_act + cubic_coef * pre_act * pre_act * pre_act))
    return 0.5 * (1.0 + tangent) + 0.5 * pre_act * (1.0 - tangent * tangent) * root_coef * (
        1.0 + 3.0 * cubic_coef * pre_act * pre_act
    )


def dot(left, right):
    return jnp.dot(left, right, preferred_element_type=jnp.float32)


def ranks(routes, experts):
    onehot = (routes[..., None] == jnp.arange(experts, dtype=jnp.int32)).astype(jnp.int32)
    rank_table = jnp.cumsum(onehot, axis=1) - 1
    return jnp.sum(onehot * rank_table, axis=2)


def sizes(rows):
    groups = lax.axis_size("dp")
    experts = groups // 2
    row_count, width = rows.shape
    capacity = 2 * max(1, 3 * row_count // (4 * experts))
    return groups, lax.axis_size("expert"), experts, row_count, width, capacity


def by_ops(
    teacher_in,
    student_in,
    teacher_route,
    student_route,
    teacher_w1,
    teacher_w2,
    student_w1,
    student_w2,
):
    groups, columns, experts, row_count, width, capacity = sizes(teacher_in)
    plane_rows = groups * capacity
    dp = lax.axis_index("dp")
    column = lax.axis_index("expert")
    plane, core = dp // 2, dp % 2
    loss_scale = 1.0 / math.sqrt(row_count)
    feat = width // columns
    piece = feat // 2

    def dispatch(values, routes):
        position = ranks(routes[:, 0][None], experts)[0]
        slot = (routes[:, 0] ^ plane) * capacity + position
        placing = (
            jnp.arange(experts * capacity, dtype=jnp.int32)[:, None] == slot[None, :]
        ).astype(jnp.bfloat16)
        own_slice = lax.dynamic_slice(values, (0, column * feat), (row_count, feat))
        slots = dot(placing[capacity:], own_slice).astype(jnp.bfloat16)
        stay = dot(placing[:capacity], values).astype(jnp.bfloat16)
        moved = [
            partner(slots[(s - 1) * capacity : s * capacity], "dp", s << 1)
            for s in range(1, experts)
        ]
        mine = jnp.concatenate(moved, axis=0)
        buffer = jnp.concatenate([stay, jnp.zeros((mine.shape[0], width), jnp.bfloat16)], axis=0)
        for m in range(columns):
            got = partner(mine, "expert", m) if m else mine
            buffer = lax.dynamic_update_slice(buffer, got, (capacity, (column ^ m) * feat))
        other = partner(buffer, "dp", 1)
        first = jnp.where(core == 0, buffer, other)
        second = jnp.where(core == 0, other, buffer)
        return jnp.concatenate([first, second], axis=0)

    def forward(flat, w1, w2):
        pre = dot(flat, w1)
        hidden = gelu_tanh(pre).astype(jnp.bfloat16)
        part = dot(hidden, w2).astype(jnp.bfloat16).reshape(plane_rows, 2, columns, piece)
        part = part.transpose(1, 2, 0, 3)
        return pre, hidden, part

    def plane_sum(part):
        keep = lax.dynamic_index_in_dim(part, core, 0, keepdims=False)
        send = lax.dynamic_index_in_dim(part, 1 - core, 0, keepdims=False)
        pair = (
            keep.astype(jnp.float32) + partner(send, "dp", 1).astype(jnp.float32)
        ).astype(jnp.bfloat16)
        total = lax.dynamic_index_in_dim(pair, column, 0, keepdims=False).astype(jnp.float32)
        for m in range(1, columns):
            out = lax.dynamic_index_in_dim(pair, column ^ m, 0, keepdims=False)
            total = total + partner(out, "expert", m).astype(jnp.float32)
        return total

    routes = jnp.concatenate([teacher_route, student_route], axis=1)
    table = lax.all_gather(routes, "dp", axis=0, tiled=True).reshape(groups, row_count, 2)
    teacher_all, student_all = table[:, :, 0], table[:, :, 1]
    block = jnp.arange(groups, dtype=jnp.int32)[:, None]
    block_plane, block_core = block // 2, block % 2
    teacher_row = (
        (teacher_all ^ plane) * plane_rows
        + (block_core * experts + (block_plane ^ teacher_all)) * capacity
        + ranks(teacher_all, experts)
    )
    student_row = jnp.where(student_all == plane, ranks(student_all, experts), -1)
    hits = jnp.arange(capacity, dtype=jnp.int32)[None, :, None] == student_row[:, None, :]
    source = jnp.sum(jnp.where(hits, teacher_row[:, None, :] + 1, 0), axis=2) - 1
    source = source.reshape(experts, 2, capacity)
    source = source[jnp.arange(experts, dtype=jnp.int32) ^ plane].transpose(1, 0, 2)
    source = source.reshape(plane_rows)

    teacher_flat = dispatch(teacher_in, teacher_route)
    student_flat = dispatch(student_in, student_route)
    _, _, teacher_part = forward(teacher_flat, teacher_w1[0], teacher_w2[0])
    teacher_sum = plane_sum(teacher_part).astype(jnp.bfloat16)
    teacher_sums = jnp.concatenate(
        [teacher_sum] + [partner(teacher_sum, "dp", s << 1) for s in range(1, experts)], axis=0
    )
    student_pre, student_hidden, student_part = forward(
        student_flat, student_w1[0], student_w2[0]
    )
    pick = (
        source[:, None] == jnp.arange(experts * plane_rows, dtype=jnp.int32)[None, :]
    ).astype(jnp.bfloat16)
    teacher_rows = dot(pick, teacher_sums)
    student_sum = plane_sum(student_part)
    upstream = ((student_sum - teacher_rows) * loss_scale).astype(jnp.bfloat16)

    half = jnp.zeros((plane_rows, width // 2), jnp.bfloat16)
    for m in range(columns):
        got = partner(upstream, "expert", m) if m else upstream
        half = lax.dynamic_update_slice(half, got, (0, (column ^ m) * piece))
    other_half = partner(half, "dp", 1)
    grad_flat = jnp.concatenate(
        [jnp.where(core == 0, half, other_half), jnp.where(core == 0, other_half, half)], axis=1
    )
    hidden_grad = dot(grad_flat, student_w2[0].T)
    pre_grad = (hidden_grad * gelu_slope(student_pre)).astype(jnp.bfloat16)
    grad_second = dot(student_hidden.T, grad_flat).astype(jnp.bfloat16)
    grad_first = dot(student_flat.T, pre_grad).astype(jnp.bfloat16)
    return (grad_first[None], grad_second[None])


def plane_order(experts, near_first=False):
    return (*range(1, experts), 0) if near_first else (*range(2, experts), 1, 0)


def place():
    dp = lax.axis_index("dp")
    return dp // 2, dp % 2, lax.axis_index("expert")


VMEM = pl.BlockSpec(memory_space=pltpu.VMEM)
ANY = pl.BlockSpec(memory_space=pl.ANY)


def call(kernel, outs, operands, out_specs=None, in_specs=None, scratch=(), grant=20 << 20, flops=0, name=None):
    return pl.pallas_call(
        kernel,
        name=name,
        out_shape=outs,
        in_specs=in_specs or [VMEM] * len(operands),
        out_specs=out_specs or [VMEM] * len(outs),
        scratch_shapes=list(scratch),
        compiler_params=pltpu.CompilerParams(vmem_limit_bytes=grant),
        cost_estimate=pl.CostEstimate(flops=flops, bytes_accessed=0, transcendentals=0),
    )(*operands)


def shape(*dims, dtype=jnp.bfloat16):
    return jax.ShapeDtypeStruct(dims, dtype)


def dot_tn(left, right):
    return lax.dot_general(
        left, right, (((0,), (0,)), ((), ())), preferred_element_type=jnp.float32
    )


def dot_nt(left, right):
    return lax.dot_general(
        left, right, (((1,), (1,)), ((), ())), preferred_element_type=jnp.float32
    )


def placing(route, experts, capacity, plane):
    rows = route.shape[1]
    known = lax.broadcasted_iota(jnp.int32, (16 * (-(-experts // 16)), rows), 0)
    onehot = jnp.where(known == route, 1.0, 0.0)
    upto = lax.broadcasted_iota(jnp.int32, (rows, rows), 0) <= lax.broadcasted_iota(
        jnp.int32, (rows, rows), 1
    )
    counts = dot(onehot.astype(jnp.bfloat16), jnp.where(upto, 1.0, 0.0).astype(jnp.bfloat16))
    position = jnp.sum(onehot * counts, axis=0, keepdims=True).astype(jnp.int32) - 1
    slot = (route ^ plane) * capacity + position
    slots = lax.broadcasted_iota(jnp.int32, (experts * capacity, rows), 0)
    return jnp.where(slots == slot, 1.0, 0.0).astype(jnp.bfloat16)


def pack_kernel(experts, capacity, feat, *refs):
    plane, _, column = place()
    values, routes, refs = refs[:2], refs[2:4], refs[4:]
    moved, refs = refs[: 2 * (experts - 1)], refs[2 * (experts - 1) :]
    slices, blocks, sems = refs[:2], refs[2:4], refs[4]
    cols = pl.ds(pl.multiple_of(column * feat, feat), feat)
    copies = [
        pltpu.make_async_copy(routes[0], blocks[0], sems.at[0]),
        pltpu.make_async_copy(routes[1], blocks[1], sems.at[1]),
        pltpu.make_async_copy(values[0].at[:, cols], slices[0], sems.at[2]),
        pltpu.make_async_copy(values[1].at[:, cols], slices[1], sems.at[3]),
    ]
    for copy in copies:
        copy.start()
    for i in range(2):
        copies[i].wait()
    places = [placing(block[...], experts, capacity, plane) for block in blocks]
    for i in range(2):
        copies[2 + i].wait()
    for i in range(2):
        sent = dot(places[i][capacity:], slices[i][...]).astype(jnp.bfloat16)
        for out, s in zip(moved[i * (experts - 1) :], plane_order(experts, i)[:-1]):
            out[...] = sent[(s - 1) * capacity : s * capacity]


def stay_kernel(experts, capacity, values, route, stay):
    plane, _, _ = place()
    place_rows = placing(route[...], experts, capacity, plane)
    stay[...] = dot(place_rows[:capacity], values[...]).astype(jnp.bfloat16)


def map_kernel(experts, capacity, routes, other_routes, out):
    plane, core, _ = place()
    for c in range(2):
        block = jnp.where(core == c, routes[...], other_routes[...])
        source = placing(block[0:1], experts, capacity, plane)
        target = placing(block[1:2], experts, capacity, plane)
        out[c] = dot_nt(target, source).astype(jnp.bfloat16)


def load_kernel(*refs):
    count = len(refs) // 2
    copies = [
        pltpu.make_async_copy(refs[i], refs[count + i], refs[-1].at[i]) for i in range(count)
    ]
    for copy in copies:
        copy.start()
    for copy in copies:
        copy.wait()


def stack_kernel(near_first, *refs):
    moved, out = refs[:-1], refs[-1]
    capacity = moved[0].shape[0]
    for ref, s in zip(moved, plane_order(len(moved) + 1, near_first)):
        out[(s - 1) * capacity : s * capacity, :] = ref[...]


def join_kernel(columns, stay, *refs):
    _, _, column = place()
    parts, flat = refs[:-1], refs[-1]
    capacity = stay.shape[0]
    feat = parts[0].shape[1]
    flat[:capacity, :] = stay[...]
    for m in range(columns):
        cols = pl.ds(pl.multiple_of((column ^ m) * feat, feat), feat)
        flat[capacity:, cols] = parts[-m if m else 0][...]


def part_pieces(hidden, w2, which, columns, out):
    half = w2.shape[1] // 2
    piece = half // columns
    for j in range(columns):
        cols = pl.ds(pl.multiple_of(which * half + j * piece, piece), piece)
        out[j] = dot(hidden, w2[:, cols]).astype(jnp.bfloat16)


def forward_kernel(columns, count, *refs):
    _, core, _ = place()
    flats, refs = refs[:count], refs[count:]
    w1, w2, send, refs = refs[0], refs[1], refs[2], refs[3:]
    for i in range(count):
        pre = dot(flats[i][...], w1[...])
        if len(refs) > count:
            refs[count + i][...] = pre
        hidden = gelu_tanh(pre).astype(jnp.bfloat16)
        refs[i][...] = hidden
        part_pieces(hidden, w2, 1 - core, columns, send.at[i])


def keep_kernel(columns, hidden_own, hidden_other, w2, *refs):
    _, core, _ = place()
    if len(refs) > 2:
        pre_own, pre_other, flat_own, flat_other, keep_own, keep_other = refs[:6]
        flat_t, hidden_t, slope = refs[6:]
    else:
        keep_own, keep_other = refs
    part_pieces(hidden_own[...], w2, core, columns, keep_own)
    part_pieces(hidden_other[...], w2, core, columns, keep_other)
    if len(refs) > 2:
        half = flat_own.shape[0]
        slope[:half, :] = gelu_slope(pre_own[...])
        slope[half:, :] = gelu_slope(pre_other[...])
        hidden_t[...] = jnp.concatenate([hidden_own[...], hidden_other[...]], axis=0).T
        step = 512
        for j in range(0, flat_own.shape[1], step):
            here = slice(j, j + step)
            both = jnp.concatenate([flat_own[:, here], flat_other[:, here]], axis=0)
            flat_t[here, :] = both.T


def pair_kernel(columns, keep_own, keep_other, *refs):
    _, core, column = place()
    half = keep_own.shape[1]
    got, (mine, *out) = refs[:-columns], refs[-columns:]
    got = [ref for ref in got if ref.dtype != jnp.int32]
    got_own, got_other = got[0].at[0], got[-1].at[len(got) % 2]
    for m in range(columns):
        for which, keep, got in ((core, keep_own, got_other), (1 - core, keep_other, got_own)):
            rows = pl.ds(pl.multiple_of(which * half, 16), half)
            both = keep[column ^ m].astype(jnp.float32) + got[column ^ m].astype(jnp.float32)
            if m:
                out[-m][rows, :] = both.astype(jnp.bfloat16)
            else:
                mine[rows, :] = both


def total_kernel(columns, experts, *refs):
    sums, out = refs[:columns], refs[columns:]
    total = sums[0][...]
    for ref in sums[1:]:
        total = total + ref[...].astype(jnp.float32)
    total = total.astype(jnp.bfloat16)
    capacity = out[0].shape[0] // 2
    for ref, s in zip(out, plane_order(experts)):
        for c in range(2):
            start = (c * experts + s) * capacity
            ref[c * capacity : (c + 1) * capacity, :] = total[start : start + capacity]


def home_kernel(experts, capacity, maps, *refs):
    got, out = refs[:experts], refs[experts:]
    for c in range(2):
        here = slice(c * capacity, (c + 1) * capacity)
        by_plane = dict(zip(plane_order(experts), got))
        rows = jnp.concatenate([by_plane[s][here, :] for s in range(experts)], axis=0)
        by_slot = dot(maps[c], rows).astype(jnp.bfloat16)
        for ref, s in zip(out, plane_order(experts)):
            ref[here, :] = by_slot[s * capacity : (s + 1) * capacity]


def upstream_kernel(columns, experts, loss_scale, *refs):
    sums, teacher, out = refs[:columns], refs[columns:-1], refs[-1]
    total = sums[0][...]
    for ref in sums[1:]:
        total = total + ref[...].astype(jnp.float32)
    capacity = teacher[0].shape[0] // 2
    teacher = dict(zip(plane_order(experts), teacher))
    rows = jnp.concatenate(
        [
            teacher[s][c * capacity : (c + 1) * capacity, :]
            for c in range(2)
            for s in range(experts)
        ],
        axis=0,
    ).astype(jnp.float32)
    out[...] = ((total - rows) * loss_scale).astype(jnp.bfloat16)


def piece_columns(which, width, piece):
    _, core, column = place()
    other, m = which
    start = (1 - core if other else core) * (width // 2) + (column ^ m) * piece
    return pl.ds(pl.multiple_of(start, piece), piece)


def use_piece(ref, cols, hidden_t, w2, hidden_grad):
    _, core, _ = place()
    half = ref.shape[0] // 2
    rows = jnp.concatenate(
        [ref[pl.ds(pl.multiple_of(block * half, 16), half), :] for block in (core, 1 - core)],
        axis=0,
    )
    term = dot_nt(rows, w2[:, cols])
    hidden_grad = term if hidden_grad is None else hidden_grad + term
    return hidden_grad, rows


def early_kernel(places, first, *refs):
    count = len(places)
    pieces, (hidden_t, w2), refs = refs[:count], refs[count : count + 2], refs[count + 2 :]
    hidden_grad = None if first else refs[0][...]
    sum_out, *grads = refs if first else refs[1:]
    piece, width = pieces[0].shape[1], w2.shape[1]
    for ref, which, out in zip(pieces, places, grads):
        cols = piece_columns(which, width, piece)
        hidden_grad, rows = use_piece(ref, cols, hidden_t, w2, hidden_grad)
        out[...] = dot(hidden_t[...], rows).astype(jnp.bfloat16)
    sum_out[...] = hidden_grad


def last_kernel(places, early, *refs):
    count = len(places)
    pieces, refs = refs[:count], refs[count:]
    done, refs = refs[: len(early)], refs[len(early) :]
    hidden_t, w2, sum_in, flat_t, slope, grad_first, grad_second, held_first, held_second, sems = refs
    piece, width = pieces[0].shape[1], w2.shape[1]
    copies = []

    def leave(source, target):
        copies.append(pltpu.make_async_copy(source, target, sems.at[len(copies)]))
        copies[-1].start()

    for ref, which in zip(done, early):
        leave(ref, grad_second.at[:, piece_columns(which, width, piece)])
    hidden_grad = sum_in[...]
    used = []
    for ref, which in zip(pieces, places):
        cols = piece_columns(which, width, piece)
        hidden_grad, rows = use_piece(ref, cols, hidden_t, w2, hidden_grad)
        used.append((cols, rows))
    pre_grad = (hidden_grad * slope[...]).astype(jnp.bfloat16)
    step = 512
    for j in range(width // step):
        here = slice(j * step, (j + 1) * step)
        held_first[here, :] = dot(flat_t[here, :], pre_grad).astype(jnp.bfloat16)
        leave(held_first.at[here, :], grad_first.at[here, :])
    for i, (cols, rows) in enumerate(used):
        held_second[i] = dot(hidden_t[...], rows).astype(jnp.bfloat16)
        leave(held_second.at[i], grad_second.at[:, cols])
    for copy in copies:
        copy.wait()


def by_kernels(
    teacher_in,
    student_in,
    teacher_route,
    student_route,
    teacher_w1,
    teacher_w2,
    student_w1,
    student_w2,
):
    groups, columns, experts, row_count, width, capacity = sizes(teacher_in)
    plane_rows = groups * capacity
    loss_scale = 1.0 / math.sqrt(row_count)
    feat = width // columns
    piece = feat // 2
    hid = teacher_w1.shape[2]
    f32 = jnp.float32

    def after(value, *others):
        return lax.optimization_barrier((value, others))[0]

    def over_planes(sent, near_first=False):
        return [
            partner(value, "dp", s << 1) for value, s in zip(sent, plane_order(experts, near_first))
        ]

    def spread(mine):
        return [mine] + [partner(mine, "expert", m) for m in range(1, columns)]

    def across(value):
        return partner(value, "dp", 1)

    def load(*weights):
        return call(
            load_kernel,
            [shape(*w.shape) for w in weights],
            weights,
            in_specs=[ANY] * len(weights),
            name="load",
            scratch=[pltpu.SemaphoreType.DMA((len(weights),))],
        )

    def forward(flats, w1, w2, keep_pre, name, units=0):
        half, count = plane_rows // 2, len(flats)
        pre = [shape(half, hid, dtype=f32)] * count if keep_pre else []
        return call(
            lambda *refs: forward_kernel(columns, count, *refs),
            [shape(count, columns, half, piece)] + [shape(half, hid)] * count + pre,
            [*flats, w1, w2],
            flops=units * plane_rows * width * hid,
            name=name,
        )

    def keep(own, other, w2, state, outs):
        return call(
            lambda *refs: keep_kernel(columns, *refs),
            [shape(columns, plane_rows // 2, piece)] * 2 + outs,
            [own, other, w2, *state],
            flops=(64 if state else 0) * plane_rows * width * hid,
            name="keep_s" if state else "keep_t",
        )

    def pair(kept, got, marks=()):
        return call(
            lambda *refs: pair_kernel(columns, *refs),
            [shape(plane_rows, piece, dtype=f32)] + [shape(plane_rows, piece)] * (columns - 1),
            [*kept, *marks, *got],
            name="pair",
        )

    def collect(mine, *out):
        return [mine] + [
            partner(value, "expert", columns - 1 - i) for i, value in enumerate(out)
        ]

    route_t = teacher_route.reshape(1, row_count)
    route_s = student_route.reshape(1, row_count)
    def stay(values, route):
        return call(
            lambda *refs: stay_kernel(experts, capacity, *refs),
            [shape(capacity, width)],
            [values, route],
            name="stay",
        )[0]

    sent = call(
        lambda *refs: pack_kernel(experts, capacity, feat, *refs),
        [shape(capacity, feat)] * (2 * (experts - 1)),
        [teacher_in, student_in, route_t, route_s],
        in_specs=[ANY] * 4,
        grant=(253 << 20) // 4,
        name="pack",
        scratch=[pltpu.VMEM((row_count, feat), jnp.bfloat16)] * 2
        + [pltpu.VMEM((1, row_count), jnp.int32)] * 2
        + [pltpu.SemaphoreType.DMA((4,))],
    )
    stay_s = stay(student_in, route_s)
    routes = jnp.concatenate([route_t, route_s], axis=0)
    other_routes = across(routes)
    def stack(moved, near_first, units=0):
        return call(
            lambda *refs: stack_kernel(near_first, *refs),
            [shape((experts - 1) * capacity, feat)],
            moved,
            flops=units * plane_rows * width * hid,
            name="stack",
        )[0]

    sent_t, sent_s = sent[: experts - 1], sent[experts - 1 :]
    moved_t = over_planes(sent_t)
    moved_s = over_planes(sent_s, True)
    mine_t, mine_s = stack(moved_t, False, 0), stack(moved_s, True, 8)
    w1_t, w2_t = load(*after((teacher_w1[0], teacher_w2[0]), mine_s))
    stay_t = stay(after(teacher_in, mine_s), route_t)
    got_t, got_s = spread(mine_t), spread(mine_s)
    got_t, got_s = (got[:1] + got[:0:-1] for got in (got_t, got_s))
    w1_s, w2_s = load(student_w1[0], student_w2[0])
    (maps,) = call(
        lambda *refs: map_kernel(experts, capacity, *refs),
        [shape(2, experts * capacity, experts * capacity)],
        [routes, other_routes],
        name="maps",
    )

    def join(rows, got):
        return call(
            lambda *refs: join_kernel(columns, *refs),
            [shape(plane_rows // 2, width)],
            [rows, *got],
            name="join",
        )[0]

    flat_t_own = join(stay_t, after(got_t, w1_t))
    flat_t_other = across(flat_t_own)

    send, hidden_own = forward([flat_t_own], w1_t, w2_t, False, "forward_t", 24)
    got_own = across(send)
    send, hidden_other = forward([flat_t_other], w1_t, w2_t, False, "forward_t", 0)
    got_other = across(send)
    kept = keep(hidden_own, hidden_other, w2_t, [], [])
    (mark,) = call(
        lambda source, out: out.__setitem__(Ellipsis, source[...]),
        [shape(1, row_count, dtype=jnp.int32)],
        [after(route_t, got_s, w1_s, stay_s, kept[0])],
        flops=8 * plane_rows * width * hid,
        name="mark",
    )
    pieces_t = pair(kept, [got_own, got_other], [mark])
    sums_t = collect(*pieces_t)

    flat_own = join(stay_s, after(got_s, pieces_t[0]))
    flat_other = across(flat_own)
    send, hidden_own, hidden_other, pre_own, pre_other = forward(
        [flat_own, flat_other], w1_s, w2_s, True, "forward_s"
    )
    got = [across(send)]
    *kept, flat_t, hidden_t, slope = keep(
        hidden_own,
        hidden_other,
        w2_s,
        [pre_own, pre_other, flat_own, flat_other],
        [shape(width, plane_rows), shape(hid, plane_rows), shape(plane_rows, hid, dtype=f32)],
    )

    pieces_s = pair(kept, got)
    sums_s = collect(*pieces_s)

    home = call(
        lambda *refs: total_kernel(columns, experts, *refs),
        [shape(2 * capacity, piece)] * experts,
        after(sums_t, pieces_s[0], maps),
    )
    *sent, near, own = home
    home = [*over_planes([*sent, after(near, sums_s[1])]), own]
    slots = call(
        lambda *refs: home_kernel(experts, capacity, *refs),
        [shape(2 * capacity, piece)] * experts,
        [maps, *home],
        flops=4 * plane_rows * width * hid,
        name="home",
    )
    teachers = [*over_planes(slots[:-1]), slots[-1]]
    (upstream,) = call(
        lambda *refs: upstream_kernel(columns, experts, loss_scale, *refs),
        [shape(plane_rows, piece)],
        [*sums_s, *teachers],
    )
    early = {}

    def backward(pieces, total):
        first = total is None
        places = tuple(pieces)
        total, *done = call(
            lambda *refs: early_kernel(places, first, *refs),
            [shape(plane_rows, hid, dtype=f32)] + [shape(hid, piece)] * len(places),
            [*pieces.values(), hidden_t, w2_s] + ([] if first else [total]),
            name="early",
        )
        early.update(zip(places, done))
        return total

    def finish(pieces, total):
        places, kept_places = tuple(pieces), tuple(early)
        return call(
            lambda *refs: last_kernel(places, kept_places, *refs),
            [shape(width, hid), shape(hid, width)],
            [*pieces.values(), *early.values(), hidden_t, w2_s, total, flat_t, slope],
            out_specs=[ANY, ANY],
            scratch=[
                pltpu.VMEM((width, hid), jnp.bfloat16),
                pltpu.VMEM((len(places), hid, piece), jnp.bfloat16),
                pltpu.SemaphoreType.DMA((len(places) + len(early) + width // 512,)),
            ],
            name="last",
        )

    grads = spread(upstream)
    total = backward({(0, 0): upstream, (1, 0): across(upstream)}, None)
    far = after(grads[3], total)
    total = backward({(0, 3): far}, total)
    near = after(grads[1:3], total)
    other_far = across(far)
    others = [across(value) for value in near]
    total = backward({(0, 1): near[0], (0, 2): near[1], (1, 3): other_far}, total)
    grad_first, grad_second = finish({(1, 1): others[0], (1, 2): others[1]}, total)
    return (grad_first[None], grad_second[None])

def on_device(*arrays):
    _, columns, _, row_count, width, capacity = sizes(arrays[0])
    aligned = columns == 4 and capacity % 16 == 0 and row_count % 128 == 0 and width % (256 * columns) == 0
    return by_kernels(*arrays) if aligned else by_ops(*arrays)


def solution(mesh):
    return jax.shard_map(
        on_device,
        mesh=mesh,
        in_specs=(
            P("dp", None),
            P("dp", None),
            P("dp", None),
            P("dp", None),
            P("dp", None, "expert"),
            P("dp", "expert", None),
            P("dp", None, "expert"),
            P("dp", "expert", None),
        ),
        out_specs=(P("dp", None, "expert"), P("dp", "expert", None)),
        check_vma=False,
    )
```

```python
import math

import jax
import jax.numpy as jnp
from jax import lax
from jax.experimental import pallas as pl
from jax.experimental.pallas import tpu as pltpu
from jax.sharding import PartitionSpec as P

root_coef = math.sqrt(2.0 / math.pi)
cubic_coef = 0.044715


def partner(value, axis, mask):
    return lax.ppermute(value, axis, [(i, i ^ mask) for i in range(lax.axis_size(axis))])


def gelu_tanh(pre_act):
    inner_arg = root_coef * (pre_act + cubic_coef * pre_act * pre_act * pre_act)
    return 0.5 * pre_act * (1.0 + jnp.tanh(inner_arg))


def gelu_slope(pre_act):
    tangent = jnp.tanh(root_coef * (pre_act + cubic_coef * pre_act * pre_act * pre_act))
    return 0.5 * (1.0 + tangent) + 0.5 * pre_act * (1.0 - tangent * tangent) * root_coef * (
        1.0 + 3.0 * cubic_coef * pre_act * pre_act
    )


def dot(left, right):
    return jnp.dot(left, right, preferred_element_type=jnp.float32)


def ranks(routes, experts):
    onehot = (routes[..., None] == jnp.arange(experts, dtype=jnp.int32)).astype(jnp.int32)
    rank_table = jnp.cumsum(onehot, axis=1) - 1
    return jnp.sum(onehot * rank_table, axis=2)


def sizes(rows):
    groups = lax.axis_size("dp")
    experts = groups // 2
    row_count, width = rows.shape
    capacity = 2 * max(1, 3 * row_count // (4 * experts))
    return groups, lax.axis_size("expert"), experts, row_count, width, capacity


def by_ops(
    teacher_in,
    student_in,
    teacher_route,
    student_route,
    teacher_w1,
    teacher_w2,
    student_w1,
    student_w2,
):
    groups, columns, experts, row_count, width, capacity = sizes(teacher_in)
    plane_rows = groups * capacity
    dp = lax.axis_index("dp")
    column = lax.axis_index("expert")
    plane, core = dp // 2, dp % 2
    loss_scale = 1.0 / math.sqrt(row_count)
    feat = width // columns
    piece = feat // 2

    def dispatch(values, routes):
        position = ranks(routes[:, 0][None], experts)[0]
        slot = (routes[:, 0] ^ plane) * capacity + position
        placing = (
            jnp.arange(experts * capacity, dtype=jnp.int32)[:, None] == slot[None, :]
        ).astype(jnp.bfloat16)
        own_slice = lax.dynamic_slice(values, (0, column * feat), (row_count, feat))
        slots = dot(placing[capacity:], own_slice).astype(jnp.bfloat16)
        stay = dot(placing[:capacity], values).astype(jnp.bfloat16)
        moved = [
            partner(slots[(s - 1) * capacity : s * capacity], "dp", s << 1)
            for s in range(1, experts)
        ]
        mine = jnp.concatenate(moved, axis=0)
        buffer = jnp.concatenate([stay, jnp.zeros((mine.shape[0], width), jnp.bfloat16)], axis=0)
        for m in range(columns):
            got = partner(mine, "expert", m) if m else mine
            buffer = lax.dynamic_update_slice(buffer, got, (capacity, (column ^ m) * feat))
        other = partner(buffer, "dp", 1)
        first = jnp.where(core == 0, buffer, other)
        second = jnp.where(core == 0, other, buffer)
        return jnp.concatenate([first, second], axis=0)

    def forward(flat, w1, w2):
        pre = dot(flat, w1)
        hidden = gelu_tanh(pre).astype(jnp.bfloat16)
        part = dot(hidden, w2).astype(jnp.bfloat16).reshape(plane_rows, 2, columns, piece)
        part = part.transpose(1, 2, 0, 3)
        return pre, hidden, part

    def plane_sum(part):
        keep = lax.dynamic_index_in_dim(part, core, 0, keepdims=False)
        send = lax.dynamic_index_in_dim(part, 1 - core, 0, keepdims=False)
        pair = (
            keep.astype(jnp.float32) + partner(send, "dp", 1).astype(jnp.float32)
        ).astype(jnp.bfloat16)
        total = lax.dynamic_index_in_dim(pair, column, 0, keepdims=False).astype(jnp.float32)
        for m in range(1, columns):
            out = lax.dynamic_index_in_dim(pair, column ^ m, 0, keepdims=False)
            total = total + partner(out, "expert", m).astype(jnp.float32)
        return total

    routes = jnp.concatenate([teacher_route, student_route], axis=1)
    table = lax.all_gather(routes, "dp", axis=0, tiled=True).reshape(groups, row_count, 2)
    teacher_all, student_all = table[:, :, 0], table[:, :, 1]
    block = jnp.arange(groups, dtype=jnp.int32)[:, None]
    block_plane, block_core = block // 2, block % 2
    teacher_row = (
        (teacher_all ^ plane) * plane_rows
        + (block_core * experts + (block_plane ^ teacher_all)) * capacity
        + ranks(teacher_all, experts)
    )
    student_row = jnp.where(student_all == plane, ranks(student_all, experts), -1)
    hits = jnp.arange(capacity, dtype=jnp.int32)[None, :, None] == student_row[:, None, :]
    source = jnp.sum(jnp.where(hits, teacher_row[:, None, :] + 1, 0), axis=2) - 1
    source = source.reshape(experts, 2, capacity)
    source = source[jnp.arange(experts, dtype=jnp.int32) ^ plane].transpose(1, 0, 2)
    source = source.reshape(plane_rows)

    teacher_flat = dispatch(teacher_in, teacher_route)
    student_flat = dispatch(student_in, student_route)
    _, _, teacher_part = forward(teacher_flat, teacher_w1[0], teacher_w2[0])
    teacher_sum = plane_sum(teacher_part).astype(jnp.bfloat16)
    teacher_sums = jnp.concatenate(
        [teacher_sum] + [partner(teacher_sum, "dp", s << 1) for s in range(1, experts)], axis=0
    )
    student_pre, student_hidden, student_part = forward(
        student_flat, student_w1[0], student_w2[0]
    )
    pick = (
        source[:, None] == jnp.arange(experts * plane_rows, dtype=jnp.int32)[None, :]
    ).astype(jnp.bfloat16)
    teacher_rows = dot(pick, teacher_sums)
    student_sum = plane_sum(student_part)
    upstream = ((student_sum - teacher_rows) * loss_scale).astype(jnp.bfloat16)

    half = jnp.zeros((plane_rows, width // 2), jnp.bfloat16)
    for m in range(columns):
        got = partner(upstream, "expert", m) if m else upstream
        half = lax.dynamic_update_slice(half, got, (0, (column ^ m) * piece))
    other_half = partner(half, "dp", 1)
    grad_flat = jnp.concatenate(
        [jnp.where(core == 0, half, other_half), jnp.where(core == 0, other_half, half)], axis=1
    )
    hidden_grad = dot(grad_flat, student_w2[0].T)
    pre_grad = (hidden_grad * gelu_slope(student_pre)).astype(jnp.bfloat16)
    grad_second = dot(student_hidden.T, grad_flat).astype(jnp.bfloat16)
    grad_first = dot(student_flat.T, pre_grad).astype(jnp.bfloat16)
    return (grad_first[None], grad_second[None])


def plane_order(experts, near_first=False):
    return (*range(1, experts), 0) if near_first else (*range(2, experts), 1, 0)


def place():
    dp = lax.axis_index("dp")
    return dp // 2, dp % 2, lax.axis_index("expert")


VMEM = pl.BlockSpec(memory_space=pltpu.VMEM)
ANY = pl.BlockSpec(memory_space=pl.ANY)


def call(kernel, outs, operands, out_specs=None, in_specs=None, scratch=(), grant=20 << 20, flops=0, name=None):
    return pl.pallas_call(
        kernel,
        name=name,
        out_shape=outs,
        in_specs=in_specs or [VMEM] * len(operands),
        out_specs=out_specs or [VMEM] * len(outs),
        scratch_shapes=list(scratch),
        compiler_params=pltpu.CompilerParams(vmem_limit_bytes=grant),
        cost_estimate=pl.CostEstimate(flops=flops, bytes_accessed=0, transcendentals=0),
    )(*operands)


def shape(*dims, dtype=jnp.bfloat16):
    return jax.ShapeDtypeStruct(dims, dtype)


def dot_tn(left, right):
    return lax.dot_general(
        left, right, (((0,), (0,)), ((), ())), preferred_element_type=jnp.float32
    )


def dot_nt(left, right):
    return lax.dot_general(
        left, right, (((1,), (1,)), ((), ())), preferred_element_type=jnp.float32
    )


def placing(route, experts, capacity, plane):
    rows = route.shape[1]
    known = lax.broadcasted_iota(jnp.int32, (16 * (-(-experts // 16)), rows), 0)
    onehot = jnp.where(known == route, 1.0, 0.0)
    upto = lax.broadcasted_iota(jnp.int32, (rows, rows), 0) <= lax.broadcasted_iota(
        jnp.int32, (rows, rows), 1
    )
    counts = dot(onehot.astype(jnp.bfloat16), jnp.where(upto, 1.0, 0.0).astype(jnp.bfloat16))
    position = jnp.sum(onehot * counts, axis=0, keepdims=True).astype(jnp.int32) - 1
    slot = (route ^ plane) * capacity + position
    slots = lax.broadcasted_iota(jnp.int32, (experts * capacity, rows), 0)
    return jnp.where(slots == slot, 1.0, 0.0).astype(jnp.bfloat16)


def pack_kernel(experts, capacity, feat, *refs):
    plane, _, column = place()
    values, routes, refs = refs[:2], refs[2:4], refs[4:]
    moved, refs = refs[: 2 * (experts - 1)], refs[2 * (experts - 1) :]
    slices, blocks, sems = refs[:2], refs[2:4], refs[4]
    cols = pl.ds(pl.multiple_of(column * feat, feat), feat)
    copies = [
        pltpu.make_async_copy(routes[0], blocks[0], sems.at[0]),
        pltpu.make_async_copy(routes[1], blocks[1], sems.at[1]),
        pltpu.make_async_copy(values[0].at[:, cols], slices[0], sems.at[2]),
        pltpu.make_async_copy(values[1].at[:, cols], slices[1], sems.at[3]),
    ]
    for copy in copies:
        copy.start()
    for i in range(2):
        copies[i].wait()
    places = [placing(block[...], experts, capacity, plane) for block in blocks]
    for i in range(2):
        copies[2 + i].wait()
    for i in range(2):
        sent = dot(places[i][capacity:], slices[i][...]).astype(jnp.bfloat16)
        for out, s in zip(moved[i * (experts - 1) :], plane_order(experts, i)[:-1]):
            out[...] = sent[(s - 1) * capacity : s * capacity]


def stay_kernel(experts, capacity, values, route, stay):
    plane, _, _ = place()
    place_rows = placing(route[...], experts, capacity, plane)
    stay[...] = dot(place_rows[:capacity], values[...]).astype(jnp.bfloat16)


def map_kernel(experts, capacity, routes, other_routes, out):
    plane, core, _ = place()
    for c in range(2):
        block = jnp.where(core == c, routes[...], other_routes[...])
        source = placing(block[0:1], experts, capacity, plane)
        target = placing(block[1:2], experts, capacity, plane)
        out[c] = dot_nt(target, source).astype(jnp.bfloat16)


def load_kernel(*refs):
    count = len(refs) // 2
    copies = [
        pltpu.make_async_copy(refs[i], refs[count + i], refs[-1].at[i]) for i in range(count)
    ]
    for copy in copies:
        copy.start()
    for copy in copies:
        copy.wait()


def stack_kernel(near_first, *refs):
    moved, out = refs[:-1], refs[-1]
    capacity = moved[0].shape[0]
    for ref, s in zip(moved, plane_order(len(moved) + 1, near_first)):
        out[(s - 1) * capacity : s * capacity, :] = ref[...]


def join_kernel(columns, stay, *refs):
    _, _, column = place()
    parts, flat = refs[:-1], refs[-1]
    capacity = stay.shape[0]
    feat = parts[0].shape[1]
    flat[:capacity, :] = stay[...]
    for m in range(columns):
        cols = pl.ds(pl.multiple_of((column ^ m) * feat, feat), feat)
        flat[capacity:, cols] = parts[-m if m else 0][...]


def part_pieces(hidden, w2, which, columns, out):
    half = w2.shape[1] // 2
    piece = half // columns
    for j in range(columns):
        cols = pl.ds(pl.multiple_of(which * half + j * piece, piece), piece)
        out[j] = dot(hidden, w2[:, cols]).astype(jnp.bfloat16)


def forward_kernel(columns, count, *refs):
    _, core, _ = place()
    flats, refs = refs[:count], refs[count:]
    w1, w2, send, refs = refs[0], refs[1], refs[2], refs[3:]
    for i in range(count):
        pre = dot(flats[i][...], w1[...])
        if len(refs) > count:
            refs[count + i][...] = pre
        hidden = gelu_tanh(pre).astype(jnp.bfloat16)
        refs[i][...] = hidden
        part_pieces(hidden, w2, 1 - core, columns, send.at[i])


def keep_kernel(columns, hidden_own, hidden_other, w2, *refs):
    _, core, _ = place()
    if len(refs) > 2:
        pre_own, pre_other, flat_own, flat_other, keep_own, keep_other = refs[:6]
        flat_t, hidden_t, slope = refs[6:]
    else:
        keep_own, keep_other = refs
    part_pieces(hidden_own[...], w2, core, columns, keep_own)
    part_pieces(hidden_other[...], w2, core, columns, keep_other)
    if len(refs) > 2:
        half = flat_own.shape[0]
        slope[:half, :] = gelu_slope(pre_own[...])
        slope[half:, :] = gelu_slope(pre_other[...])
        hidden_t[...] = jnp.concatenate([hidden_own[...], hidden_other[...]], axis=0).T
        step = 512
        for j in range(0, flat_own.shape[1], step):
            here = slice(j, j + step)
            both = jnp.concatenate([flat_own[:, here], flat_other[:, here]], axis=0)
            flat_t[here, :] = both.T


def pair_kernel(columns, keep_own, keep_other, *refs):
    _, core, column = place()
    half = keep_own.shape[1]
    got, (mine, *out) = refs[:-columns], refs[-columns:]
    got = [ref for ref in got if ref.dtype != jnp.int32]
    got_own, got_other = got[0].at[0], got[-1].at[len(got) % 2]
    for m in range(columns):
        for which, keep, got in ((core, keep_own, got_other), (1 - core, keep_other, got_own)):
            rows = pl.ds(pl.multiple_of(which * half, 16), half)
            both = keep[column ^ m].astype(jnp.float32) + got[column ^ m].astype(jnp.float32)
            if m:
                out[-m][rows, :] = both.astype(jnp.bfloat16)
            else:
                mine[rows, :] = both


def total_kernel(columns, experts, *refs):
    sums, out = refs[:columns], refs[columns:]
    total = sums[0][...]
    for ref in sums[1:]:
        total = total + ref[...].astype(jnp.float32)
    total = total.astype(jnp.bfloat16)
    capacity = out[0].shape[0] // 2
    for ref, s in zip(out, plane_order(experts)):
        for c in range(2):
            start = (c * experts + s) * capacity
            ref[c * capacity : (c + 1) * capacity, :] = total[start : start + capacity]


def home_kernel(experts, capacity, maps, *refs):
    got, out = refs[:experts], refs[experts:]
    for c in range(2):
        here = slice(c * capacity, (c + 1) * capacity)
        by_plane = dict(zip(plane_order(experts), got))
        rows = jnp.concatenate([by_plane[s][here, :] for s in range(experts)], axis=0)
        by_slot = dot(maps[c], rows).astype(jnp.bfloat16)
        for ref, s in zip(out, plane_order(experts)):
            ref[here, :] = by_slot[s * capacity : (s + 1) * capacity]


def upstream_kernel(columns, experts, loss_scale, *refs):
    sums, teacher, out = refs[:columns], refs[columns:-1], refs[-1]
    total = sums[0][...]
    for ref in sums[1:]:
        total = total + ref[...].astype(jnp.float32)
    capacity = teacher[0].shape[0] // 2
    teacher = dict(zip(plane_order(experts), teacher))
    rows = jnp.concatenate(
        [
            teacher[s][c * capacity : (c + 1) * capacity, :]
            for c in range(2)
            for s in range(experts)
        ],
        axis=0,
    ).astype(jnp.float32)
    out[...] = ((total - rows) * loss_scale).astype(jnp.bfloat16)


def piece_columns(which, width, piece):
    _, core, column = place()
    other, m = which
    start = (1 - core if other else core) * (width // 2) + (column ^ m) * piece
    return pl.ds(pl.multiple_of(start, piece), piece)


def use_piece(ref, cols, hidden_t, w2, hidden_grad):
    _, core, _ = place()
    half = ref.shape[0] // 2
    rows = jnp.concatenate(
        [ref[pl.ds(pl.multiple_of(block * half, 16), half), :] for block in (core, 1 - core)],
        axis=0,
    )
    term = dot_nt(rows, w2[:, cols])
    hidden_grad = term if hidden_grad is None else hidden_grad + term
    return hidden_grad, rows


def early_kernel(places, first, *refs):
    count = len(places)
    pieces, (hidden_t, w2), refs = refs[:count], refs[count : count + 2], refs[count + 2 :]
    hidden_grad = None if first else refs[0][...]
    sum_out, *grads = refs if first else refs[1:]
    piece, width = pieces[0].shape[1], w2.shape[1]
    for ref, which, out in zip(pieces, places, grads):
        cols = piece_columns(which, width, piece)
        hidden_grad, rows = use_piece(ref, cols, hidden_t, w2, hidden_grad)
        out[...] = dot(hidden_t[...], rows).astype(jnp.bfloat16)
    sum_out[...] = hidden_grad


def last_kernel(places, early, *refs):
    count = len(places)
    pieces, refs = refs[:count], refs[count:]
    done, refs = refs[: len(early)], refs[len(early) :]
    hidden_t, w2, sum_in, flat_t, slope, grad_first, grad_second, held_first, held_second, sems = refs
    piece, width = pieces[0].shape[1], w2.shape[1]
    copies = []

    def leave(source, target):
        copies.append(pltpu.make_async_copy(source, target, sems.at[len(copies)]))
        copies[-1].start()

    for ref, which in zip(done, early):
        leave(ref, grad_second.at[:, piece_columns(which, width, piece)])
    hidden_grad = sum_in[...]
    used = []
    for ref, which in zip(pieces, places):
        cols = piece_columns(which, width, piece)
        hidden_grad, rows = use_piece(ref, cols, hidden_t, w2, hidden_grad)
        used.append((cols, rows))
    pre_grad = (hidden_grad * slope[...]).astype(jnp.bfloat16)
    step = 512
    for j in range(width // step):
        here = slice(j * step, (j + 1) * step)
        held_first[here, :] = dot(flat_t[here, :], pre_grad).astype(jnp.bfloat16)
        leave(held_first.at[here, :], grad_first.at[here, :])
    for i, (cols, rows) in enumerate(used):
        held_second[i] = dot(hidden_t[...], rows).astype(jnp.bfloat16)
        leave(held_second.at[i], grad_second.at[:, cols])
    for copy in copies:
        copy.wait()


def by_kernels(
    teacher_in,
    student_in,
    teacher_route,
    student_route,
    teacher_w1,
    teacher_w2,
    student_w1,
    student_w2,
):
    groups, columns, experts, row_count, width, capacity = sizes(teacher_in)
    plane_rows = groups * capacity
    loss_scale = 1.0 / math.sqrt(row_count)
    feat = width // columns
    piece = feat // 2
    hid = teacher_w1.shape[2]
    f32 = jnp.float32

    def after(value, *others):
        return lax.optimization_barrier((value, others))[0]

    def over_planes(sent, near_first=False):
        return [
            partner(value, "dp", s << 1) for value, s in zip(sent, plane_order(experts, near_first))
        ]

    def spread(mine):
        return [mine] + [partner(mine, "expert", m) for m in range(1, columns)]

    def across(value):
        return partner(value, "dp", 1)

    def load(*weights):
        return call(
            load_kernel,
            [shape(*w.shape) for w in weights],
            weights,
            in_specs=[ANY] * len(weights),
            name="load",
            scratch=[pltpu.SemaphoreType.DMA((len(weights),))],
        )

    def forward(flats, w1, w2, keep_pre, name, units=0):
        half, count = plane_rows // 2, len(flats)
        pre = [shape(half, hid, dtype=f32)] * count if keep_pre else []
        return call(
            lambda *refs: forward_kernel(columns, count, *refs),
            [shape(count, columns, half, piece)] + [shape(half, hid)] * count + pre,
            [*flats, w1, w2],
            flops=units * plane_rows * width * hid,
            name=name,
        )

    def keep(own, other, w2, state, outs):
        return call(
            lambda *refs: keep_kernel(columns, *refs),
            [shape(columns, plane_rows // 2, piece)] * 2 + outs,
            [own, other, w2, *state],
            flops=(64 if state else 0) * plane_rows * width * hid,
            name="keep_s" if state else "keep_t",
        )

    def pair(kept, got, marks=()):
        return call(
            lambda *refs: pair_kernel(columns, *refs),
            [shape(plane_rows, piece, dtype=f32)] + [shape(plane_rows, piece)] * (columns - 1),
            [*kept, *marks, *got],
            name="pair",
        )

    def collect(mine, *out):
        return [mine] + [
            partner(value, "expert", columns - 1 - i) for i, value in enumerate(out)
        ]

    route_t = teacher_route.reshape(1, row_count)
    route_s = student_route.reshape(1, row_count)
    def stay(values, route):
        return call(
            lambda *refs: stay_kernel(experts, capacity, *refs),
            [shape(capacity, width)],
            [values, route],
            name="stay",
        )[0]

    sent = call(
        lambda *refs: pack_kernel(experts, capacity, feat, *refs),
        [shape(capacity, feat)] * (2 * (experts - 1)),
        [teacher_in, student_in, route_t, route_s],
        in_specs=[ANY] * 4,
        grant=(253 << 20) // 4,
        name="pack",
        scratch=[pltpu.VMEM((row_count, feat), jnp.bfloat16)] * 2
        + [pltpu.VMEM((1, row_count), jnp.int32)] * 2
        + [pltpu.SemaphoreType.DMA((4,))],
    )
    stay_s = stay(student_in, route_s)
    routes = jnp.concatenate([route_t, route_s], axis=0)
    other_routes = across(routes)
    def stack(moved, near_first, units=0):
        return call(
            lambda *refs: stack_kernel(near_first, *refs),
            [shape((experts - 1) * capacity, feat)],
            moved,
            flops=units * plane_rows * width * hid,
            name="stack",
        )[0]

    sent_t, sent_s = sent[: experts - 1], sent[experts - 1 :]
    moved_t = over_planes(sent_t)
    moved_s = over_planes(sent_s, True)
    mine_t, mine_s = stack(moved_t, False, 0), stack(moved_s, True, 8)
    w1_t, w2_t = load(*after((teacher_w1[0], teacher_w2[0]), mine_s))
    stay_t = stay(after(teacher_in, mine_s), route_t)
    got_t, got_s = spread(mine_t), spread(mine_s)
    got_t, got_s = (got[:1] + got[:0:-1] for got in (got_t, got_s))
    w1_s, w2_s = load(student_w1[0], student_w2[0])
    (maps,) = call(
        lambda *refs: map_kernel(experts, capacity, *refs),
        [shape(2, experts * capacity, experts * capacity)],
        [routes, other_routes],
        name="maps",
    )

    def join(rows, got):
        return call(
            lambda *refs: join_kernel(columns, *refs),
            [shape(plane_rows // 2, width)],
            [rows, *got],
            name="join",
        )[0]

    flat_t_own = join(stay_t, after(got_t, w1_t))
    flat_t_other = across(flat_t_own)

    send, hidden_own = forward([flat_t_own], w1_t, w2_t, False, "forward_t", 24)
    got_own = across(send)
    send, hidden_other = forward([flat_t_other], w1_t, w2_t, False, "forward_t", 0)
    got_other = across(send)
    kept = keep(hidden_own, hidden_other, w2_t, [], [])
    (mark,) = call(
        lambda source, out: out.__setitem__(Ellipsis, source[...]),
        [shape(1, row_count, dtype=jnp.int32)],
        [after(route_t, got_s, w1_s, stay_s, kept[0])],
        flops=8 * plane_rows * width * hid,
        name="mark",
    )
    pieces_t = pair(kept, [got_own, got_other], [mark])
    sums_t = collect(*pieces_t)

    flat_own = join(stay_s, after(got_s, pieces_t[0]))
    flat_other = across(flat_own)
    send, hidden_own, hidden_other, pre_own, pre_other = forward(
        [flat_own, flat_other], w1_s, w2_s, True, "forward_s"
    )
    got = [across(send)]
    *kept, flat_t, hidden_t, slope = keep(
        hidden_own,
        hidden_other,
        w2_s,
        [pre_own, pre_other, flat_own, flat_other],
        [shape(width, plane_rows), shape(hid, plane_rows), shape(plane_rows, hid, dtype=f32)],
    )

    pieces_s = pair(kept, got)
    sums_s = collect(*pieces_s)

    home = call(
        lambda *refs: total_kernel(columns, experts, *refs),
        [shape(2 * capacity, piece)] * experts,
        after(sums_t, pieces_s[0], maps),
    )
    home = [*over_planes(home[:-1]), home[-1]]
    slots = call(
        lambda *refs: home_kernel(experts, capacity, *refs),
        [shape(2 * capacity, piece)] * experts,
        [maps, *home],
        flops=4 * plane_rows * width * hid,
        name="home",
    )
    *sent, near, own = slots
    teachers = [*over_planes([*sent, after(near, sums_s[1])]), own]
    (upstream,) = call(
        lambda *refs: upstream_kernel(columns, experts, loss_scale, *refs),
        [shape(plane_rows, piece)],
        [*sums_s, *teachers],
    )
    early = {}

    def backward(pieces, total):
        first = total is None
        places = tuple(pieces)
        total, *done = call(
            lambda *refs: early_kernel(places, first, *refs),
            [shape(plane_rows, hid, dtype=f32)] + [shape(hid, piece)] * len(places),
            [*pieces.values(), hidden_t, w2_s] + ([] if first else [total]),
            name="early",
        )
        early.update(zip(places, done))
        return total

    def finish(pieces, total):
        places, kept_places = tuple(pieces), tuple(early)
        return call(
            lambda *refs: last_kernel(places, kept_places, *refs),
            [shape(width, hid), shape(hid, width)],
            [*pieces.values(), *early.values(), hidden_t, w2_s, total, flat_t, slope],
            out_specs=[ANY, ANY],
            scratch=[
                pltpu.VMEM((width, hid), jnp.bfloat16),
                pltpu.VMEM((len(places), hid, piece), jnp.bfloat16),
                pltpu.SemaphoreType.DMA((len(places) + len(early) + width // 512,)),
            ],
            name="last",
        )

    grads = spread(upstream)
    total = backward({(0, 0): upstream, (1, 0): across(upstream)}, None)
    far = after(grads[3], total)
    total = backward({(0, 3): far}, total)
    near = after(grads[1:3], total)
    other_far = across(far)
    others = [across(value) for value in near]
    total = backward({(0, 1): near[0], (0, 2): near[1], (1, 3): other_far}, total)
    grad_first, grad_second = finish({(1, 1): others[0], (1, 2): others[1]}, total)
    return (grad_first[None], grad_second[None])

def on_device(*arrays):
    _, columns, _, row_count, width, capacity = sizes(arrays[0])
    aligned = columns == 4 and capacity % 16 == 0 and row_count % 128 == 0 and width % (256 * columns) == 0
    return by_kernels(*arrays) if aligned else by_ops(*arrays)


def solution(mesh):
    return jax.shard_map(
        on_device,
        mesh=mesh,
        in_specs=(
            P("dp", None),
            P("dp", None),
            P("dp", None),
            P("dp", None),
            P("dp", None, "expert"),
            P("dp", "expert", None),
            P("dp", None, "expert"),
            P("dp", "expert", None),
        ),
        out_specs=(P("dp", None, "expert"), P("dp", "expert", None)),
        check_vma=False,
    )
```
